128 devices in a mesh: sector: 32 (over y, z, core), blk: 4 (over x).
Axes of the slice: x: 4, y: 4, z: 4, core: 2. Of those that a mesh axis runs over, the one named last changes fastest.
Arguments:
- visible_feats: bfloat16 [262144, 256], P(('sector', 'blk')), may hold values from -6 to 6
- grid_pos: bfloat16 [256, 32, 40, 256], P('sector', 'blk'), may hold values from -6 to 6
- vis_cells: int32 [262144], P(('sector', 'blk')), may hold values from 0 to 2559, as said below
- vis_count: int32 [128], P(('sector', 'blk')), may hold values from 512 to 2048, as said below
- owner: int32 [262144], P(('sector', 'blk')), may hold values from 0 to 127, as said below
- slot: int32 [262144], P(('sector', 'blk')), may hold values from 0 to 1023, as said below
- window: int32 [128, 1024], P(('sector', 'blk')), may hold values from 0 to 3, never falling along the last dimension, each value on 1 to 512 neighbouring positions
- enc_gain1: float32 [256], replicated, may hold values from 0.1 to 1.9
- attn_in: bfloat16 [256, 768], replicated, may hold values from -2 to 2
- attn_out: bfloat16 [256, 256], replicated, may hold values from -0.375 to 0.375
- enc_gain2: float32 [256], replicated, may hold values from 0.1 to 1.9
- mlp_in: bfloat16 [256, 1024], replicated, may hold values from -0.375 to 0.375
- mlp_out: bfloat16 [1024, 256], replicated, may hold values from -0.1875 to 0.1875
- mask_token: float32 [256], replicated, may hold values from -4 to 4
- dec_gain: float32 [256], replicated, may hold values from 0.1 to 1.9
- conv_weight: bfloat16 [27, 256, 256], replicated, may hold values from -0.078125 to 0.078125
- conv_bias: float32 [256], replicated, may hold values from -3 to 3
Outputs:
- decoded: bfloat16 [256, 32, 40, 256], P('sector', 'blk')
The draws below stay inside these ranges and needn't reach their ends.
Inputs may be any that keep to these rules, and one draw needn't show every extreme that they name: `vis_cells`: the first vis_count entries of a device are distinct cells of its block; later entries are ignored. `vis_count`: counts sum to 131072; 2048 is reached on some device in every draw. On each device the owners of the live entries never fall along the list; each device sends each owner 1 to 18 live entries, and 18 is reached by some pair in every draw. Later entries are ignored. `slot`: the live entries of all devices sent to one owner take each of its 1024 slots exactly once. Later entries are ignored.
All inputs are finite; a program needn't handle non-finite values.
Results may differ from the reference program's by a relative error of at most 0.0062.
Values may be sent and summed in bfloat16 or wider, within the bound.
No kernel may reach another device: no remote copies, remote signals or barrier semaphores. Data moves between devices by JAX's collectives and lax.ppermute only.
A program may use at most 128 MiB of HBM per device.

```python
import math
import jax
import jax.numpy as jnp
import numpy as np
from jax import lax

C = 256
HEAD_DIM = 32
FF_ENC = 1024
AZ_DEV = 8
RAD_DEV = 8
HGT = 40
ENC_DEV = 1024
WIN_MOST = 512
CELLS = 2560
VCAP = 2048
NAZ = 256
NRAD = 32
N_SECTOR = 32
N_BLK = 4
DEVICES = 128


def routing_plan(key):
    pair_mean = ENC_DEV // DEVICES
    jitter = pair_mean // 4
    key_heavy, key_source, key_shift = jax.random.split(key, 3)
    heavy_rank = jax.random.permutation(key_heavy, DEVICES)
    heavy = heavy_rank < DEVICES // 4
    base_rows = jnp.where(heavy, 7 * pair_mean // 4, 3 * pair_mean // 4).astype(jnp.int32)
    first_heavy = jnp.argmax(heavy_rank == 0).astype(jnp.int32)
    source_jitter = jax.random.randint(key_source, (DEVICES,), 0, jitter + 1).astype(jnp.int32)
    source_jitter = source_jitter.at[first_heavy].set(jitter)
    source_jitter = source_jitter.at[(first_heavy + DEVICES - 1) % DEVICES].set(0)
    source_rows = base_rows + source_jitter - jnp.roll(source_jitter, 1)
    shift_jitter = jax.random.randint(key_shift, (DEVICES,), 0, jitter + 1).astype(jnp.int32)
    shift_jitter = shift_jitter.at[0].set(jitter).at[DEVICES - 1].set(0)
    shift_rows = shift_jitter - jnp.roll(shift_jitter, 1)
    offsets = (jnp.arange(DEVICES)[None, :] - jnp.arange(DEVICES)[:, None]) % DEVICES
    return source_rows[:, None] + shift_rows[offsets]


def route_rows(key):
    pair_rows = routing_plan(key)
    row_ends = jnp.cumsum(pair_rows, axis=1)
    row_index = jnp.arange(VCAP, dtype=jnp.int32)
    owners = jax.vmap(lambda ends_row: jnp.searchsorted(ends_row, row_index, side='right'))(row_ends)
    owners = jnp.minimum(owners, DEVICES - 1).astype(jnp.int32)
    row_starts = row_ends - pair_rows
    within = row_index[None, :] - jnp.take_along_axis(row_starts, owners, axis=1)
    before = jnp.cumsum(pair_rows, axis=0) - pair_rows
    raw_slot = jnp.take_along_axis(before, owners, axis=1) + within
    row_live = row_index[None, :] < jnp.sum(pair_rows, axis=1)[:, None]
    raw_slot = jnp.where(row_live, raw_slot, 0).astype(jnp.int32)
    key_perm = jax.random.fold_in(key, 5)
    slot_perms = jax.vmap(lambda owner_id: jax.random.permutation(jax.random.fold_in(key_perm, owner_id), ENC_DEV))(jnp.arange(DEVICES))
    slot_ids = slot_perms[owners, raw_slot].astype(jnp.int32)
    return (owners, slot_ids)


def draw_vis_count(key, part):
    pair_rows = routing_plan(key)
    return jnp.sum(pair_rows, axis=1).astype(jnp.int32)


def draw_owner(key, part):
    owners, slot_ids = route_rows(key)
    return owners.reshape(-1)


def draw_slot(key, part):
    owners, slot_ids = route_rows(key)
    return slot_ids.reshape(-1)


def draw_vis_cells(key, part):
    key = jax.random.fold_in(key, 7)
    picks = jax.vmap(lambda device_id: jax.random.permutation(jax.random.fold_in(key, device_id), CELLS)[:VCAP])(jnp.arange(DEVICES))
    return picks.reshape(-1).astype(jnp.int32)


def draw_attn_in(key, part):
    key = jax.random.fold_in(key, 11)
    key_base = jax.random.fold_in(key, 0)
    base = jax.random.normal(key_base, (C, 3 * C), jnp.float32) * C ** (-0.5)
    return jnp.clip(base, -2.0, 2.0).astype(jnp.bfloat16)


def steps_of(own_key, extent, cuts, least, largest):
    loudness = 1.0
    for dim, blocks in cuts:
        draws = jax.random.uniform(jax.random.fold_in(jax.random.fold_in(own_key, 6), dim), (blocks,), jnp.float32, least / len(cuts), largest / len(cuts))
        loudness = loudness * jnp.repeat(jnp.exp(draws), extent[dim] // blocks).reshape((-1,) + (1,) * (len(extent) - 1 - dim))
    return loudness


def length_profile(amount, total, reach, skew):
    portions = [(1 << 20) // math.isqrt(standing ** skew) + 1 for standing in range(2, amount + 1)]
    surplus, holding = total - reach - (amount - 1), [1] * (amount - 1)
    while surplus > 0:
        free = [i for i in range(amount - 1) if holding[i] < reach]
        whole, left = sum([portions[i] for i in free]), surplus
        for i in free:
            extra = min(reach - holding[i], max(1, left * portions[i] // whole), surplus)
            holding[i] = holding[i] + extra
            surplus = surplus - extra
    return np.array([reach] + holding)


def uneven_parts(own_key, count, total, reach, skew):
    if count == 2:
        one = jax.random.randint(own_key, (), max(1, total - reach), min(reach, total - 1) + 1)
        return jnp.stack([one, total - one])
    sizes = jnp.asarray(length_profile(count, total, reach, skew), jnp.int32)
    twos = (count - 1) // 2
    giver, receiver = sizes[1:1 + 2 * twos:2], sizes[2:2 + 2 * twos:2]
    slack = jnp.minimum(giver - 1, reach - receiver)
    passed = jax.random.randint(jax.random.fold_in(own_key, 1), (twos,), 0, 1 << 20) % (slack + 1)
    sizes = sizes.at[1:1 + 2 * twos:2].set(giver - passed).at[2:2 + 2 * twos:2].set(receiver + passed)
    return sizes[jax.random.permutation(jax.random.fold_in(own_key, 2), count)]


def bell_draw(own_key, shape, deviation, limit, cuts=(), kind=jnp.bfloat16):
    array = deviation * jax.random.normal(own_key, shape, jnp.float32)
    if cuts:
        array = array * steps_of(own_key, shape, cuts, -0.22, 0.18)
    return jnp.clip(array, -limit, limit).astype(kind)


def setup_inputs(seed: int = 0) -> dict:
    streams_of = jax.random.split(jax.random.key(seed), 18)
    return {
        "visible_feats": bell_draw(streams_of[0], (DEVICES * VCAP, C), 1.0, 6.0, ((0, 128),)),
        "grid_pos": bell_draw(streams_of[1], (NAZ, NRAD, HGT, C), 1.0, 6.0, ((0, 32), (1, 4))),
        "vis_cells": draw_vis_cells(jax.random.fold_in(streams_of[17], 71), 0),
        "vis_count": draw_vis_count(jax.random.fold_in(streams_of[17], 71), 0),
        "owner": draw_owner(jax.random.fold_in(streams_of[17], 71), 0),
        "slot": draw_slot(jax.random.fold_in(streams_of[17], 71), 0),
        "window": jax.vmap(lambda own: jnp.searchsorted(jnp.cumsum(uneven_parts(own, 4, ENC_DEV, WIN_MOST, 1)), jnp.arange(ENC_DEV), side="right"))(jax.random.split(streams_of[6], DEVICES)).reshape((DEVICES, ENC_DEV)).astype(jnp.int32),
        "enc_gain1": jnp.clip(1.0 + 0.18 * jax.random.normal(streams_of[7], (C,), jnp.float32), 0.1, 1.9),
        "attn_in": draw_attn_in(jax.random.fold_in(streams_of[17], 71), 0),
        "attn_out": bell_draw(streams_of[9], (C, C), C ** -0.5, 0.375),
        "enc_gain2": jnp.clip(1.0 + 0.18 * jax.random.normal(streams_of[10], (C,), jnp.float32), 0.1, 1.9),
        "mlp_in": bell_draw(streams_of[11], (C, FF_ENC), C ** -0.5, 0.375),
        "mlp_out": bell_draw(streams_of[12], (FF_ENC, C), FF_ENC ** -0.5, 0.1875),
        "mask_token": bell_draw(streams_of[13], (C,), 1.0, 4.0, (), jnp.float32),
        "dec_gain": jnp.clip(1.0 + 0.18 * jax.random.normal(streams_of[14], (C,), jnp.float32), 0.1, 1.9),
        "conv_weight": bell_draw(streams_of[15], (27, C, C), (27 * C) ** -0.5, 0.078125),
        "conv_bias": bell_draw(streams_of[16], (C,), 0.5, 3.0, (), jnp.float32),
    }


EPSILON = 1e-05

def layer_norm(values, gain_vec):
    values = values.astype(jnp.float32)
    center = values - lax.optimization_barrier(jnp.mean(values, axis=-1, keepdims=True))
    spread = lax.optimization_barrier(jnp.mean(center * center, axis=-1, keepdims=True))
    return center * lax.rsqrt(spread + EPSILON) * gain_vec

def encode_block(block_rows, window_ids, enc_gain1, attn_in, attn_out, enc_gain2, mlp_in, mlp_out):
    total_rows, channels = block_rows.shape
    head_count = channels // HEAD_DIM
    normed = layer_norm(block_rows, enc_gain1).astype(jnp.bfloat16)
    projected = jnp.dot(normed, attn_in, preferred_element_type=jnp.float32).astype(jnp.bfloat16)
    projected = lax.optimization_barrier(projected).astype(jnp.float32)
    queries = projected[:, :channels].reshape(total_rows, head_count, HEAD_DIM)
    keys_all = projected[:, channels:2 * channels].reshape(total_rows, head_count, HEAD_DIM)
    values_all = projected[:, 2 * channels:].reshape(total_rows, head_count, HEAD_DIM)
    scores = jnp.einsum('qhd,khd->hqk', queries, keys_all) * HEAD_DIM ** (-0.5)
    same_window = window_ids[:, None] == window_ids[None, :]
    scores = jnp.where(same_window[None], scores, -jnp.inf)
    row_max = lax.optimization_barrier(jnp.max(scores, axis=-1, keepdims=True))
    weights = jnp.exp(scores - row_max)
    weights = (weights / lax.optimization_barrier(jnp.sum(weights, axis=-1, keepdims=True))).astype(jnp.bfloat16)
    weights = lax.optimization_barrier(weights).astype(jnp.float32)
    attended = jnp.einsum('hqk,khd->qhd', weights, values_all).astype(jnp.bfloat16).reshape(total_rows, channels)
    after_attn = block_rows.astype(jnp.float32) + jnp.dot(attended, attn_out, preferred_element_type=jnp.float32)
    normed_two = layer_norm(after_attn, enc_gain2).astype(jnp.bfloat16)
    hidden = jax.nn.gelu(jnp.dot(normed_two, mlp_in, preferred_element_type=jnp.float32)).astype(jnp.bfloat16)
    return (after_attn + jnp.dot(hidden, mlp_out, preferred_element_type=jnp.float32)).astype(jnp.bfloat16)

def reference(visible_feats, grid_pos, vis_cells, vis_count, owner, slot, window, enc_gain1, attn_in, attn_out, enc_gain2, mlp_in, mlp_out, mask_token, dec_gain, conv_weight, conv_bias):
    device_count = N_SECTOR * N_BLK
    cell_total = AZ_DEV * RAD_DEV * HGT
    pos_dev = grid_pos.reshape(N_SECTOR, AZ_DEV, N_BLK, RAD_DEV, HGT, C).transpose(0, 2, 1, 3, 4, 5)
    pos_dev = pos_dev.reshape(device_count, cell_total, C)
    cell_list = vis_cells.reshape(device_count, VCAP)
    row_live = jnp.arange(VCAP, dtype=jnp.int32)[None, :] < vis_count[:, None]
    pos_rows = jax.vmap(lambda table, picks: table[picks])(pos_dev, cell_list)
    enc_input = (visible_feats.reshape(device_count, VCAP, C).astype(jnp.float32) + pos_rows.astype(jnp.float32)).astype(jnp.bfloat16)
    target = jnp.where(row_live, owner.reshape(device_count, VCAP) * ENC_DEV + slot.reshape(device_count, VCAP), device_count * ENC_DEV).astype(jnp.int32)
    owner_rows = jnp.zeros((device_count * ENC_DEV, C), jnp.bfloat16)
    owner_rows = owner_rows.at[target.reshape(-1)].set(enc_input.reshape(-1, C), mode='drop')

    def encode_owner(operand_pair):
        return encode_block(operand_pair[0], operand_pair[1], enc_gain1, attn_in, attn_out, enc_gain2, mlp_in, mlp_out)
    encoded = lax.map(encode_owner, (owner_rows.reshape(device_count, ENC_DEV, C), window))
    encoded_flat = encoded.reshape(device_count * ENC_DEV, C)
    back_rows = encoded_flat[jnp.minimum(target, device_count * ENC_DEV - 1)]
    cell_target = jnp.where(row_live, cell_list, cell_total).astype(jnp.int32)

    def fill_device(cell_pick, rows_back, pos_table):
        filled = jnp.broadcast_to(mask_token.astype(jnp.float32), (cell_total, C))
        filled = filled.at[cell_pick].set(rows_back.astype(jnp.float32), mode='drop')
        return (filled + pos_table.astype(jnp.float32)).astype(jnp.bfloat16)
    dec_dev = jax.vmap(fill_device)(cell_target, back_rows, pos_dev)
    dec_input = dec_dev.reshape(N_SECTOR, N_BLK, AZ_DEV, RAD_DEV, HGT, C).transpose(0, 2, 1, 3, 4, 5)
    dec_input = dec_input.reshape(NAZ, NRAD, HGT, C)
    dec_input = lax.optimization_barrier(dec_input)
    dec_normed = layer_norm(dec_input, dec_gain).astype(jnp.bfloat16)
    padded = jnp.pad(dec_normed, ((1, 1), (0, 0), (0, 0), (0, 0)), mode='wrap')
    padded = jnp.pad(padded, ((0, 0), (1, 1), (1, 1), (0, 0)))
    conv_sum = jnp.broadcast_to(conv_bias.astype(jnp.float32), (NAZ * NRAD * HGT, C))
    for offset_az in range(3):
        for offset_rad in range(3):
            for offset_hgt in range(3):
                tap_index = offset_az * 9 + offset_rad * 3 + offset_hgt
                shifted = padded[offset_az:offset_az + NAZ, offset_rad:offset_rad + NRAD, offset_hgt:offset_hgt + HGT]
                conv_sum = conv_sum + jnp.dot(shifted.reshape(-1, C), conv_weight[tap_index], preferred_element_type=jnp.float32)
    decoded = dec_input.astype(jnp.float32) + jax.nn.gelu(conv_sum).reshape(NAZ, NRAD, HGT, C)
    return decoded.astype(jnp.bfloat16)
```

```python
import functools

import jax
import jax.numpy as jnp
from jax import lax
from jax.experimental import pallas as pl
from jax.experimental.pallas import tpu as pltpu
from jax.sharding import PartitionSpec as P

HEAD_DIM = 32
EPSILON = 1e-05
F32 = jnp.float32
BF16 = jnp.bfloat16
I32 = jnp.int32
CAP = 18
MSG = 40
VMEM_LIMIT = 48 * 2**20


def iota(shape, dim):
    return lax.broadcasted_iota(I32, shape, dim)


def one_hot(mask):
    return jnp.where(mask, 1.0, 0.0).astype(BF16)


def dot(a, b):
    return jnp.dot(a, b, preferred_element_type=F32)


def dot_nt(a, b):
    return lax.dot_general(a, b, (((1,), (1,)), ((), ())), preferred_element_type=F32)


def eye_mask(n):
    return iota((n, n), 0) == iota((n, n), 1)


def layer_norm(values, gain_vec):
    center = values - jnp.mean(values, axis=-1, keepdims=True)
    spread = jnp.mean(center * center, axis=-1, keepdims=True)
    return center * lax.rsqrt(spread + EPSILON) * gain_vec


def gelu(x):
    return 0.5 * x * (1.0 + jnp.tanh(0.7978845608028654 * (x + 0.044715 * (x * x * x))))


def send_kernel(
    count_ref, cells_ref, owner_ref, slot_ref, vis_ref, pos_ref,
    msg_ref, starts_ref,
    left_scr, right_scr, meta_scr, starts_smem, sem,
):
    entries = cells_ref.shape[1]
    owners = msg_ref.shape[0]
    cell_total = pos_ref.shape[0]
    entry = iota((1, entries), 1)
    live = entry < count_ref[0]
    owner = jnp.where(live, owner_ref[...], owners)
    owner_id = iota((owners, entries), 0)
    start_col = jnp.sum(jnp.where(owner < owner_id, 1.0, 0.0), axis=1, keepdims=True)
    start_row = jnp.sum(jnp.where(eye_mask(owners), start_col, 0.0), axis=0, keepdims=True)
    starts_ref[...] = start_row.astype(I32)
    copy = pltpu.make_async_copy(starts_ref, starts_smem, sem)
    copy.start()
    belongs = owner == owner_id
    first = jnp.sum(jnp.where(belongs, start_col, 0.0), axis=0, keepdims=True)
    within = jnp.where(live, entry - first.astype(I32), 64)
    cells = cells_ref[...]
    slots = slot_ref[...]
    parts = jnp.concatenate(
        [cells >> 6, cells & 63, slots >> 5, slots & 31, within, within, within, within], axis=0
    ).astype(F32).astype(BF16)
    eye = one_hot(eye_mask(128))
    lane = iota((128, 128), 1)
    cell_cols = []
    meta_parts = []
    for b in range(entries // 128):
        turned = dot_nt(eye, parts[:, b * 128 : (b + 1) * 128])
        cell_cols.append((turned[:, 0:1] * 64.0 + turned[:, 1:2]).astype(I32))
        place = turned[:, 4:5].astype(I32)
        meta_parts.append(
            jnp.where(
                lane == place,
                turned[:, 2:3] + 1.0,
                jnp.where(lane == place + 32, turned[:, 3:4], 0.0),
            ).astype(BF16)
        )
    meta_scr[...] = dot(one_hot(belongs), jnp.concatenate(meta_parts, axis=0))
    step = 512
    for b in range(entries // step):
        col = jnp.concatenate(cell_cols[b * step // 128 : (b + 1) * step // 128], axis=0)
        pick = one_hot(iota((step, cell_total), 1) == col)
        rows = vis_ref[b * step : (b + 1) * step, :].astype(F32) + dot(pick, pos_ref[...])
        rows = rows.astype(BF16).astype(F32)
        left_scr[b * step : (b + 1) * step, :] = rows[:, 0:128]
        right_scr[b * step : (b + 1) * step, :] = rows[:, 128:256]
    left_scr[entries:, :] = jnp.zeros((left_scr.shape[0] - entries, 128), F32)
    right_scr[entries:, :] = jnp.zeros((right_scr.shape[0] - entries, 128), F32)
    copy.wait()
    sub = iota((8, 128), 0)

    def emit(o, carry):
        start = starts_smem[0, o]
        msg_ref[o, 0:16, :] = left_scr[pl.ds(start, 16), :].astype(BF16)
        msg_ref[o, 16:32, :] = right_scr[pl.ds(start, 16), :].astype(BF16)
        left = left_scr[pl.ds(start + 16, 8), :]
        right = pltpu.roll(right_scr[pl.ds(start + 16, 8), :], 2, 0)
        last = jnp.where(sub < 2, left, jnp.where(sub < 4, right, meta_scr[pl.ds(o, 1), :]))
        msg_ref[o, 32:40, :] = last.astype(BF16)
        return carry

    lax.fori_loop(0, owners, emit, 0, unroll=4)


def send_rows(vis_count, cells, owner, slot, vis, pos, owners):
    entries = vis.shape[0]
    vmem = pl.BlockSpec(memory_space=pltpu.VMEM)
    smem = pl.BlockSpec(memory_space=pltpu.SMEM)
    return pl.pallas_call(
        send_kernel,
        out_shape=(
            jax.ShapeDtypeStruct((owners, MSG, 128), BF16),
            jax.ShapeDtypeStruct((1, owners), I32),
        ),
        in_specs=[smem, vmem, vmem, vmem, vmem, vmem],
        out_specs=(vmem, vmem),
        scratch_shapes=[
            pltpu.VMEM((entries + 24, 128), F32),
            pltpu.VMEM((entries + 24, 128), F32),
            pltpu.VMEM((owners, 128), F32),
            pltpu.SMEM((1, owners), I32),
            pltpu.SemaphoreType.DMA,
        ],
        compiler_params=pltpu.CompilerParams(vmem_limit_bytes=VMEM_LIMIT),
        name="send_rows",
    )(vis_count, cells, owner, slot, vis, pos)


def owner_kernel(
    span_ref, msg_ref, window_ref, gain1_ref, attn_in_ref, attn_out_ref, gain2_ref,
    mlp_in_ref, mlp_out_ref,
    back_ref,
    tail_scr, q_scr, k_scr, v_scr, att_scr,
):
    owners = msg_ref.shape[0]
    rows = window_ref.shape[1]
    channels = attn_out_ref.shape[0]
    head_count = channels // HEAD_DIM
    full = 16 * owners
    tail_scr[...] = msg_ref[:, 32:40, :].astype(F32).reshape(owners * 8, 128)

    def tail(j):
        return tail_scr[pl.ds(j, owners, stride=8), :]

    meta = tail(4).astype(BF16)
    place = iota((128, full), 0)
    inner = iota((128, full), 1) & 15
    spread = (
        jnp.where(place == inner, 32.0, 0.0) + jnp.where(place == inner + 32, 1.0, 0.0)
    ).astype(BF16)
    wide = dot(meta, spread)
    of_sender = (iota((owners, full), 1) >> 4) == iota((owners, full), 0)
    slot_full = jnp.sum(jnp.where(of_sender, wide, 0.0), axis=0, keepdims=True) - 32.0
    eye = eye_mask(owners)
    meta32 = meta.astype(F32)
    tail_cols = [meta32[:, j : j + 1] * 32.0 + meta32[:, j + 32 : j + 33] - 32.0 for j in (16, 17)]
    tail_slots = [jnp.sum(jnp.where(eye, c, 0.0), axis=0, keepdims=True) for c in tail_cols]
    slot_row = jnp.concatenate([slot_full] + tail_slots, axis=1).astype(I32)
    left = msg_ref[:, 0:16, :].reshape(full, 128)
    right = msg_ref[:, 16:32, :].reshape(full, 128)
    main = jnp.concatenate([left, right], axis=1)
    rest = jnp.concatenate(
        [
            jnp.concatenate([tail(0), tail(2)], axis=1),
            jnp.concatenate([tail(1), tail(3)], axis=1),
        ],
        axis=0,
    ).astype(BF16)
    step = 256
    for b in range(rows // step):
        sel = one_hot(slot_row == iota((step, slot_row.shape[1]), 0) + b * step)
        x = dot(sel[:, :full], main) + dot(sel[:, full:], rest)
        att_scr[b * step : (b + 1) * step, :] = x
        normed = layer_norm(x, gain1_ref[...]).astype(BF16)
        projected = dot(normed, attn_in_ref[...]).astype(BF16)
        q_scr[b * step : (b + 1) * step, :] = projected[:, :channels]
        k_scr[b * step : (b + 1) * step, :] = projected[:, channels : 2 * channels]
        v_scr[b * step : (b + 1) * step, :] = projected[:, 2 * channels :]
    q_step = 128
    win_row = window_ref[...].astype(F32)
    head_of_lane = iota((q_step, channels), 1) // HEAD_DIM
    eye_q = eye_mask(q_step)

    def attend(qi, key_count, key_start):
        q_rows = pl.ds(pl.multiple_of(qi * q_step, q_step), q_step)
        k_rows = pl.ds(key_start, key_count)
        q = q_scr[q_rows, :]
        keys = k_scr[k_rows, :]
        vals = v_scr[k_rows, :]
        q_win = window_ref[:, q_rows].astype(F32)
        q_win = jnp.sum(jnp.where(eye_q, q_win, 0.0), axis=1, keepdims=True)
        k_win = window_ref[:, k_rows].astype(F32)
        bias = jnp.where(q_win == k_win, 0.0, -jnp.inf)
        total = jnp.zeros((q_step, channels), F32)
        for h in range(head_count):
            q_h = jnp.where(head_of_lane == h, q.astype(F32), 0.0).astype(BF16)
            s = dot_nt(q_h, keys) * HEAD_DIM ** (-0.5) + bias
            e = jnp.exp(s - jnp.max(s, axis=1, keepdims=True))
            norm = 1.0 / jnp.sum(e, axis=1, keepdims=True)
            o = dot(e.astype(BF16), vals) * norm
            total = jnp.where(head_of_lane == h, o, total)
        x = att_scr[q_rows, :] + dot(total.astype(BF16), attn_out_ref[...])
        att_scr[q_rows, :] = x

    def q_block(qi, carry):
        low = span_ref[0, qi]
        count = span_ref[1, qi]
        for n in range(1, rows // 256 + 1):

            @pl.when(count == n)
            def _():
                attend(qi, 256 * n, pl.multiple_of(low, 128))

        return carry

    lax.fori_loop(0, rows // q_step, q_block, 0)
    step = 256
    for b in range(rows // step):
        part = slice(b * step, (b + 1) * step)
        x = att_scr[part, :]
        normed = layer_norm(x, gain2_ref[...]).astype(BF16)
        hidden = gelu(dot(normed, mlp_in_ref[...])).astype(BF16)
        q_scr[part, :] = (x + dot(hidden, mlp_out_ref[...])).astype(BF16)
    slot_f = slot_row.astype(F32)
    eye128 = eye_mask(128)
    step = 512
    for b in range(full // step + 1):
        size = step if b < full // step else 2 * owners
        cols = []
        for i in range(size // 128):
            at = b * step + i * 128
            cols.append(
                jnp.sum(jnp.where(eye128, slot_f[:, at : at + 128], 0.0), axis=1, keepdims=True)
            )
        col = jnp.concatenate(cols, axis=0).astype(I32)
        pick = one_hot(iota((size, rows), 1) == col)
        out = dot(pick, q_scr[...])
        if b < full // step:
            o = b * step // 16
            n = step // 16
            out = out.astype(BF16)
            back_ref[o : o + n, 0:16, :] = out[:, 0:128].reshape(n, 16, 128)
            back_ref[o : o + n, 16:32, :] = out[:, 128:256].reshape(n, 16, 128)
        else:
            for j in range(2):
                tail_scr[pl.ds(j, owners, stride=8), :] = out[j * owners : (j + 1) * owners, 0:128]
                tail_scr[pl.ds(j + 2, owners, stride=8), :] = out[
                    j * owners : (j + 1) * owners, 128:256
                ]
            back_ref[:, 32:40, :] = tail_scr[...].astype(BF16).reshape(owners, 8, 128)


def owner_encode(span, msg, window, gain1, attn_in, attn_out, gain2, mlp_in, mlp_out):
    owners = msg.shape[0]
    rows = window.shape[1]
    channels = attn_out.shape[0]
    vmem = pl.BlockSpec(memory_space=pltpu.VMEM)
    smem = pl.BlockSpec(memory_space=pltpu.SMEM)
    return pl.pallas_call(
        owner_kernel,
        out_shape=jax.ShapeDtypeStruct((owners, MSG, 128), BF16),
        in_specs=[smem] + [vmem] * 8,
        out_specs=vmem,
        scratch_shapes=[
            pltpu.VMEM((owners * 8, 128), F32),
            pltpu.VMEM((rows, channels), BF16),
            pltpu.VMEM((rows, channels), BF16),
            pltpu.VMEM((rows, channels), BF16),
            pltpu.VMEM((rows, channels), F32),
        ],
        compiler_params=pltpu.CompilerParams(vmem_limit_bytes=VMEM_LIMIT),
        name="owner_encode",
    )(span, msg, window, gain1, attn_in, attn_out, gain2, mlp_in, mlp_out)


def place_kernel(
    count_ref, starts_ref, back_ref, cells_ref, pos_ref, token_ref, gain_ref,
    dec_ref, normed_ref,
    left_scr, right_scr,
):
    owners = back_ref.shape[0]
    entries = cells_ref.shape[1]
    cell_total = pos_ref.shape[0]
    count = count_ref[0]
    left_scr[...] = jnp.zeros(left_scr.shape, F32)
    right_scr[...] = jnp.zeros(right_scr.shape, F32)

    def take(o, carry):
        start = starts_ref[0, o]
        block = back_ref[o].astype(F32)
        left_scr[pl.ds(start, 16), :] = block[0:16]
        right_scr[pl.ds(start, 16), :] = block[16:32]
        left_scr[pl.ds(start + 16, 2), :] = block[32:34]
        right_scr[pl.ds(start + 16, 2), :] = block[34:36]
        return carry

    lax.fori_loop(0, owners, take, 0, unroll=4)
    rows = jnp.concatenate([left_scr[0:entries, :], right_scr[0:entries, :]], axis=1).astype(BF16)
    cells = jnp.where(iota((1, entries), 1) < count, cells_ref[...], -1)
    step = 512
    for b in range(cell_total // step):
        part = slice(b * step, (b + 1) * step)
        hit = jnp.where(cells == iota((step, entries), 0) + b * step, 1.0, 0.0)
        filled = dot(hit.astype(BF16), rows)
        seen = jnp.sum(hit, axis=1, keepdims=True)
        filled = jnp.where(seen > 0.5, filled, token_ref[...])
        dec = (filled + pos_ref[part, :].astype(F32)).astype(BF16)
        dec_ref[part, :] = dec
        normed_ref[part, :] = layer_norm(dec.astype(F32), gain_ref[...]).astype(BF16)


def place_rows(vis_count, starts, back, cells, pos, token, gain):
    vmem = pl.BlockSpec(memory_space=pltpu.VMEM)
    smem = pl.BlockSpec(memory_space=pltpu.SMEM)
    return pl.pallas_call(
        place_kernel,
        out_shape=(
            jax.ShapeDtypeStruct(pos.shape, BF16),
            jax.ShapeDtypeStruct(pos.shape, BF16),
        ),
        in_specs=[smem, smem] + [vmem] * 5,
        out_specs=(vmem, vmem),
        scratch_shapes=[pltpu.VMEM((cells.shape[1] + 24, 128), F32)] * 2,
        compiler_params=pltpu.CompilerParams(vmem_limit_bytes=VMEM_LIMIT),
        name="place_rows",
    )(vis_count, starts, back, cells, pos, token, gain)


def conv_kernel(
    dims, normed_ref, dec_ref, az_low_ref, az_high_ref, rad_low_ref, rad_high_ref, corner_ref,
    weight_ref, bias_ref,
    out_ref,
    wide_scr,
):
    az, rad, height = dims
    channels = bias_ref.shape[1]
    plane = rad * height
    pitch = (rad + 2) * height

    def put(at, rows):
        n = rows.shape[0]
        h = iota((n, 1), 0) % height
        values = rows.astype(F32)
        wide_scr[at : at + n, channels : 2 * channels] = rows
        below = jnp.where(h == 0, 0.0, pltpu.roll(values, 1, 0))
        wide_scr[at : at + n, 0:channels] = below.astype(BF16)
        above = jnp.where(h == height - 1, 0.0, pltpu.roll(values, n - 1, 0))
        wide_scr[at : at + n, 2 * channels :] = above.astype(BF16)

    for a in range(az + 2):
        base = a * pitch
        if a == 0:
            row, lo, hi = az_low_ref[...], corner_ref[0], corner_ref[1]
        elif a == az + 1:
            row, lo, hi = az_high_ref[...], corner_ref[2], corner_ref[3]
        else:
            i = a - 1
            row = normed_ref[i * plane : (i + 1) * plane, :]
            lo = rad_low_ref[i * height : (i + 1) * height, :]
            hi = rad_high_ref[i * height : (i + 1) * height, :]
        put(base, lo)
        put(base + height, row)
        put(base + height + plane, hi)
    for a in range(az):
        total = jnp.broadcast_to(bias_ref[...], (plane, channels))
        for da in range(3):
            for dr in range(3):
                at = (a + da) * pitch + dr * height
                total = total + dot(wide_scr[at : at + plane, :], weight_ref[da * 3 + dr])
        part = slice(a * plane, (a + 1) * plane)
        out_ref[part, :] = (dec_ref[part, :].astype(F32) + gelu(total)).astype(BF16)


def conv_block(dims, normed, dec, az_low, az_high, rad_low, rad_high, corners, weight, bias):
    az, rad, height = dims
    channels = normed.shape[1]
    vmem = pl.BlockSpec(memory_space=pltpu.VMEM)
    return pl.pallas_call(
        functools.partial(conv_kernel, dims),
        out_shape=jax.ShapeDtypeStruct(normed.shape, BF16),
        in_specs=[vmem] * 9,
        out_specs=vmem,
        scratch_shapes=[pltpu.VMEM(((az + 2) * (rad + 2) * height, 3 * channels), BF16)],
        compiler_params=pltpu.CompilerParams(vmem_limit_bytes=VMEM_LIMIT),
        name="conv_block",
    )(normed, dec, az_low, az_high, rad_low, rad_high, corners, weight, bias)


def key_spans(window_ids, q_step):
    rows = window_ids.shape[0]
    blocks = window_ids.reshape(rows // q_step, q_step)
    low = jnp.sum(window_ids[None, :] < blocks[:, 0:1], axis=1, dtype=I32)
    high = jnp.sum(window_ids[None, :] <= blocks[:, q_step - 1 :], axis=1, dtype=I32)
    low = low // 128 * 128
    count = (high - low + 255) // 256
    low = jnp.minimum(low, rows - 256 * count)
    return jnp.stack([low, count])


def exchange(values):
    return lax.all_to_all(values, ("sector", "blk"), split_axis=0, concat_axis=0, tiled=True)


def body(
    visible_feats, grid_pos, vis_cells, vis_count, owner, slot, window, enc_gain1, attn_in,
    attn_out, enc_gain2, mlp_in, mlp_out, mask_token, dec_gain, conv_weight, conv_bias,
):
    n_sector = lax.axis_size("sector")
    n_blk = lax.axis_size("blk")
    owners = n_sector * n_blk
    az, rad, height, channels = grid_pos.shape
    cell_total = az * rad * height
    pos = grid_pos.reshape(cell_total, channels)
    cells = vis_cells.reshape(1, -1)
    message, starts = send_rows(
        vis_count, cells, owner.reshape(1, -1), slot.reshape(1, -1), visible_feats, pos, owners
    )
    message = exchange(message)
    back = owner_encode(
        key_spans(window[0], 128), message, window, enc_gain1.reshape(1, -1), attn_in, attn_out,
        enc_gain2.reshape(1, -1), mlp_in, mlp_out,
    )
    back = exchange(back)
    dec, normed = place_rows(
        vis_count, starts, back, cells, pos, mask_token.reshape(1, -1), dec_gain.reshape(1, -1)
    )
    cube = normed.reshape(az, rad, height, channels)
    up = [(i, (i + 1) % n_sector) for i in range(n_sector)]
    down = [(t, s) for s, t in up]
    outward = [(i, i + 1) for i in range(n_blk - 1)]
    inward = [(t, s) for s, t in outward]

    def both(first, second):
        return [(s * n_blk + r, s2 * n_blk + r2) for s, s2 in first for r, r2 in second]

    def flat(values):
        return values.reshape(-1, channels)

    az_low = lax.ppermute(flat(cube[az - 1]), "sector", up)
    az_high = lax.ppermute(flat(cube[0]), "sector", down)
    rad_low = lax.ppermute(flat(cube[:, rad - 1]), "blk", outward)
    rad_high = lax.ppermute(flat(cube[:, 0]), "blk", inward)
    every = ("sector", "blk")
    corners = jnp.stack(
        [
            lax.ppermute(cube[az - 1, rad - 1], every, both(up, outward)),
            lax.ppermute(cube[az - 1, 0], every, both(up, inward)),
            lax.ppermute(cube[0, rad - 1], every, both(down, outward)),
            lax.ppermute(cube[0, 0], every, both(down, inward)),
        ]
    )
    decoded = conv_block(
        (az, rad, height), normed, dec, az_low, az_high, rad_low, rad_high, corners,
        conv_weight.reshape(9, 3 * channels, channels), conv_bias.reshape(1, -1),
    )
    return decoded.reshape(az, rad, height, channels)


def solution(mesh):
    lists = P(("sector", "blk"))
    return jax.shard_map(
        body,
        mesh=mesh,
        in_specs=(
            P(("sector", "blk"), None),
            P("sector", "blk", None, None),
            lists,
            lists,
            lists,
            lists,
            P(("sector", "blk"), None),
        )
        + (P(),) * 10,
        out_specs=P("sector", "blk", None, None),
        check_vma=False,
    )
```

```python
import jax
import jax.numpy as jnp
from jax import lax
from jax.experimental import pallas as pl
from jax.experimental.pallas import tpu as pltpu
from jax.sharding import PartitionSpec as P

HEAD_DIM = 32
EPSILON = 1e-05
F32 = jnp.float32
BF16 = jnp.bfloat16
I32 = jnp.int32
CAP = 18
MSG = 40
VMEM_LIMIT = 48 * 2**20


def iota(shape, dim):
    return lax.broadcasted_iota(I32, shape, dim)


def one_hot(mask):
    return jnp.where(mask, 1.0, 0.0).astype(BF16)


def dot(a, b):
    return jnp.dot(a, b, preferred_element_type=F32)


def dot_nt(a, b):
    return lax.dot_general(a, b, (((1,), (1,)), ((), ())), preferred_element_type=F32)


def eye_mask(n):
    return iota((n, n), 0) == iota((n, n), 1)


def layer_norm(values, gain_vec):
    center = values - jnp.mean(values, axis=-1, keepdims=True)
    spread = jnp.mean(center * center, axis=-1, keepdims=True)
    return center * lax.rsqrt(spread + EPSILON) * gain_vec


def gelu(x):
    return 0.5 * x * (1.0 + jnp.tanh(0.7978845608028654 * (x + 0.044715 * (x * x * x))))


def send_kernel(
    count_ref, cells_ref, owner_ref, slot_ref, vis_ref, pos_ref,
    msg_ref, starts_ref,
    left_scr, right_scr, meta_scr, starts_smem, sem,
    cells_in, owner_in, slot_in, vis_in, pos_in, in_sems,
):
    entries = cells_ref.shape[1]
    owners = msg_ref.shape[0]
    cell_total = pos_ref.shape[0]
    loads = [
        pltpu.make_async_copy(src, dst, in_sems.at[i])
        for i, (src, dst) in enumerate(
            [
                (owner_ref, owner_in),
                (cells_ref, cells_in),
                (slot_ref, slot_in),
                (pos_ref, pos_in),
                (vis_ref, vis_in),
            ]
        )
    ]
    for load in loads:
        load.start()
    for load in loads[:3]:
        load.wait()
    entry = iota((1, entries), 1)
    live = entry < count_ref[0]
    owner = jnp.where(live, owner_in[...], owners)
    owner_id = iota((owners, entries), 0)
    start_col = jnp.sum(jnp.where(owner < owner_id, 1.0, 0.0), axis=1, keepdims=True)
    start_row = jnp.sum(jnp.where(eye_mask(owners), start_col, 0.0), axis=0, keepdims=True)
    starts_ref[...] = start_row.astype(I32)
    copy = pltpu.make_async_copy(starts_ref, starts_smem, sem)
    copy.start()
    belongs = owner == owner_id
    first = jnp.sum(jnp.where(belongs, start_col, 0.0), axis=0, keepdims=True)
    within = jnp.where(live, entry - first.astype(I32), 64)
    cells = cells_in[...]
    slots = slot_in[...]
    parts = jnp.concatenate(
        [cells >> 6, cells & 63, slots >> 5, slots & 31, within, within, within, within], axis=0
    ).astype(F32).astype(BF16)
    eye = one_hot(eye_mask(128))
    lane = iota((128, 128), 1)
    cell_cols = []
    meta_parts = []
    for b in range(entries // 128):
        turned = dot_nt(eye, parts[:, b * 128 : (b + 1) * 128])
        cell_cols.append((turned[:, 0:1] * 64.0 + turned[:, 1:2]).astype(I32))
        place = turned[:, 4:5].astype(I32)
        meta_parts.append(
            jnp.where(
                lane == place,
                turned[:, 2:3] + 1.0,
                jnp.where(lane == place + 32, turned[:, 3:4], 0.0),
            ).astype(BF16)
        )
    meta_scr[...] = dot(one_hot(belongs), jnp.concatenate(meta_parts, axis=0))
    for load in loads[3:]:
        load.wait()
    step = 512
    for b in range(entries // step):
        col = jnp.concatenate(cell_cols[b * step // 128 : (b + 1) * step // 128], axis=0)
        pick = one_hot(iota((step, cell_total), 1) == col)
        rows = vis_in[b * step : (b + 1) * step, :].astype(F32) + dot(pick, pos_in[...])
        rows = rows.astype(BF16).astype(F32)
        left_scr[b * step : (b + 1) * step, :] = rows[:, 0:128]
        right_scr[b * step : (b + 1) * step, :] = rows[:, 128:256]
    left_scr[entries:, :] = jnp.zeros((left_scr.shape[0] - entries, 128), F32)
    right_scr[entries:, :] = jnp.zeros((right_scr.shape[0] - entries, 128), F32)
    copy.wait()
    sub = iota((8, 128), 0)

    def emit(o, carry):
        start = starts_smem[0, o]
        msg_ref[o, 0:16, :] = left_scr[pl.ds(start, 16), :].astype(BF16)
        msg_ref[o, 16:32, :] = right_scr[pl.ds(start, 16), :].astype(BF16)
        left = left_scr[pl.ds(start + 16, 8), :]
        right = pltpu.roll(right_scr[pl.ds(start + 16, 8), :], 2, 0)
        last = jnp.where(sub < 2, left, jnp.where(sub < 4, right, meta_scr[pl.ds(o, 1), :]))
        msg_ref[o, 32:40, :] = last.astype(BF16)
        return carry

    lax.fori_loop(0, owners, emit, 0, unroll=4)


def send_rows(vis_count, cells, owner, slot, vis, pos, owners):
    entries = vis.shape[0]
    vmem = pl.BlockSpec(memory_space=pltpu.VMEM)
    smem = pl.BlockSpec(memory_space=pltpu.SMEM)
    return pl.pallas_call(
        send_kernel,
        out_shape=(
            jax.ShapeDtypeStruct((owners, MSG, 128), BF16),
            jax.ShapeDtypeStruct((1, owners), I32),
        ),
        in_specs=[smem] + [pl.BlockSpec(memory_space=pltpu.HBM)] * 5,
        out_specs=(vmem, vmem),
        scratch_shapes=[
            pltpu.VMEM((entries + 24, 128), F32),
            pltpu.VMEM((entries + 24, 128), F32),
            pltpu.VMEM((owners, 128), F32),
            pltpu.SMEM((1, owners), I32),
            pltpu.SemaphoreType.DMA,
            pltpu.VMEM(cells.shape, I32),
            pltpu.VMEM(cells.shape, I32),
            pltpu.VMEM(cells.shape, I32),
            pltpu.VMEM(vis.shape, BF16),
            pltpu.VMEM(pos.shape, BF16),
            pltpu.SemaphoreType.DMA((5,)),
        ],
        compiler_params=pltpu.CompilerParams(vmem_limit_bytes=VMEM_LIMIT),
        name="send_rows",
    )(vis_count, cells, owner, slot, vis, pos)


def owner_kernel(
    span_ref, msg_ref, window_ref, gain1_ref, attn_in_ref, attn_out_ref, gain2_ref,
    mlp_in_ref, mlp_out_ref,
    back_ref,
    tail_scr, q_scr, k_scr, v_scr, win_scr, att_scr, x_scr,
):
    owners = msg_ref.shape[0]
    rows = window_ref.shape[1]
    channels = attn_out_ref.shape[0]
    head_count = channels // HEAD_DIM
    full = 16 * owners
    tail_scr[...] = msg_ref[:, 32:40, :].astype(F32).reshape(owners * 8, 128)

    def tail(j):
        return tail_scr[pl.ds(j, owners, stride=8), :]

    meta = tail(4).astype(BF16)
    place = iota((128, full), 0)
    inner = iota((128, full), 1) & 15
    spread = (
        jnp.where(place == inner, 32.0, 0.0) + jnp.where(place == inner + 32, 1.0, 0.0)
    ).astype(BF16)
    wide = dot(meta, spread)
    of_sender = (iota((owners, full), 1) >> 4) == iota((owners, full), 0)
    slot_full = jnp.sum(jnp.where(of_sender, wide, 0.0), axis=0, keepdims=True) - 32.0
    eye = eye_mask(owners)
    meta32 = meta.astype(F32)
    tail_cols = [meta32[:, j : j + 1] * 32.0 + meta32[:, j + 32 : j + 33] - 32.0 for j in (16, 17)]
    tail_slots = [jnp.sum(jnp.where(eye, c, 0.0), axis=0, keepdims=True) for c in tail_cols]
    slot_row = jnp.concatenate([slot_full] + tail_slots, axis=1).astype(I32)
    left = msg_ref[:, 0:16, :].reshape(full, 128)
    right = msg_ref[:, 16:32, :].reshape(full, 128)
    main = jnp.concatenate([left, right], axis=1)
    rest = jnp.concatenate(
        [
            jnp.concatenate([tail(0), tail(2)], axis=1),
            jnp.concatenate([tail(1), tail(3)], axis=1),
        ],
        axis=0,
    ).astype(BF16)
    step = 256
    for b in range(rows // step):
        part = slice(b * step, (b + 1) * step)
        sel = one_hot(slot_row == iota((step, slot_row.shape[1]), 0) + b * step)
        x = dot(sel[:, :full], main) + dot(sel[:, full:], rest)
        x_scr[part, :] = x
        normed = layer_norm(x, gain1_ref[...]).astype(BF16)
        projected = dot(normed, attn_in_ref[...]).astype(BF16)
        q_scr[part, :] = projected[:, :channels]
        k_scr[part, :] = projected[:, channels : 2 * channels]
        ones = jnp.ones((step, 128), BF16)
        v_scr[part, 0:128] = projected[:, 2 * channels : 2 * channels + 128]
        v_scr[part, 128:256] = ones
        v_scr[part, 256:384] = projected[:, 2 * channels + 128 :]
        v_scr[part, 384:512] = ones
    q_step = 128
    eye_q = eye_mask(q_step)
    for i in range(rows // 128):
        part = slice(i * 128, (i + 1) * 128)
        ids = window_ref[:, part].astype(F32)
        ids = jnp.sum(jnp.where(eye_q, ids, 0.0), axis=1, keepdims=True)
        win_scr[part, :] = jnp.broadcast_to(ids, (128, 128)).astype(I32)
    head_of_lane = iota((1, channels), 1) // HEAD_DIM
    lane_head = (iota((1, channels), 1) & 127) // HEAD_DIM
    head_mask = [one_hot(head_of_lane == h) for h in range(head_count)]
    scale = HEAD_DIM ** (-0.5) * 1.4426950408889634
    stack = 4
    half_heads = head_count // 2

    def attend(qi, key_count, key_start):
        q_rows = pl.ds(pl.multiple_of(qi * q_step, q_step), q_step)
        k_rows = pl.ds(key_start, key_count)
        q = q_scr[q_rows, :]
        keys = k_scr[k_rows, :]
        q_win = win_scr[q_rows, :]
        q_win = jnp.concatenate([q_win] * (key_count // 128), axis=1)
        bias = jnp.where(q_win == window_ref[:, k_rows], 0.0, -jnp.inf)
        bias = jnp.concatenate([bias] * stack, axis=0)
        groups = []
        for half in range(2):
            for g in range(half_heads // 4):
                groups.append((half, range(g * 4, (g + 1) * 4)))

        def scores(half, heads):
            queries = jnp.concatenate([q * head_mask[half * half_heads + h] for h in heads], axis=0)
            return dot_nt(queries, keys) + bias

        def weigh(s):
            top = jnp.max(s, axis=1, keepdims=True)
            return jnp.exp2(((s - top) * scale).astype(BF16))

        totals = [None, None]

        def mix(half, heads, e):
            o = dot(e, v_scr[k_rows, 256 * half : 256 * half + 256])
            total = totals[half]
            for i, h in enumerate(heads):
                block = o[i * q_step : (i + 1) * q_step]
                total = block if total is None else jnp.where(lane_head == h, block, total)
            totals[half] = total

        ahead = scores(*groups[0])
        held = None
        for i in range(len(groups)):
            s = ahead
            if i + 1 < len(groups):
                ahead = scores(*groups[i + 1])
            e = weigh(s)
            if held is not None:
                mix(*held)
            held = (*groups[i], e)
        mix(*held)

        for half in range(2):
            total = totals[half]
            att_scr[q_rows, 128 * half : 128 * half + 128] = (
                total[:, 0:128] * (1.0 / total[:, 128:256])
            ).astype(BF16)

    def q_block(qi, carry):
        low = span_ref[0, qi]
        count = span_ref[1, qi]
        for n in range(1, rows // 256 + 1):

            @pl.when(count == n)
            def _():
                attend(qi, 256 * n, pl.multiple_of(low, 128))

        return carry

    lax.fori_loop(0, rows // q_step, q_block, 0)
    step = 256
    for b in range(rows // step):
        part = slice(b * step, (b + 1) * step)
        x = x_scr[part, :] + dot(att_scr[part, :], attn_out_ref[...])
        normed = layer_norm(x, gain2_ref[...]).astype(BF16)
        hidden = gelu(dot(normed, mlp_in_ref[...])).astype(BF16)
        q_scr[part, :] = (x + dot(hidden, mlp_out_ref[...])).astype(BF16)
    slot_f = slot_row.astype(F32)
    eye128 = eye_mask(128)
    step = 512
    for b in range(full // step + 1):
        size = step if b < full // step else 2 * owners
        cols = []
        for i in range(size // 128):
            at = b * step + i * 128
            cols.append(
                jnp.sum(jnp.where(eye128, slot_f[:, at : at + 128], 0.0), axis=1, keepdims=True)
            )
        col = jnp.concatenate(cols, axis=0).astype(I32)
        pick = one_hot(iota((size, rows), 1) == col)
        out = dot(pick, q_scr[...])
        if b < full // step:
            o = b * step // 16
            n = step // 16
            out = out.astype(BF16)
            back_ref[o : o + n, 0:16, :] = out[:, 0:128].reshape(n, 16, 128)
            back_ref[o : o + n, 16:32, :] = out[:, 128:256].reshape(n, 16, 128)
        else:
            for j in range(2):
                tail_scr[pl.ds(j, owners, stride=8), :] = out[j * owners : (j + 1) * owners, 0:128]
                tail_scr[pl.ds(j + 2, owners, stride=8), :] = out[
                    j * owners : (j + 1) * owners, 128:256
                ]
            back_ref[:, 32:40, :] = tail_scr[...].astype(BF16).reshape(owners, 8, 128)


def owner_encode(span, msg, window, gain1, attn_in, attn_out, gain2, mlp_in, mlp_out):
    owners = msg.shape[0]
    rows = window.shape[1]
    channels = attn_out.shape[0]
    vmem = pl.BlockSpec(memory_space=pltpu.VMEM)
    smem = pl.BlockSpec(memory_space=pltpu.SMEM)
    return pl.pallas_call(
        owner_kernel,
        out_shape=jax.ShapeDtypeStruct((owners, MSG, 128), BF16),
        in_specs=[smem] + [vmem] * 8,
        out_specs=vmem,
        scratch_shapes=[
            pltpu.VMEM((owners * 8, 128), F32),
            pltpu.VMEM((rows, channels), BF16),
            pltpu.VMEM((rows, channels), BF16),
            pltpu.VMEM((rows, 2 * channels), BF16),
            pltpu.VMEM((rows, 128), I32),
            pltpu.VMEM((rows, channels), BF16),
            pltpu.VMEM((rows, channels), F32),
        ],
        compiler_params=pltpu.CompilerParams(vmem_limit_bytes=VMEM_LIMIT),
        name="owner_encode",
    )(span, msg, window, gain1, attn_in, attn_out, gain2, mlp_in, mlp_out)


def fill_cells(ids, cells, rows, token, pos, gain):
    hit = jnp.where(cells == ids, 1.0, 0.0)
    filled = dot(hit.astype(BF16), rows)
    seen = jnp.sum(hit, axis=1, keepdims=True)
    filled = jnp.where(seen > 0.5, filled, token)
    dec = (filled + pos.astype(F32)).astype(BF16)
    return dec, layer_norm(dec.astype(F32), gain).astype(BF16)


def edge_kernel(
    count_ref, starts_ref, back_ref, cells_ref, pos_ref, token_ref, gain_ref,
    rows_ref, dec_ref, first_ref, last_ref,
    left_scr, right_scr,
):
    owners = back_ref.shape[0]
    entries = cells_ref.shape[1]
    az, rad, height, channels = pos_ref.shape
    left_scr[...] = jnp.zeros(left_scr.shape, F32)
    right_scr[...] = jnp.zeros(right_scr.shape, F32)

    def take(o, carry):
        start = starts_ref[0, o]
        block = back_ref[o].astype(F32)
        left_scr[pl.ds(start, 16), :] = block[0:16]
        right_scr[pl.ds(start, 16), :] = block[16:32]
        left_scr[pl.ds(start + 16, 2), :] = block[32:34]
        right_scr[pl.ds(start + 16, 2), :] = block[34:36]
        return carry

    lax.fori_loop(0, owners, take, 0, unroll=8)
    rows = jnp.concatenate([left_scr[0:entries, :], right_scr[0:entries, :]], axis=1).astype(BF16)
    rows_ref[...] = rows
    cells = jnp.where(iota((1, entries), 1) < count_ref[0], cells_ref[...], -1)
    at = [(a, r) for r in (0, rad - 1) for a in range(az)]
    ids = jnp.concatenate(
        [iota((height, entries), 0) + (a * rad + r) * height for a, r in at], axis=0
    )
    pos = jnp.concatenate([pos_ref[a, r].astype(F32) for a, r in at], axis=0)
    dec, normed = fill_cells(ids, cells, rows, token_ref[...], pos, gain_ref[...])
    dec_ref[...] = dec.reshape(dec_ref.shape)
    first_ref[...] = normed[: az * height]
    last_ref[...] = normed[az * height :]


def place_edges(vis_count, starts, back, cells, pos, token, gain):
    az, rad, height, channels = pos.shape
    entries = cells.shape[1]
    vmem = pl.BlockSpec(memory_space=pltpu.VMEM)
    smem = pl.BlockSpec(memory_space=pltpu.SMEM)
    edges = jax.ShapeDtypeStruct((2, az * height, channels), BF16)
    edge = jax.ShapeDtypeStruct((az * height, channels), BF16)
    return pl.pallas_call(
        edge_kernel,
        out_shape=(jax.ShapeDtypeStruct((entries, channels), BF16), edges, edge, edge),
        in_specs=[smem, smem] + [vmem] * 5,
        out_specs=(vmem,) * 4,
        scratch_shapes=[pltpu.VMEM((entries + 24, 128), F32)] * 2,
        compiler_params=pltpu.CompilerParams(vmem_limit_bytes=VMEM_LIMIT),
        cost_estimate=pl.CostEstimate(flops=6 * 10**8, bytes_accessed=4 * 10**6, transcendentals=0),
        name="place_edges",
    )(vis_count, starts, back, cells, pos, token, gain)


def mid_kernel(
    count_ref, rows_ref, cells_ref, pos_ref, token_ref, gain_ref,
    dec_ref, normed_ref,
):
    entries = cells_ref.shape[1]
    az, rad, height, channels = pos_ref.shape
    size = (rad - 2) * height
    rows = rows_ref[...]
    cells = jnp.where(iota((1, entries), 1) < count_ref[0], cells_ref[...], -1)
    for a in range(0, az, 2):
        ids = jnp.concatenate(
            [iota((size, entries), 0) + (i * rad + 1) * height for i in (a, a + 1)], axis=0
        )
        pos = jnp.concatenate(
            [pos_ref[i, 1 : rad - 1].reshape(size, channels) for i in (a, a + 1)], axis=0
        )
        dec, normed = fill_cells(ids, cells, rows, token_ref[...], pos, gain_ref[...])
        dec_ref[a : a + 2] = dec.reshape(2, size, channels)
        normed_ref[a : a + 2] = normed.reshape(2, size, channels)


def place_mid(vis_count, rows, cells, pos, token, gain):
    az, rad, height, channels = pos.shape
    vmem = pl.BlockSpec(memory_space=pltpu.VMEM)
    smem = pl.BlockSpec(memory_space=pltpu.SMEM)
    mid = jax.ShapeDtypeStruct((az, (rad - 2) * height, channels), BF16)
    return pl.pallas_call(
        mid_kernel,
        out_shape=(mid, mid),
        in_specs=[smem] + [vmem] * 5,
        out_specs=(vmem, vmem),
        compiler_params=pltpu.CompilerParams(vmem_limit_bytes=VMEM_LIMIT),
        cost_estimate=pl.CostEstimate(flops=2 * 10**9, bytes_accessed=6 * 10**6, transcendentals=0),
        name="place_mid",
    )(vis_count, rows, cells, pos, token, gain)


def rim_kernel(mid_ref, edge0_ref, edge1_ref, low_ref, high_ref, first_ref, last_ref):
    az, size, channels = mid_ref.shape
    height = low_ref.shape[0] // az
    for a, ref in ((0, first_ref), (az - 1, last_ref)):
        part = slice(a * height, (a + 1) * height)
        ref[0:height] = low_ref[part]
        ref[height : 2 * height] = edge0_ref[part]
        ref[2 * height : 2 * height + size] = mid_ref[a]
        ref[2 * height + size : 3 * height + size] = edge1_ref[part]
        ref[3 * height + size :] = high_ref[part]


def rim_rows(mid, edge0, edge1, low, high):
    az, size, channels = mid.shape
    vmem = pl.BlockSpec(memory_space=pltpu.VMEM)
    out = jax.ShapeDtypeStruct((size + 4 * (low.shape[0] // az), channels), BF16)
    return pl.pallas_call(
        rim_kernel,
        out_shape=(out, out),
        in_specs=[vmem] * 5,
        out_specs=(vmem, vmem),
        compiler_params=pltpu.CompilerParams(vmem_limit_bytes=8 * 2**20),
        name="rim_rows",
    )(mid, edge0, edge1, low, high)


def widen(scr, at, rows, height):
    n, channels = rows.shape
    h = iota((n, 1), 0) % height
    values = rows.astype(F32)
    scr[at : at + n, channels : 2 * channels] = rows
    below = jnp.where(h == 0, 0.0, pltpu.roll(values, 1, 0))
    scr[at : at + n, 0:channels] = below.astype(BF16)
    above = jnp.where(h == height - 1, 0.0, pltpu.roll(values, n - 1, 0))
    scr[at : at + n, 2 * channels :] = above.astype(BF16)


def conv_kernel(
    mid_ref, edge0_ref, edge1_ref, low_ref, high_ref, mid_dec_ref, edge_dec_ref, weight_ref, bias_ref,
    out_ref, partial_ref,
    wide_scr, weight_scr, done_scr, weight_sems, out_sems,
):
    az, size, channels = mid_ref.shape
    height = low_ref.shape[0] // az
    plane = size + 2 * height
    pitch = plane + 2 * height
    loads = [
        pltpu.make_async_copy(weight_ref.at[pl.ds(3 * i, 3)], weight_scr.at[pl.ds(3 * i, 3)], weight_sems.at[i])
        for i in range(3)
    ]
    for load in loads:
        load.start()
    for a in range(az):
        base = a * pitch
        part = slice(a * height, (a + 1) * height)
        widen(wide_scr, base, low_ref[part], height)
        widen(wide_scr, base + height, edge0_ref[part], height)
        widen(wide_scr, base + 2 * height, mid_ref[a], height)
        widen(wide_scr, base + 2 * height + size, edge1_ref[part], height)
        widen(wide_scr, base + 3 * height + size, high_ref[part], height)
    for load in loads:
        load.wait()
    stores = []
    for a in range(az):
        total = jnp.broadcast_to(bias_ref[...], (plane, channels))
        for da in range(3):
            if not 0 <= a + da - 1 < az:
                continue
            for dr in range(3):
                at = (a + da - 1) * pitch + dr * height
                total = total + dot(wide_scr[at : at + plane, :], weight_scr[da * 3 + dr])
        if a in (0, az - 1):
            partial_ref[a // (az - 1)] = total
            continue
        part = slice(a * height, (a + 1) * height)
        dec = jnp.concatenate([edge_dec_ref[0, part], mid_dec_ref[a], edge_dec_ref[1, part]], axis=0)
        done_scr[a - 1] = (dec.astype(F32) + gelu(total)).astype(BF16)
        store = pltpu.make_async_copy(
            done_scr.at[a - 1], out_ref.at[pl.ds(a * plane, plane)], out_sems.at[a - 1]
        )
        store.start()
        stores.append(store)
    for store in stores:
        store.wait()


def conv_inner(mid, edge0, edge1, low, high, mid_dec, edge_dec, weight, bias):
    az, size, channels = mid.shape
    height = low.shape[0] // az
    plane = size + 2 * height
    vmem = pl.BlockSpec(memory_space=pltpu.VMEM)
    hbm = pl.BlockSpec(memory_space=pltpu.HBM)
    return pl.pallas_call(
        conv_kernel,
        out_shape=(
            jax.ShapeDtypeStruct((az * plane, channels), BF16),
            jax.ShapeDtypeStruct((2, plane, channels), F32),
        ),
        in_specs=[vmem] * 7 + [hbm, vmem],
        out_specs=(hbm, vmem),
        scratch_shapes=[
            pltpu.VMEM((az * (plane + 2 * height), 3 * channels), BF16),
            pltpu.VMEM(weight.shape, BF16),
            pltpu.VMEM((az - 2, plane, channels), BF16),
            pltpu.SemaphoreType.DMA((3,)),
            pltpu.SemaphoreType.DMA((az - 2,)),
        ],
        compiler_params=pltpu.CompilerParams(vmem_limit_bytes=VMEM_LIMIT),
        cost_estimate=pl.CostEstimate(flops=8 * 10**9, bytes_accessed=10**7, transcendentals=0),
        name="conv_inner",
    )(mid, edge0, edge1, low, high, mid_dec, edge_dec, weight, bias)


def conv_edge_kernel(
    low_ref, high_ref, partial_ref, mid_dec_ref, edge_dec_ref, weight_ref, given_ref,
    out_ref,
    wide_scr, weight_scr, done_scr, weight_sems, out_sems,
):
    az, size, channels = mid_dec_ref.shape
    plane = partial_ref.shape[1]
    height = (plane - size) // 2
    pitch = plane + 2 * height
    loads = [
        pltpu.make_async_copy(weight_ref.at[pl.ds(6 * i, 3)], weight_scr.at[pl.ds(3 * i, 3)], weight_sems.at[i])
        for i in range(2)
    ]
    for load in loads:
        load.start()
    widen(wide_scr, 0, low_ref[...], height)
    widen(wide_scr, pitch, high_ref[...], height)
    stores = []
    for i in range(2):
        a = i * (az - 1)
        loads[i].wait()
        total = partial_ref[i]
        for dr in range(3):
            at = i * pitch + dr * height
            total = total + dot(wide_scr[at : at + plane, :], weight_scr[i * 3 + dr])
        part = slice(a * height, (a + 1) * height)
        dec = jnp.concatenate([edge_dec_ref[0, part], mid_dec_ref[a], edge_dec_ref[1, part]], axis=0)
        done_scr[i] = (dec.astype(F32) + gelu(total)).astype(BF16)
        store = pltpu.make_async_copy(
            done_scr.at[i], out_ref.at[pl.ds(a * plane, plane)], out_sems.at[i]
        )
        store.start()
        stores.append(store)
    for store in stores:
        store.wait()


def conv_edges(low, high, partial, mid_dec, edge_dec, weight, given):
    plane, channels = partial.shape[1:]
    vmem = pl.BlockSpec(memory_space=pltpu.VMEM)
    hbm = pl.BlockSpec(memory_space=pltpu.HBM)
    return pl.pallas_call(
        conv_edge_kernel,
        out_shape=jax.ShapeDtypeStruct(given.shape, BF16),
        in_specs=[vmem] * 5 + [hbm, hbm],
        out_specs=hbm,
        scratch_shapes=[
            pltpu.VMEM((2 * low.shape[0], 3 * channels), BF16),
            pltpu.VMEM((6,) + weight.shape[1:], BF16),
            pltpu.VMEM((2, plane, channels), BF16),
            pltpu.SemaphoreType.DMA((2,)),
            pltpu.SemaphoreType.DMA((2,)),
        ],
        input_output_aliases={6: 0},
        compiler_params=pltpu.CompilerParams(vmem_limit_bytes=24 * 2**20),
        name="conv_edges",
    )(low, high, partial, mid_dec, edge_dec, weight, given)


def key_spans(window_ids, q_step):
    rows = window_ids.shape[0]
    blocks = window_ids.reshape(rows // q_step, q_step)
    low = jnp.sum(window_ids[None, :] < blocks[:, 0:1], axis=1, dtype=I32)
    high = jnp.sum(window_ids[None, :] <= blocks[:, q_step - 1 :], axis=1, dtype=I32)
    low = low // 128 * 128
    count = (high - low + 255) // 256
    low = jnp.minimum(low, rows - 256 * count)
    return jnp.stack([low, count])


def exchange(values):
    return lax.all_to_all(values, ("sector", "blk"), split_axis=0, concat_axis=0, tiled=True)


def body(
    visible_feats, grid_pos, vis_cells, vis_count, owner, slot, window, enc_gain1, attn_in,
    attn_out, enc_gain2, mlp_in, mlp_out, mask_token, dec_gain, conv_weight, conv_bias,
):
    n_sector = lax.axis_size("sector")
    n_blk = lax.axis_size("blk")
    owners = n_sector * n_blk
    az, rad, height, channels = grid_pos.shape
    cell_total = az * rad * height
    pos = grid_pos.reshape(cell_total, channels)
    cells = vis_cells.reshape(1, -1)
    message, starts = send_rows(
        vis_count, cells, owner.reshape(1, -1), slot.reshape(1, -1), visible_feats, pos, owners
    )
    message = exchange(message)
    back = owner_encode(
        key_spans(window[0], 128), message, window, enc_gain1.reshape(1, -1), attn_in, attn_out,
        enc_gain2.reshape(1, -1), mlp_in, mlp_out,
    )
    back = exchange(back)
    token = mask_token.reshape(1, -1)
    gain = dec_gain.reshape(1, -1)
    rows, edge_dec, edge0, edge1 = place_edges(vis_count, starts, back, cells, grid_pos, token, gain)
    outward = [(i, i + 1) for i in range(n_blk - 1)]
    inward = [(t, s) for s, t in outward]
    rad_low = lax.ppermute(edge1, "blk", outward)
    rad_high = lax.ppermute(edge0, "blk", inward)
    mid_dec, mid = place_mid(vis_count, rows, cells, grid_pos, token, gain)
    first, last = rim_rows(mid, edge0, edge1, rad_low, rad_high)
    up = [(i, (i + 1) % n_sector) for i in range(n_sector)]
    down = [(t, s) for s, t in up]
    az_low = lax.ppermute(last, "sector", up)
    az_high = lax.ppermute(first, "sector", down)
    weight = conv_weight.reshape(9, 3 * channels, channels)
    inner, partial = conv_inner(
        mid, edge0, edge1, rad_low, rad_high, mid_dec, edge_dec, weight, conv_bias.reshape(1, -1)
    )
    decoded = conv_edges(az_low, az_high, partial, mid_dec, edge_dec, weight, inner)
    return decoded.reshape(az, rad, height, channels)


def solution(mesh):
    lists = P(("sector", "blk"))
    return jax.shard_map(
        body,
        mesh=mesh,
        in_specs=(
            P(("sector", "blk"), None),
            P("sector", "blk", None, None),
            lists,
            lists,
            lists,
            lists,
            P(("sector", "blk"), None),
        )
        + (P(),) * 10,
        out_specs=P("sector", "blk", None, None),
        check_vma=False,
    )
```

```python
import jax
import jax.numpy as jnp
from jax import lax
from jax.experimental import pallas as pl
from jax.experimental.pallas import tpu as pltpu
from jax.sharding import PartitionSpec as P

HEAD_DIM = 32
EPSILON = 1e-05
F32 = jnp.float32
BF16 = jnp.bfloat16
I32 = jnp.int32
CAP = 18
MSG = 40


def iota(shape, dim):
    return lax.broadcasted_iota(I32, shape, dim)


def one_hot(mask):
    return jnp.where(mask, 1.0, 0.0).astype(BF16)


def dot(a, b):
    return jnp.dot(a, b, preferred_element_type=F32)


def dot_nt(a, b):
    return lax.dot_general(a, b, (((1,), (1,)), ((), ())), preferred_element_type=F32)


def eye_mask(n):
    return iota((n, n), 0) == iota((n, n), 1)


def layer_norm(values, gain_vec):
    center = values - jnp.mean(values, axis=-1, keepdims=True)
    spread = jnp.mean(center * center, axis=-1, keepdims=True)
    return center * lax.rsqrt(spread + EPSILON) * gain_vec


def gelu(x):
    return 0.5 * x * (1.0 + jnp.tanh(0.7978845608028654 * (x + 0.044715 * (x * x * x))))


def send_kernel(
    count_ref, cells_ref, owner_ref, slot_ref, vis_ref, pos_ref,
    msg_ref, starts_ref,
    left_scr, right_scr, meta_scr, starts_smem, sem,
    cells_in, owner_in, slot_in, vis_in, pos_in, in_sems,
):
    entries = cells_ref.shape[1]
    owners = msg_ref.shape[0]
    cell_total = pos_ref.shape[0]
    loads = [
        pltpu.make_async_copy(src, dst, in_sems.at[i])
        for i, (src, dst) in enumerate(
            [
                (owner_ref, owner_in),
                (cells_ref, cells_in),
                (slot_ref, slot_in),
                (pos_ref, pos_in),
                (vis_ref, vis_in),
            ]
        )
    ]
    for load in loads:
        load.start()
    for load in loads[:3]:
        load.wait()
    entry = iota((1, entries), 1)
    live = entry < count_ref[0]
    owner = jnp.where(live, owner_in[...], owners)
    owner_id = iota((owners, entries), 0)
    start_col = jnp.sum(jnp.where(owner < owner_id, 1.0, 0.0), axis=1, keepdims=True)
    start_row = jnp.sum(jnp.where(eye_mask(owners), start_col, 0.0), axis=0, keepdims=True)
    starts_ref[...] = start_row.astype(I32)
    copy = pltpu.make_async_copy(starts_ref, starts_smem, sem)
    copy.start()
    belongs = owner == owner_id
    first = jnp.sum(jnp.where(belongs, start_col, 0.0), axis=0, keepdims=True)
    within = jnp.where(live, entry - first.astype(I32), 64)
    cells = cells_in[...]
    slots = slot_in[...]
    parts = jnp.concatenate(
        [cells >> 6, cells & 63, slots >> 5, slots & 31, within, within, within, within], axis=0
    ).astype(F32).astype(BF16)
    eye = one_hot(eye_mask(128))
    lane = iota((128, 128), 1)
    cell_cols = []
    meta_parts = []
    for b in range(entries // 128):
        turned = dot_nt(eye, parts[:, b * 128 : (b + 1) * 128])
        cell_cols.append((turned[:, 0:1] * 64.0 + turned[:, 1:2]).astype(I32))
        place = turned[:, 4:5].astype(I32)
        meta_parts.append(
            jnp.where(
                lane == place,
                turned[:, 2:3] + 1.0,
                jnp.where(lane == place + 32, turned[:, 3:4], 0.0),
            ).astype(BF16)
        )
    meta_scr[...] = dot(one_hot(belongs), jnp.concatenate(meta_parts, axis=0))
    for load in loads[3:]:
        load.wait()
    step = 512
    for b in range(entries // step):
        col = jnp.concatenate(cell_cols[b * step // 128 : (b + 1) * step // 128], axis=0)
        pick = one_hot(iota((step, cell_total), 1) == col)
        rows = vis_in[b * step : (b + 1) * step, :].astype(F32) + dot(pick, pos_in[...])
        rows = rows.astype(BF16).astype(F32)
        left_scr[b * step : (b + 1) * step, :] = rows[:, 0:128]
        right_scr[b * step : (b + 1) * step, :] = rows[:, 128:256]
    left_scr[entries:, :] = jnp.zeros((left_scr.shape[0] - entries, 128), F32)
    right_scr[entries:, :] = jnp.zeros((right_scr.shape[0] - entries, 128), F32)
    copy.wait()
    sub = iota((8, 128), 0)

    def emit(o, carry):
        start = starts_smem[0, o]
        msg_ref[o, 0:16, :] = left_scr[pl.ds(start, 16), :].astype(BF16)
        msg_ref[o, 16:32, :] = right_scr[pl.ds(start, 16), :].astype(BF16)
        left = left_scr[pl.ds(start + 16, 8), :]
        right = pltpu.roll(right_scr[pl.ds(start + 16, 8), :], 2, 0)
        last = jnp.where(sub < 2, left, jnp.where(sub < 4, right, meta_scr[pl.ds(o, 1), :]))
        msg_ref[o, 32:40, :] = last.astype(BF16)
        return carry

    lax.fori_loop(0, owners, emit, 0, unroll=4)


def send_rows(vis_count, cells, owner, slot, vis, pos, owners):
    entries = vis.shape[0]
    vmem = pl.BlockSpec(memory_space=pltpu.VMEM)
    smem = pl.BlockSpec(memory_space=pltpu.SMEM)
    return pl.pallas_call(
        send_kernel,
        out_shape=(
            jax.ShapeDtypeStruct((owners, MSG, 128), BF16),
            jax.ShapeDtypeStruct((1, owners), I32),
        ),
        in_specs=[smem] + [pl.BlockSpec(memory_space=pltpu.HBM)] * 5,
        out_specs=(vmem, vmem),
        scratch_shapes=[
            pltpu.VMEM((entries + 24, 128), F32),
            pltpu.VMEM((entries + 24, 128), F32),
            pltpu.VMEM((owners, 128), F32),
            pltpu.SMEM((1, owners), I32),
            pltpu.SemaphoreType.DMA,
            pltpu.VMEM(cells.shape, I32),
            pltpu.VMEM(cells.shape, I32),
            pltpu.VMEM(cells.shape, I32),
            pltpu.VMEM(vis.shape, BF16),
            pltpu.VMEM(pos.shape, BF16),
            pltpu.SemaphoreType.DMA((5,)),
        ],
        compiler_params=pltpu.CompilerParams(vmem_limit_bytes=60 * 2**20),
        name="send_rows",
    )(vis_count, cells, owner, slot, vis, pos)


def owner_kernel(
    msg_ref, window_ref, gain1_ref, attn_in_ref, attn_out_ref, gain2_ref,
    mlp_in_ref, mlp_out_ref,
    back_ref,
    order_scr, tail_scr, q_scr, k_scr, v_scr, win_scr, att_scr, x_scr,
):
    owners = msg_ref.shape[0]
    rows = window_ref.shape[1]
    channels = attn_out_ref.shape[0]
    head_count = channels // HEAD_DIM
    full = 16 * owners
    ids = window_ref[...]
    windows = range(4)
    length = [jnp.sum(jnp.where(ids == w, 1.0, 0.0)).astype(I32) for w in windows]
    old = [sum(length[:w], jnp.int32(0)) for w in windows]
    new = []
    for w in windows:
        ahead = [
            jnp.where(length[v] >= length[w] if v < w else length[v] > length[w], length[v], 0)
            for v in windows
            if v != w
        ]
        new.append(sum(ahead, jnp.int32(0)))
    end = [new[w] + length[w] for w in windows]
    place_row = iota((1, rows), 1)
    order = sum([jnp.where(place_row >= end[w], 1, 0) for w in windows])
    order_scr[...] = order
    tail_scr[...] = msg_ref[:, 32:40, :].astype(F32).reshape(owners * 8, 128)

    def tail(j):
        return tail_scr[pl.ds(j, owners, stride=8), :]

    meta = tail(4).astype(BF16)
    place = iota((128, full), 0)
    inner = iota((128, full), 1) & 15
    spread = (
        jnp.where(place == inner, 32.0, 0.0) + jnp.where(place == inner + 32, 1.0, 0.0)
    ).astype(BF16)
    wide = dot(meta, spread)
    of_sender = (iota((owners, full), 1) >> 4) == iota((owners, full), 0)
    slot_full = jnp.sum(jnp.where(of_sender, wide, 0.0), axis=0, keepdims=True) - 32.0
    eye = eye_mask(owners)
    meta32 = meta.astype(F32)
    tail_cols = [meta32[:, j : j + 1] * 32.0 + meta32[:, j + 32 : j + 33] - 32.0 for j in (16, 17)]
    tail_slots = [jnp.sum(jnp.where(eye, c, 0.0), axis=0, keepdims=True) for c in tail_cols]
    slot_row = jnp.concatenate([slot_full] + tail_slots, axis=1).astype(I32)
    moved = slot_row + (new[0] - old[0])
    for w in windows[1:]:
        moved = jnp.where(slot_row >= old[w], slot_row + (new[w] - old[w]), moved)
    slot_row = jnp.where(slot_row >= 0, moved, -1)
    left = msg_ref[:, 0:16, :].reshape(full, 128)
    right = msg_ref[:, 16:32, :].reshape(full, 128)
    main = jnp.concatenate([left, right], axis=1)
    rest = jnp.concatenate(
        [
            jnp.concatenate([tail(0), tail(2)], axis=1),
            jnp.concatenate([tail(1), tail(3)], axis=1),
        ],
        axis=0,
    ).astype(BF16)
    step = 256
    step = 1024
    for b in range(rows // step):
        part = slice(b * step, (b + 1) * step)
        sel = one_hot(slot_row == iota((step, slot_row.shape[1]), 0) + b * step)
        x = dot(sel[:, :full], main) + dot(sel[:, full:], rest)
        x_scr[part, :] = x
        normed = layer_norm(x, gain1_ref[...]).astype(BF16)
        projected = dot(normed, attn_in_ref[...]).astype(BF16)
        q_scr[part, :] = projected[:, :channels]
        k_scr[part, :] = projected[:, channels : 2 * channels]
        ones = jnp.ones((step, 128), BF16)
        v_scr[part, 0:128] = projected[:, 2 * channels : 2 * channels + 128]
        v_scr[part, 128:256] = ones
        v_scr[part, 256:384] = projected[:, 2 * channels + 128 :]
        v_scr[part, 384:512] = ones
    q_step = 256
    eye_q = eye_mask(128)
    for i in range(rows // 128):
        part = slice(i * 128, (i + 1) * 128)
        ids = order_scr[:, part].astype(F32)
        ids = jnp.sum(jnp.where(eye_q, ids, 0.0), axis=1, keepdims=True)
        win_scr[part, :] = jnp.broadcast_to(ids, (128, 128)).astype(I32)
    head_of_lane = iota((1, channels), 1) // HEAD_DIM
    lane_head = (iota((1, channels), 1) & 127) // HEAD_DIM
    head_mask = [one_hot(head_of_lane == h) for h in range(head_count)]
    scale = HEAD_DIM ** (-0.5) * 1.4426950408889634
    stack = 4
    half_heads = head_count // 2

    def attend(qi, key_count, key_start):
        q_rows = pl.ds(pl.multiple_of(qi * q_step, q_step), q_step)
        k_rows = pl.ds(key_start, key_count)
        q = q_scr[q_rows, :]
        keys = k_scr[k_rows, :]
        q_win = win_scr[q_rows, :]
        q_win = jnp.concatenate([q_win] * (key_count // 128), axis=1)
        bias = jnp.where(q_win == order_scr[:, k_rows], 0.0, -jnp.inf)
        bias = jnp.concatenate([bias] * stack, axis=0)
        groups = []
        for half in range(2):
            for g in range(half_heads // 4):
                groups.append((half, range(g * 4, (g + 1) * 4)))

        def scores(half, heads):
            queries = jnp.concatenate([q * head_mask[half * half_heads + h] for h in heads], axis=0)
            return dot_nt(queries, keys) + bias

        def weigh(s):
            top = jnp.max(s, axis=1, keepdims=True)
            return jnp.exp2(((s - top) * scale).astype(BF16))

        totals = [None, None]

        def mix(half, heads, e):
            o = dot(e, v_scr[k_rows, 256 * half : 256 * half + 256])
            total = totals[half]
            for i, h in enumerate(heads):
                block = o[i * q_step : (i + 1) * q_step]
                total = block if total is None else jnp.where(lane_head == h, block, total)
            totals[half] = total

        ahead = scores(*groups[0])
        held = None
        for i in range(len(groups)):
            s = ahead
            if i + 1 < len(groups):
                ahead = scores(*groups[i + 1])
            e = weigh(s)
            if held is not None:
                mix(*held)
            held = (*groups[i], e)
        mix(*held)

        for half in range(2):
            total = totals[half]
            att_scr[q_rows, 128 * half : 128 * half + 128] = (
                total[:, 0:128] * (1.0 / total[:, 128:256])
            ).astype(BF16)

    def q_block(qi, carry):
        first = qi * q_step
        low = jnp.int32(0)
        high = jnp.int32(rows)
        for w in windows:
            low = jnp.maximum(low, jnp.where(new[w] <= first, new[w], 0))
            high = jnp.minimum(high, jnp.where(end[w] >= first + q_step, end[w], rows))
        low = (low >> 7) << 7
        count = (high - low + 255) >> 8
        low = jnp.minimum(low, rows - 256 * count)
        for n in range(1, rows // 256 + 1):

            @pl.when(count == n)
            def _():
                attend(qi, 256 * n, pl.multiple_of(low, 128))

        return carry

    lax.fori_loop(0, rows // q_step, q_block, 0)
    step = 256
    for b in range(rows // step):
        part = slice(b * step, (b + 1) * step)
        x = x_scr[part, :] + dot(att_scr[part, :], attn_out_ref[...])
        normed = layer_norm(x, gain2_ref[...]).astype(BF16)
        hidden = gelu(dot(normed, mlp_in_ref[...])).astype(BF16)
        q_scr[part, :] = (x + dot(hidden, mlp_out_ref[...])).astype(BF16)
    slot_f = slot_row.astype(F32)
    eye128 = eye_mask(128)
    step = 512
    for b in range(full // step + 1):
        size = step if b < full // step else 2 * owners
        cols = []
        for i in range(size // 128):
            at = b * step + i * 128
            cols.append(
                jnp.sum(jnp.where(eye128, slot_f[:, at : at + 128], 0.0), axis=1, keepdims=True)
            )
        col = jnp.concatenate(cols, axis=0).astype(I32)
        pick = one_hot(iota((size, rows), 1) == col)
        out = dot(pick, q_scr[...])
        if b < full // step:
            o = b * step // 16
            n = step // 16
            out = out.astype(BF16)
            back_ref[o : o + n, 0:16, :] = out[:, 0:128].reshape(n, 16, 128)
            back_ref[o : o + n, 16:32, :] = out[:, 128:256].reshape(n, 16, 128)
        else:
            for j in range(2):
                tail_scr[pl.ds(j, owners, stride=8), :] = out[j * owners : (j + 1) * owners, 0:128]
                tail_scr[pl.ds(j + 2, owners, stride=8), :] = out[
                    j * owners : (j + 1) * owners, 128:256
                ]
            back_ref[:, 32:40, :] = tail_scr[...].astype(BF16).reshape(owners, 8, 128)


def owner_encode(msg, window, gain1, attn_in, attn_out, gain2, mlp_in, mlp_out):
    owners = msg.shape[0]
    rows = window.shape[1]
    channels = attn_out.shape[0]
    vmem = pl.BlockSpec(memory_space=pltpu.VMEM)
    return pl.pallas_call(
        owner_kernel,
        out_shape=jax.ShapeDtypeStruct((owners, MSG, 128), BF16),
        in_specs=[vmem] * 8,
        out_specs=vmem,
        scratch_shapes=[
            pltpu.VMEM((1, rows), I32),
            pltpu.VMEM((owners * 8, 128), F32),
            pltpu.VMEM((rows, channels), BF16),
            pltpu.VMEM((rows, channels), BF16),
            pltpu.VMEM((rows, 2 * channels), BF16),
            pltpu.VMEM((rows, 128), I32),
            pltpu.VMEM((rows, channels), BF16),
            pltpu.VMEM((rows, channels), F32),
        ],
        compiler_params=pltpu.CompilerParams(vmem_limit_bytes=40 * 2**20),
        name="owner_encode",
    )(msg, window, gain1, attn_in, attn_out, gain2, mlp_in, mlp_out)


def fill_cells(ids, cells, rows, token, pos, gain):
    hit = jnp.where(cells == ids, 1.0, 0.0)
    filled = dot(hit.astype(BF16), rows)
    seen = jnp.sum(hit, axis=1, keepdims=True)
    filled = jnp.where(seen > 0.5, filled, token)
    dec = (filled + pos.astype(F32)).astype(BF16)
    return dec, layer_norm(dec.astype(F32), gain).astype(BF16)


def edge_kernel(
    count_ref, starts_ref, back_ref, cells_ref, pos_ref, token_ref, gain_ref,
    rows_ref, dec_ref, first_ref, last_ref,
    left_scr, right_scr,
):
    owners = back_ref.shape[0]
    entries = cells_ref.shape[1]
    az, rad, height, channels = pos_ref.shape
    left_scr[...] = jnp.zeros(left_scr.shape, F32)
    right_scr[...] = jnp.zeros(right_scr.shape, F32)

    def take(o, carry):
        start = starts_ref[0, o]
        block = back_ref[o].astype(F32)
        left_scr[pl.ds(start, 16), :] = block[0:16]
        right_scr[pl.ds(start, 16), :] = block[16:32]
        left_scr[pl.ds(start + 16, 2), :] = block[32:34]
        right_scr[pl.ds(start + 16, 2), :] = block[34:36]
        return carry

    lax.fori_loop(0, owners, take, 0, unroll=8)
    rows = jnp.concatenate([left_scr[0:entries, :], right_scr[0:entries, :]], axis=1).astype(BF16)
    rows_ref[...] = rows
    cells = jnp.where(iota((1, entries), 1) < count_ref[0], cells_ref[...], -1)
    at = [(a, r) for r in (0, rad - 1) for a in range(az)]
    ids = jnp.concatenate(
        [iota((height, entries), 0) + (a * rad + r) * height for a, r in at], axis=0
    )
    pos = jnp.concatenate([pos_ref[a, r].astype(F32) for a, r in at], axis=0)
    dec, normed = fill_cells(ids, cells, rows, token_ref[...], pos, gain_ref[...])
    dec_ref[...] = dec.reshape(dec_ref.shape)
    first_ref[...] = normed[: az * height]
    last_ref[...] = normed[az * height :]


def place_edges(vis_count, starts, back, cells, pos, token, gain):
    az, rad, height, channels = pos.shape
    entries = cells.shape[1]
    vmem = pl.BlockSpec(memory_space=pltpu.VMEM)
    smem = pl.BlockSpec(memory_space=pltpu.SMEM)
    edges = jax.ShapeDtypeStruct((2, az * height, channels), BF16)
    edge = jax.ShapeDtypeStruct((az * height, channels), BF16)
    return pl.pallas_call(
        edge_kernel,
        out_shape=(jax.ShapeDtypeStruct((entries, channels), BF16), edges, edge, edge),
        in_specs=[smem, smem] + [vmem] * 5,
        out_specs=(vmem,) * 4,
        scratch_shapes=[pltpu.VMEM((entries + 24, 128), F32)] * 2,
        compiler_params=pltpu.CompilerParams(vmem_limit_bytes=24 * 2**20),
        cost_estimate=pl.CostEstimate(flops=6 * 10**8, bytes_accessed=4 * 10**6, transcendentals=0),
        name="place_edges",
    )(vis_count, starts, back, cells, pos, token, gain)


def mid_kernel(
    count_ref, rows_ref, cells_ref, pos_ref, token_ref, gain_ref,
    dec_ref, normed_ref,
):
    entries = cells_ref.shape[1]
    az, rad, height, channels = pos_ref.shape
    size = (rad - 2) * height
    rows = rows_ref[...]
    cells = jnp.where(iota((1, entries), 1) < count_ref[0], cells_ref[...], -1)
    for a in range(0, az, 2):
        ids = jnp.concatenate(
            [iota((size, entries), 0) + (i * rad + 1) * height for i in (a, a + 1)], axis=0
        )
        pos = jnp.concatenate(
            [pos_ref[i, 1 : rad - 1].reshape(size, channels) for i in (a, a + 1)], axis=0
        )
        dec, normed = fill_cells(ids, cells, rows, token_ref[...], pos, gain_ref[...])
        dec_ref[a : a + 2] = dec.reshape(2, size, channels)
        normed_ref[a : a + 2] = normed.reshape(2, size, channels)


def place_mid(vis_count, rows, cells, pos, token, gain):
    az, rad, height, channels = pos.shape
    vmem = pl.BlockSpec(memory_space=pltpu.VMEM)
    smem = pl.BlockSpec(memory_space=pltpu.SMEM)
    mid = jax.ShapeDtypeStruct((az, (rad - 2) * height, channels), BF16)
    return pl.pallas_call(
        mid_kernel,
        out_shape=(mid, mid),
        in_specs=[smem] + [vmem] * 5,
        out_specs=(vmem, vmem),
        compiler_params=pltpu.CompilerParams(vmem_limit_bytes=24 * 2**20),
        cost_estimate=pl.CostEstimate(flops=2 * 10**9, bytes_accessed=6 * 10**6, transcendentals=0),
        name="place_mid",
    )(vis_count, rows, cells, pos, token, gain)


def rim_kernel(mid_ref, edge0_ref, edge1_ref, low_ref, high_ref, first_ref, last_ref):
    az, size, channels = mid_ref.shape
    height = low_ref.shape[0] // az
    for a, ref in ((0, first_ref), (az - 1, last_ref)):
        part = slice(a * height, (a + 1) * height)
        ref[0:height] = low_ref[part]
        ref[height : 2 * height] = edge0_ref[part]
        ref[2 * height : 2 * height + size] = mid_ref[a]
        ref[2 * height + size : 3 * height + size] = edge1_ref[part]
        ref[3 * height + size :] = high_ref[part]


def rim_rows(mid, edge0, edge1, low, high):
    az, size, channels = mid.shape
    vmem = pl.BlockSpec(memory_space=pltpu.VMEM)
    out = jax.ShapeDtypeStruct((size + 4 * (low.shape[0] // az), channels), BF16)
    return pl.pallas_call(
        rim_kernel,
        out_shape=(out, out),
        in_specs=[vmem] * 5,
        out_specs=(vmem, vmem),
        compiler_params=pltpu.CompilerParams(vmem_limit_bytes=8 * 2**20),
        name="rim_rows",
    )(mid, edge0, edge1, low, high)


def widen(scr, at, rows, height):
    n, channels = rows.shape
    h = iota((n, 1), 0) % height
    values = rows.astype(F32)
    scr[at : at + n, channels : 2 * channels] = rows
    below = jnp.where(h == 0, 0.0, pltpu.roll(values, 1, 0))
    scr[at : at + n, 0:channels] = below.astype(BF16)
    above = jnp.where(h == height - 1, 0.0, pltpu.roll(values, n - 1, 0))
    scr[at : at + n, 2 * channels :] = above.astype(BF16)


def conv_kernel(
    mid_ref, edge0_ref, edge1_ref, low_ref, high_ref, mid_dec_ref, edge_dec_ref, weight_ref, bias_ref,
    out_ref, partial_ref,
    wide_scr, done_scr, out_sems,
):
    az, size, channels = mid_ref.shape
    height = low_ref.shape[0] // az
    plane = size + 2 * height
    pitch = plane + 2 * height

    def spread(a):
        base = a * pitch
        part = slice(a * height, (a + 1) * height)
        widen(wide_scr, base, low_ref[part], height)
        widen(wide_scr, base + height, edge0_ref[part], height)
        widen(wide_scr, base + 2 * height, mid_ref[a], height)
        widen(wide_scr, base + 2 * height + size, edge1_ref[part], height)
        widen(wide_scr, base + 3 * height + size, high_ref[part], height)

    def taps(a):
        total = jnp.broadcast_to(bias_ref[...], (plane, channels))
        for da in range(3):
            if not 0 <= a + da - 1 < az:
                continue
            for dr in range(3):
                at = (a + da - 1) * pitch + dr * height
                total = total + dot(wide_scr[at : at + plane, :], weight_ref[da * 3 + dr])
        return total

    def finish(a, total):
        if a in (0, az - 1):
            partial_ref[a // (az - 1)] = total
            return
        part = slice(a * height, (a + 1) * height)
        dec = jnp.concatenate([edge_dec_ref[0, part], mid_dec_ref[a], edge_dec_ref[1, part]], axis=0)
        done_scr[a - 1] = (dec.astype(F32) + gelu(total)).astype(BF16)

    spread(0)
    spread(1)
    spread(2)
    stores = []
    held = taps(0)
    for a in range(1, az + 1):
        if a < az:
            total = taps(a)
        if a + 2 < az:
            spread(a + 2)
        finish(a - 1, held)
        held = total
        if 0 < a - 1 < az - 1:
            store = pltpu.make_async_copy(
                done_scr.at[a - 2], out_ref.at[pl.ds((a - 1) * plane, plane)], out_sems.at[a - 2]
            )
            stores.append(store)
            store.start()
    for store in stores:
        store.wait()


def conv_inner(mid, edge0, edge1, low, high, mid_dec, edge_dec, weight, bias):
    az, size, channels = mid.shape
    height = low.shape[0] // az
    plane = size + 2 * height
    vmem = pl.BlockSpec(memory_space=pltpu.VMEM)
    hbm = pl.BlockSpec(memory_space=pltpu.HBM)
    return pl.pallas_call(
        conv_kernel,
        out_shape=(
            jax.ShapeDtypeStruct((az * plane, channels), BF16),
            jax.ShapeDtypeStruct((2, plane, channels), F32),
        ),
        in_specs=[vmem] * 9,
        out_specs=(hbm, vmem),
        scratch_shapes=[
            pltpu.VMEM((az * (plane + 2 * height), 3 * channels), BF16),
            pltpu.VMEM((az - 2, plane, channels), BF16),
            pltpu.SemaphoreType.DMA((az - 2,)),
        ],
        compiler_params=pltpu.CompilerParams(vmem_limit_bytes=32 * 2**20),
        cost_estimate=pl.CostEstimate(flops=8 * 10**9, bytes_accessed=10**7, transcendentals=0),
        name="conv_inner",
    )(mid, edge0, edge1, low, high, mid_dec, edge_dec, weight, bias)


def conv_edge_kernel(
    low_ref, high_ref, partial_ref, mid_dec_ref, edge_dec_ref, weight_ref, given_ref,
    out_ref,
    wide_scr, done_scr, out_sems,
):
    az, size, channels = mid_dec_ref.shape
    plane = partial_ref.shape[1]
    height = (plane - size) // 2
    pitch = plane + 2 * height
    widen(wide_scr, 0, low_ref[...], height)
    widen(wide_scr, pitch, high_ref[...], height)
    stores = []
    for i in range(2):
        a = i * (az - 1)
        total = partial_ref[i]
        for dr in range(3):
            at = i * pitch + dr * height
            total = total + dot(wide_scr[at : at + plane, :], weight_ref[i * 6 + dr])
        part = slice(a * height, (a + 1) * height)
        dec = jnp.concatenate([edge_dec_ref[0, part], mid_dec_ref[a], edge_dec_ref[1, part]], axis=0)
        done_scr[i] = (dec.astype(F32) + gelu(total)).astype(BF16)
        store = pltpu.make_async_copy(
            done_scr.at[i], out_ref.at[pl.ds(a * plane, plane)], out_sems.at[i]
        )
        store.start()
        stores.append(store)
    for store in stores:
        store.wait()


def conv_edges(low, high, partial, mid_dec, edge_dec, weight, given):
    plane, channels = partial.shape[1:]
    vmem = pl.BlockSpec(memory_space=pltpu.VMEM)
    hbm = pl.BlockSpec(memory_space=pltpu.HBM)
    return pl.pallas_call(
        conv_edge_kernel,
        out_shape=jax.ShapeDtypeStruct(given.shape, BF16),
        in_specs=[vmem] * 6 + [hbm],
        out_specs=hbm,
        scratch_shapes=[
            pltpu.VMEM((2 * low.shape[0], 3 * channels), BF16),
            pltpu.VMEM((2, plane, channels), BF16),
            pltpu.SemaphoreType.DMA((2,)),
        ],
        input_output_aliases={6: 0},
        compiler_params=pltpu.CompilerParams(vmem_limit_bytes=16 * 2**20),
        name="conv_edges",
    )(low, high, partial, mid_dec, edge_dec, weight, given)


def exchange(values):
    return lax.all_to_all(values, ("sector", "blk"), split_axis=0, concat_axis=0, tiled=True)


def body(
    visible_feats, grid_pos, vis_cells, vis_count, owner, slot, window, enc_gain1, attn_in,
    attn_out, enc_gain2, mlp_in, mlp_out, mask_token, dec_gain, conv_weight, conv_bias,
):
    n_sector = lax.axis_size("sector")
    n_blk = lax.axis_size("blk")
    owners = n_sector * n_blk
    az, rad, height, channels = grid_pos.shape
    cell_total = az * rad * height
    pos = grid_pos.reshape(cell_total, channels)
    cells = vis_cells.reshape(1, -1)
    message, starts = send_rows(
        vis_count, cells, owner.reshape(1, -1), slot.reshape(1, -1), visible_feats, pos, owners
    )
    message = exchange(message)
    back = owner_encode(
        message, window, enc_gain1.reshape(1, -1), attn_in, attn_out,
        enc_gain2.reshape(1, -1), mlp_in, mlp_out,
    )
    back = exchange(back)
    token = mask_token.reshape(1, -1)
    gain = dec_gain.reshape(1, -1)
    rows, edge_dec, edge0, edge1 = place_edges(vis_count, starts, back, cells, grid_pos, token, gain)
    outward = [(i, i + 1) for i in range(n_blk - 1)]
    inward = [(t, s) for s, t in outward]
    rad_low = lax.ppermute(edge1, "blk", outward)
    rad_high = lax.ppermute(edge0, "blk", inward)
    mid_dec, mid = place_mid(vis_count, rows, cells, grid_pos, token, gain)
    first, last = rim_rows(mid, edge0, edge1, rad_low, rad_high)
    up = [(i, (i + 1) % n_sector) for i in range(n_sector)]
    down = [(t, s) for s, t in up]
    az_low = lax.ppermute(last, "sector", up)
    az_high = lax.ppermute(first, "sector", down)
    weight = conv_weight.reshape(9, 3 * channels, channels)
    inner, partial = conv_inner(
        mid, edge0, edge1, rad_low, rad_high, mid_dec, edge_dec, weight, conv_bias.reshape(1, -1)
    )
    decoded = conv_edges(az_low, az_high, partial, mid_dec, edge_dec, weight, inner)
    return decoded.reshape(az, rad, height, channels)


def solution(mesh):
    lists = P(("sector", "blk"))
    return jax.shard_map(
        body,
        mesh=mesh,
        in_specs=(
            P(("sector", "blk"), None),
            P("sector", "blk", None, None),
            lists,
            lists,
            lists,
            lists,
            P(("sector", "blk"), None),
        )
        + (P(),) * 10,
        out_specs=P("sector", "blk", None, None),
        check_vma=False,
    )
```

```python
import jax
import jax.numpy as jnp
from jax import lax
from jax.experimental import pallas as pl
from jax.experimental.pallas import tpu as pltpu
from jax.sharding import PartitionSpec as P

HEAD_DIM = 32
EPSILON = 1e-05
F32 = jnp.float32
BF16 = jnp.bfloat16
I32 = jnp.int32
CAP = 18
MSG = 40


def iota(shape, dim):
    return lax.broadcasted_iota(I32, shape, dim)


def one_hot(mask):
    return jnp.where(mask, 1.0, 0.0).astype(BF16)


def dot(a, b):
    return jnp.dot(a, b, preferred_element_type=F32)


def dot_nt(a, b):
    return lax.dot_general(a, b, (((1,), (1,)), ((), ())), preferred_element_type=F32)


def eye_mask(n):
    return iota((n, n), 0) == iota((n, n), 1)


def layer_norm(values, gain_vec):
    center = values - jnp.mean(values, axis=-1, keepdims=True)
    spread = jnp.mean(center * center, axis=-1, keepdims=True)
    return center * lax.rsqrt(spread + EPSILON) * gain_vec


def gelu(x):
    return 0.5 * x * (1.0 + jnp.tanh(0.7978845608028654 * (x + 0.044715 * (x * x * x))))


def send_kernel(
    count_ref, cells_ref, owner_ref, slot_ref, vis_ref, pos_ref,
    msg_ref, starts_ref,
    left_scr, right_scr, meta_scr, starts_smem, sem,
    cells_in, owner_in, slot_in, vis_in, pos_in, in_sems,
):
    entries = cells_ref.shape[1]
    owners = msg_ref.shape[0]
    cell_total = pos_ref.shape[0]
    loads = [
        pltpu.make_async_copy(src, dst, in_sems.at[i])
        for i, (src, dst) in enumerate(
            [
                (owner_ref, owner_in),
                (cells_ref, cells_in),
                (slot_ref, slot_in),
                (pos_ref, pos_in),
                (vis_ref, vis_in),
            ]
        )
    ]
    for load in loads:
        load.start()
    for load in loads[:3]:
        load.wait()
    entry = iota((1, entries), 1)
    live = entry < count_ref[0]
    owner = jnp.where(live, owner_in[...], owners)
    owner_id = iota((owners, entries), 0)
    start_col = jnp.sum(jnp.where(owner < owner_id, 1.0, 0.0), axis=1, keepdims=True)
    start_row = jnp.sum(jnp.where(eye_mask(owners), start_col, 0.0), axis=0, keepdims=True)
    starts_ref[...] = start_row.astype(I32)
    copy = pltpu.make_async_copy(starts_ref, starts_smem, sem)
    copy.start()
    belongs = owner == owner_id
    first = jnp.sum(jnp.where(belongs, start_col, 0.0), axis=0, keepdims=True)
    within = jnp.where(live, entry - first.astype(I32), 64)
    cells = cells_in[...]
    slots = slot_in[...]
    parts = jnp.concatenate(
        [cells >> 6, cells & 63, slots >> 5, slots & 31, within, within, within, within], axis=0
    ).astype(F32).astype(BF16)
    eye = one_hot(eye_mask(128))
    lane = iota((128, 128), 1)
    cell_cols = []
    meta_parts = []
    for b in range(entries // 128):
        turned = dot_nt(eye, parts[:, b * 128 : (b + 1) * 128])
        cell_cols.append((turned[:, 0:1] * 64.0 + turned[:, 1:2]).astype(I32))
        place = turned[:, 4:5].astype(I32)
        meta_parts.append(
            jnp.where(
                lane == place,
                turned[:, 2:3] + 1.0,
                jnp.where(lane == place + 32, turned[:, 3:4], 0.0),
            ).astype(BF16)
        )
    meta_scr[...] = dot(one_hot(belongs), jnp.concatenate(meta_parts, axis=0))
    for load in loads[3:]:
        load.wait()
    step = 512
    for b in range(entries // step):
        col = jnp.concatenate(cell_cols[b * step // 128 : (b + 1) * step // 128], axis=0)
        pick = one_hot(iota((step, cell_total), 1) == col)
        rows = vis_in[b * step : (b + 1) * step, :].astype(F32) + dot(pick, pos_in[...])
        rows = rows.astype(BF16).astype(F32)
        left_scr[b * step : (b + 1) * step, :] = rows[:, 0:128]
        right_scr[b * step : (b + 1) * step, :] = rows[:, 128:256]
    left_scr[entries:, :] = jnp.zeros((left_scr.shape[0] - entries, 128), F32)
    right_scr[entries:, :] = jnp.zeros((right_scr.shape[0] - entries, 128), F32)
    copy.wait()
    sub = iota((8, 128), 0)

    def emit(o, carry):
        start = starts_smem[0, o]
        msg_ref[o, 0:16, :] = left_scr[pl.ds(start, 16), :].astype(BF16)
        msg_ref[o, 16:32, :] = right_scr[pl.ds(start, 16), :].astype(BF16)
        left = left_scr[pl.ds(start + 16, 8), :]
        right = pltpu.roll(right_scr[pl.ds(start + 16, 8), :], 2, 0)
        last = jnp.where(sub < 2, left, jnp.where(sub < 4, right, meta_scr[pl.ds(o, 1), :]))
        msg_ref[o, 32:40, :] = last.astype(BF16)
        return carry

    lax.fori_loop(0, owners, emit, 0, unroll=4)


def send_rows(vis_count, cells, owner, slot, vis, pos, owners):
    entries = vis.shape[0]
    vmem = pl.BlockSpec(memory_space=pltpu.VMEM)
    smem = pl.BlockSpec(memory_space=pltpu.SMEM)
    return pl.pallas_call(
        send_kernel,
        out_shape=(
            jax.ShapeDtypeStruct((owners, MSG, 128), BF16),
            jax.ShapeDtypeStruct((1, owners), I32),
        ),
        in_specs=[smem] + [pl.BlockSpec(memory_space=pltpu.HBM)] * 5,
        out_specs=(vmem, vmem),
        scratch_shapes=[
            pltpu.VMEM((entries + 24, 128), F32),
            pltpu.VMEM((entries + 24, 128), F32),
            pltpu.VMEM((owners, 128), F32),
            pltpu.SMEM((1, owners), I32),
            pltpu.SemaphoreType.DMA,
            pltpu.VMEM(cells.shape, I32),
            pltpu.VMEM(cells.shape, I32),
            pltpu.VMEM(cells.shape, I32),
            pltpu.VMEM(vis.shape, BF16),
            pltpu.VMEM(pos.shape, BF16),
            pltpu.SemaphoreType.DMA((5,)),
        ],
        compiler_params=pltpu.CompilerParams(vmem_limit_bytes=60 * 2**20),
        name="send_rows",
    )(vis_count, cells, owner, slot, vis, pos)


def owner_kernel(
    msg_ref, window_ref, gain1_ref, attn_in_ref, attn_out_ref, gain2_ref,
    mlp_in_ref, mlp_out_ref,
    back_ref,
    order_scr, tail_scr, q_scr, k_scr, v_scr, win_scr, att_scr, x_scr,
):
    owners = msg_ref.shape[0]
    rows = window_ref.shape[1]
    channels = attn_out_ref.shape[0]
    head_count = channels // HEAD_DIM
    full = 16 * owners
    ids = window_ref[...]
    windows = range(4)
    length = [jnp.sum(jnp.where(ids == w, 1.0, 0.0)).astype(I32) for w in windows]
    old = [sum(length[:w], jnp.int32(0)) for w in windows]
    new = []
    for w in windows:
        ahead = [
            jnp.where(length[v] >= length[w] if v < w else length[v] > length[w], length[v], 0)
            for v in windows
            if v != w
        ]
        new.append(sum(ahead, jnp.int32(0)))
    end = [new[w] + length[w] for w in windows]
    place_row = iota((1, rows), 1)
    order = sum([jnp.where(place_row >= end[w], 1, 0) for w in windows])
    order_scr[...] = order
    tail_scr[...] = msg_ref[:, 32:40, :].astype(F32).reshape(owners * 8, 128)

    def tail(j):
        return tail_scr[pl.ds(j, owners, stride=8), :]

    meta = tail(4).astype(BF16)
    place = iota((128, full), 0)
    inner = iota((128, full), 1) & 15
    spread = (
        jnp.where(place == inner, 32.0, 0.0) + jnp.where(place == inner + 32, 1.0, 0.0)
    ).astype(BF16)
    wide = dot(meta, spread)
    of_sender = (iota((owners, full), 1) >> 4) == iota((owners, full), 0)
    slot_full = jnp.sum(jnp.where(of_sender, wide, 0.0), axis=0, keepdims=True) - 32.0
    eye = eye_mask(owners)
    meta32 = meta.astype(F32)
    tail_cols = [meta32[:, j : j + 1] * 32.0 + meta32[:, j + 32 : j + 33] - 32.0 for j in (16, 17)]
    tail_slots = [jnp.sum(jnp.where(eye, c, 0.0), axis=0, keepdims=True) for c in tail_cols]
    slot_row = jnp.concatenate([slot_full] + tail_slots, axis=1).astype(I32)
    moved = slot_row + (new[0] - old[0])
    for w in windows[1:]:
        moved = jnp.where(slot_row >= old[w], slot_row + (new[w] - old[w]), moved)
    slot_row = jnp.where(slot_row >= 0, moved, -1)
    left = msg_ref[:, 0:16, :].reshape(full, 128)
    right = msg_ref[:, 16:32, :].reshape(full, 128)
    main = jnp.concatenate([left, right], axis=1)
    rest = jnp.concatenate(
        [
            jnp.concatenate([tail(0), tail(2)], axis=1),
            jnp.concatenate([tail(1), tail(3)], axis=1),
        ],
        axis=0,
    ).astype(BF16)
    step = 256
    step = 1024
    for b in range(rows // step):
        part = slice(b * step, (b + 1) * step)
        sel = one_hot(slot_row == iota((step, slot_row.shape[1]), 0) + b * step)
        x = dot(sel[:, :full], main) + dot(sel[:, full:], rest)
        x_scr[part, :] = x
        normed = layer_norm(x, gain1_ref[...]).astype(BF16)
        projected = dot(normed, attn_in_ref[...]).astype(BF16)
        q_scr[part, :] = projected[:, :channels]
        k_scr[part, :] = projected[:, channels : 2 * channels]
        ones = jnp.ones((step, 128), BF16)
        v_scr[part, 0:128] = projected[:, 2 * channels : 2 * channels + 128]
        v_scr[part, 128:256] = ones
        v_scr[part, 256:384] = projected[:, 2 * channels + 128 :]
        v_scr[part, 384:512] = ones
    q_step = 256
    eye_q = eye_mask(128)
    for i in range(rows // 128):
        part = slice(i * 128, (i + 1) * 128)
        ids = order_scr[:, part].astype(F32)
        ids = jnp.sum(jnp.where(eye_q, ids, 0.0), axis=1, keepdims=True)
        win_scr[part, :] = jnp.broadcast_to(ids, (128, 128)).astype(I32)
    head_of_lane = iota((1, channels), 1) // HEAD_DIM
    lane_head = (iota((1, channels), 1) & 127) // HEAD_DIM
    head_mask = [one_hot(head_of_lane == h) for h in range(head_count)]
    scale = HEAD_DIM ** (-0.5) * 1.4426950408889634
    stack = 4
    half_heads = head_count // 2

    def attend(qi, key_count, key_start):
        q_rows = pl.ds(pl.multiple_of(qi * q_step, q_step), q_step)
        k_rows = pl.ds(key_start, key_count)
        q = q_scr[q_rows, :]
        keys = k_scr[k_rows, :]
        q_win = win_scr[q_rows, :]
        q_win = jnp.concatenate([q_win] * (key_count // 128), axis=1)
        bias = jnp.where(q_win == order_scr[:, k_rows], 0.0, -jnp.inf)
        bias = jnp.concatenate([bias] * stack, axis=0)
        groups = []
        for half in range(2):
            for g in range(half_heads // 4):
                groups.append((half, range(g * 4, (g + 1) * 4)))

        def scores(half, heads):
            queries = jnp.concatenate([q * head_mask[half * half_heads + h] for h in heads], axis=0)
            return dot_nt(queries, keys) + bias

        def weigh(s):
            top = jnp.max(s, axis=1, keepdims=True)
            return jnp.exp2(((s - top) * scale).astype(BF16))

        totals = [None, None]

        def mix(half, heads, e):
            o = dot(e, v_scr[k_rows, 256 * half : 256 * half + 256])
            total = totals[half]
            for i, h in enumerate(heads):
                block = o[i * q_step : (i + 1) * q_step]
                total = block if total is None else jnp.where(lane_head == h, block, total)
            totals[half] = total

        ahead = scores(*groups[0])
        held = None
        for i in range(len(groups)):
            s = ahead
            if i + 1 < len(groups):
                ahead = scores(*groups[i + 1])
            e = weigh(s)
            if held is not None:
                mix(*held)
            held = (*groups[i], e)
        mix(*held)

        for half in range(2):
            total = totals[half]
            att_scr[q_rows, 128 * half : 128 * half + 128] = (
                total[:, 0:128] * (1.0 / total[:, 128:256])
            ).astype(BF16)

    def q_block(qi, carry):
        first = qi * q_step
        low = jnp.int32(0)
        high = jnp.int32(rows)
        for w in windows:
            low = jnp.maximum(low, jnp.where(new[w] <= first, new[w], 0))
            high = jnp.minimum(high, jnp.where(end[w] >= first + q_step, end[w], rows))
        low = (low >> 7) << 7
        count = (high - low + 255) >> 8
        low = jnp.minimum(low, rows - 256 * count)
        for n in range(1, rows // 256 + 1):

            @pl.when(count == n)
            def _():
                attend(qi, 256 * n, pl.multiple_of(low, 128))

        return carry

    lax.fori_loop(0, rows // q_step, q_block, 0)
    step = 256
    for b in range(rows // step):
        part = slice(b * step, (b + 1) * step)
        x = x_scr[part, :] + dot(att_scr[part, :], attn_out_ref[...])
        normed = layer_norm(x, gain2_ref[...]).astype(BF16)
        hidden = gelu(dot(normed, mlp_in_ref[...])).astype(BF16)
        q_scr[part, :] = (x + dot(hidden, mlp_out_ref[...])).astype(BF16)
    slot_f = slot_row.astype(F32)
    eye128 = eye_mask(128)
    step = 512
    for b in range(full // step + 1):
        size = step if b < full // step else 2 * owners
        cols = []
        for i in range(size // 128):
            at = b * step + i * 128
            cols.append(
                jnp.sum(jnp.where(eye128, slot_f[:, at : at + 128], 0.0), axis=1, keepdims=True)
            )
        col = jnp.concatenate(cols, axis=0).astype(I32)
        pick = one_hot(iota((size, rows), 1) == col)
        out = dot(pick, q_scr[...])
        if b < full // step:
            o = b * step // 16
            n = step // 16
            out = out.astype(BF16)
            back_ref[o : o + n, 0:16, :] = out[:, 0:128].reshape(n, 16, 128)
            back_ref[o : o + n, 16:32, :] = out[:, 128:256].reshape(n, 16, 128)
        else:
            for j in range(2):
                tail_scr[pl.ds(j, owners, stride=8), :] = out[j * owners : (j + 1) * owners, 0:128]
                tail_scr[pl.ds(j + 2, owners, stride=8), :] = out[
                    j * owners : (j + 1) * owners, 128:256
                ]
            back_ref[:, 32:40, :] = tail_scr[...].astype(BF16).reshape(owners, 8, 128)


def owner_encode(msg, window, gain1, attn_in, attn_out, gain2, mlp_in, mlp_out):
    owners = msg.shape[0]
    rows = window.shape[1]
    channels = attn_out.shape[0]
    vmem = pl.BlockSpec(memory_space=pltpu.VMEM)
    return pl.pallas_call(
        owner_kernel,
        out_shape=jax.ShapeDtypeStruct((owners, MSG, 128), BF16),
        in_specs=[vmem] * 8,
        out_specs=vmem,
        scratch_shapes=[
            pltpu.VMEM((1, rows), I32),
            pltpu.VMEM((owners * 8, 128), F32),
            pltpu.VMEM((rows, channels), BF16),
            pltpu.VMEM((rows, channels), BF16),
            pltpu.VMEM((rows, 2 * channels), BF16),
            pltpu.VMEM((rows, 128), I32),
            pltpu.VMEM((rows, channels), BF16),
            pltpu.VMEM((rows, channels), F32),
        ],
        compiler_params=pltpu.CompilerParams(vmem_limit_bytes=40 * 2**20),
        name="owner_encode",
    )(msg, window, gain1, attn_in, attn_out, gain2, mlp_in, mlp_out)


def hit_kernel(
    count_ref, cells_ref, pos_ref, token_ref,
    edge_hit_ref, edge_base_ref, mid_hit_ref, mid_base_ref,
):
    entries = cells_ref.shape[1]
    az, rad, height, channels = pos_ref.shape
    cells = jnp.where(iota((1, entries), 1) < count_ref[0], cells_ref[...], -1)

    def prepare(first, rows, pos):
        hit = jnp.where(cells == iota((rows, entries), 0) + first, 1.0, 0.0)
        seen = jnp.sum(hit, axis=1, keepdims=True)
        pos = pos.astype(F32)
        return hit.astype(BF16), jnp.where(seen > 0.5, pos, token_ref[...] + pos)

    for a in range(az):
        for side, r in ((0, 0), (1, rad - 1)):
            at = (side * az + a) * height
            hit, base = prepare((a * rad + r) * height, height, pos_ref[a, r])
            edge_hit_ref[at : at + height, :] = hit
            edge_base_ref[at : at + height, :] = base
        size = (rad - 2) * height
        hit, base = prepare(
            (a * rad + 1) * height, size, pos_ref[a, 1 : rad - 1].reshape(size, channels)
        )
        mid_hit_ref[a * size : (a + 1) * size, :] = hit
        mid_base_ref[a * size : (a + 1) * size, :] = base


def cell_hits(vis_count, cells, pos, token):
    az, rad, height, channels = pos.shape
    entries = cells.shape[1]
    vmem = pl.BlockSpec(memory_space=pltpu.VMEM)
    smem = pl.BlockSpec(memory_space=pltpu.SMEM)
    edge = 2 * az * height
    mid = az * (rad - 2) * height
    return pl.pallas_call(
        hit_kernel,
        out_shape=(
            jax.ShapeDtypeStruct((edge, entries), BF16),
            jax.ShapeDtypeStruct((edge, channels), F32),
            jax.ShapeDtypeStruct((mid, entries), BF16),
            jax.ShapeDtypeStruct((mid, channels), F32),
        ),
        in_specs=[smem] + [vmem] * 3,
        out_specs=(vmem,) * 4,
        compiler_params=pltpu.CompilerParams(vmem_limit_bytes=24 * 2**20),
        cost_estimate=pl.CostEstimate(flops=3 * 10**9, bytes_accessed=15 * 10**6, transcendentals=0),
        name="cell_hits",
    )(vis_count, cells, pos, token)


def edge_kernel(
    starts_ref, back_ref, hit_ref, base_ref, gain_ref,
    rows_ref, dec_ref, first_ref, last_ref,
    left_scr, right_scr,
):
    owners = back_ref.shape[0]
    entries = hit_ref.shape[1]
    half = first_ref.shape[0]
    left_scr[...] = jnp.zeros(left_scr.shape, F32)
    right_scr[...] = jnp.zeros(right_scr.shape, F32)

    def take(o, carry):
        start = starts_ref[0, o]
        block = back_ref[o].astype(F32)
        left_scr[pl.ds(start, 16), :] = block[0:16]
        right_scr[pl.ds(start, 16), :] = block[16:32]
        left_scr[pl.ds(start + 16, 2), :] = block[32:34]
        right_scr[pl.ds(start + 16, 2), :] = block[34:36]
        return carry

    lax.fori_loop(0, owners, take, 0, unroll=8)
    rows = jnp.concatenate([left_scr[0:entries, :], right_scr[0:entries, :]], axis=1).astype(BF16)
    rows_ref[...] = rows
    dec = (dot(hit_ref[...], rows) + base_ref[...]).astype(BF16)
    normed = layer_norm(dec.astype(F32), gain_ref[...]).astype(BF16)
    dec_ref[...] = dec.reshape(dec_ref.shape)
    first_ref[...] = normed[:half]
    last_ref[...] = normed[half:]


def place_edges(starts, back, hit, base, gain):
    entries = hit.shape[1]
    cells, channels = base.shape
    vmem = pl.BlockSpec(memory_space=pltpu.VMEM)
    smem = pl.BlockSpec(memory_space=pltpu.SMEM)
    edges = jax.ShapeDtypeStruct((2, cells // 2, channels), BF16)
    edge = jax.ShapeDtypeStruct((cells // 2, channels), BF16)
    return pl.pallas_call(
        edge_kernel,
        out_shape=(jax.ShapeDtypeStruct((entries, channels), BF16), edges, edge, edge),
        in_specs=[smem] + [vmem] * 4,
        out_specs=(vmem,) * 4,
        scratch_shapes=[pltpu.VMEM((entries + 24, 128), F32)] * 2,
        compiler_params=pltpu.CompilerParams(vmem_limit_bytes=16 * 2**20),
        cost_estimate=pl.CostEstimate(flops=6 * 10**8, bytes_accessed=4 * 10**6, transcendentals=0),
        name="place_edges",
    )(starts, back, hit, base, gain)


def mid_kernel(rows_ref, hit_ref, base_ref, gain_ref, dec_ref, normed_ref):
    az, size, channels = dec_ref.shape
    for a in range(0, az, 2):
        part = slice(a * size, (a + 2) * size)
        dec = (dot(hit_ref[part, :], rows_ref[...]) + base_ref[part, :]).astype(BF16)
        normed = layer_norm(dec.astype(F32), gain_ref[...]).astype(BF16)
        dec_ref[a : a + 2] = dec.reshape(2, size, channels)
        normed_ref[a : a + 2] = normed.reshape(2, size, channels)


def place_mid(az, rows, hit, base, gain):
    cells, channels = base.shape
    vmem = pl.BlockSpec(memory_space=pltpu.VMEM)
    mid = jax.ShapeDtypeStruct((az, cells // az, channels), BF16)
    return pl.pallas_call(
        mid_kernel,
        out_shape=(mid, mid),
        in_specs=[vmem] * 4,
        out_specs=(vmem, vmem),
        compiler_params=pltpu.CompilerParams(vmem_limit_bytes=16 * 2**20),
        cost_estimate=pl.CostEstimate(flops=2 * 10**9, bytes_accessed=6 * 10**6, transcendentals=0),
        name="place_mid",
    )(rows, hit, base, gain)


def ring_ends():
    place = lax.axis_index("blk")
    return place == 0, place == lax.axis_size("blk") - 1


def rim_kernel(mid_ref, edge0_ref, edge1_ref, low_ref, high_ref, first_ref, last_ref):
    az, size, channels = mid_ref.shape
    height = low_ref.shape[0] // az
    inside, outside = ring_ends()
    for a, ref in ((0, first_ref), (az - 1, last_ref)):
        part = slice(a * height, (a + 1) * height)
        ref[0:height] = jnp.where(inside, 0.0, low_ref[part].astype(F32)).astype(BF16)
        ref[height : 2 * height] = edge0_ref[part]
        ref[2 * height : 2 * height + size] = mid_ref[a]
        ref[2 * height + size : 3 * height + size] = edge1_ref[part]
        ref[3 * height + size :] = jnp.where(outside, 0.0, high_ref[part].astype(F32)).astype(BF16)


def rim_rows(mid, edge0, edge1, low, high):
    az, size, channels = mid.shape
    vmem = pl.BlockSpec(memory_space=pltpu.VMEM)
    out = jax.ShapeDtypeStruct((size + 4 * (low.shape[0] // az), channels), BF16)
    return pl.pallas_call(
        rim_kernel,
        out_shape=(out, out),
        in_specs=[vmem] * 5,
        out_specs=(vmem, vmem),
        compiler_params=pltpu.CompilerParams(vmem_limit_bytes=8 * 2**20),
        name="rim_rows",
    )(mid, edge0, edge1, low, high)


def widen(scr, at, rows, height, drop=None):
    n, channels = rows.shape
    h = iota((n, 1), 0) % height
    values = rows.astype(F32)
    if drop is not None:
        values = jnp.where(drop, 0.0, values)
        rows = values.astype(BF16)
    scr[at : at + n, channels : 2 * channels] = rows
    below = jnp.where(h == 0, 0.0, pltpu.roll(values, 1, 0))
    scr[at : at + n, 0:channels] = below.astype(BF16)
    above = jnp.where(h == height - 1, 0.0, pltpu.roll(values, n - 1, 0))
    scr[at : at + n, 2 * channels :] = above.astype(BF16)


def conv_kernel(
    mid_ref, edge0_ref, edge1_ref, low_ref, high_ref, mid_dec_ref, edge_dec_ref, weight_ref, bias_ref,
    out_ref, partial_ref,
    wide_scr, done_scr, out_sems,
):
    az, size, channels = mid_ref.shape
    height = low_ref.shape[0] // az
    plane = size + 2 * height
    pitch = plane + 2 * height
    inside, outside = ring_ends()

    def spread(a):
        base = a * pitch
        part = slice(a * height, (a + 1) * height)
        widen(wide_scr, base, low_ref[part], height, inside)
        widen(wide_scr, base + height, edge0_ref[part], height)
        widen(wide_scr, base + 2 * height, mid_ref[a], height)
        widen(wide_scr, base + 2 * height + size, edge1_ref[part], height)
        widen(wide_scr, base + 3 * height + size, high_ref[part], height, outside)

    def taps(a):
        total = jnp.broadcast_to(bias_ref[...], (plane, channels))
        for da in range(3):
            if not 0 <= a + da - 1 < az:
                continue
            for dr in range(3):
                at = (a + da - 1) * pitch + dr * height
                total = total + dot(wide_scr[at : at + plane, :], weight_ref[da * 3 + dr])
        return total

    def finish(a, total):
        if a in (0, az - 1):
            partial_ref[a // (az - 1)] = total
            return
        part = slice(a * height, (a + 1) * height)
        dec = jnp.concatenate([edge_dec_ref[0, part], mid_dec_ref[a], edge_dec_ref[1, part]], axis=0)
        done_scr[a - 1] = (dec.astype(F32) + gelu(total)).astype(BF16)

    spread(0)
    spread(1)
    spread(2)
    stores = []
    held = taps(0)
    for a in range(1, az + 1):
        if a < az:
            total = taps(a)
        if a + 2 < az:
            spread(a + 2)
        finish(a - 1, held)
        held = total
        if 0 < a - 1 < az - 1:
            store = pltpu.make_async_copy(
                done_scr.at[a - 2], out_ref.at[pl.ds((a - 1) * plane, plane)], out_sems.at[a - 2]
            )
            stores.append(store)
            store.start()
    for store in stores:
        store.wait()


def conv_inner(mid, edge0, edge1, low, high, mid_dec, edge_dec, weight, bias):
    az, size, channels = mid.shape
    height = low.shape[0] // az
    plane = size + 2 * height
    vmem = pl.BlockSpec(memory_space=pltpu.VMEM)
    hbm = pl.BlockSpec(memory_space=pltpu.HBM)
    return pl.pallas_call(
        conv_kernel,
        out_shape=(
            jax.ShapeDtypeStruct((az * plane, channels), BF16),
            jax.ShapeDtypeStruct((2, plane, channels), F32),
        ),
        in_specs=[vmem] * 9,
        out_specs=(hbm, vmem),
        scratch_shapes=[
            pltpu.VMEM((az * (plane + 2 * height), 3 * channels), BF16),
            pltpu.VMEM((az - 2, plane, channels), BF16),
            pltpu.SemaphoreType.DMA((az - 2,)),
        ],
        compiler_params=pltpu.CompilerParams(vmem_limit_bytes=32 * 2**20),
        cost_estimate=pl.CostEstimate(flops=8 * 10**9, bytes_accessed=10**7, transcendentals=0),
        name="conv_inner",
    )(mid, edge0, edge1, low, high, mid_dec, edge_dec, weight, bias)


def conv_edge_kernel(
    low_ref, high_ref, partial_ref, mid_dec_ref, edge_dec_ref, weight_ref, given_ref,
    out_ref,
    wide_scr, done_scr, out_sems,
):
    az, size, channels = mid_dec_ref.shape
    plane = partial_ref.shape[1]
    height = (plane - size) // 2
    pitch = plane + 2 * height
    widen(wide_scr, 0, low_ref[...], height)
    widen(wide_scr, pitch, high_ref[...], height)
    stores = []
    for i in range(2):
        a = i * (az - 1)
        total = partial_ref[i]
        for dr in range(3):
            at = i * pitch + dr * height
            total = total + dot(wide_scr[at : at + plane, :], weight_ref[i * 6 + dr])
        part = slice(a * height, (a + 1) * height)
        dec = jnp.concatenate([edge_dec_ref[0, part], mid_dec_ref[a], edge_dec_ref[1, part]], axis=0)
        done_scr[i] = (dec.astype(F32) + gelu(total)).astype(BF16)
        store = pltpu.make_async_copy(
            done_scr.at[i], out_ref.at[pl.ds(a * plane, plane)], out_sems.at[i]
        )
        store.start()
        stores.append(store)
    for store in stores:
        store.wait()


def conv_edges(low, high, partial, mid_dec, edge_dec, weight, given):
    plane, channels = partial.shape[1:]
    vmem = pl.BlockSpec(memory_space=pltpu.VMEM)
    hbm = pl.BlockSpec(memory_space=pltpu.HBM)
    return pl.pallas_call(
        conv_edge_kernel,
        out_shape=jax.ShapeDtypeStruct(given.shape, BF16),
        in_specs=[vmem] * 6 + [hbm],
        out_specs=hbm,
        scratch_shapes=[
            pltpu.VMEM((2 * low.shape[0], 3 * channels), BF16),
            pltpu.VMEM((2, plane, channels), BF16),
            pltpu.SemaphoreType.DMA((2,)),
        ],
        input_output_aliases={6: 0},
        compiler_params=pltpu.CompilerParams(vmem_limit_bytes=16 * 2**20),
        name="conv_edges",
    )(low, high, partial, mid_dec, edge_dec, weight, given)


def exchange(values):
    return lax.all_to_all(values, ("sector", "blk"), split_axis=0, concat_axis=0, tiled=True)


def body(
    visible_feats, grid_pos, vis_cells, vis_count, owner, slot, window, enc_gain1, attn_in,
    attn_out, enc_gain2, mlp_in, mlp_out, mask_token, dec_gain, conv_weight, conv_bias,
):
    n_sector = lax.axis_size("sector")
    n_blk = lax.axis_size("blk")
    owners = n_sector * n_blk
    az, rad, height, channels = grid_pos.shape
    cell_total = az * rad * height
    pos = grid_pos.reshape(cell_total, channels)
    cells = vis_cells.reshape(1, -1)
    message, starts = send_rows(
        vis_count, cells, owner.reshape(1, -1), slot.reshape(1, -1), visible_feats, pos, owners
    )
    message = exchange(message)
    back = owner_encode(
        message, window, enc_gain1.reshape(1, -1), attn_in, attn_out,
        enc_gain2.reshape(1, -1), mlp_in, mlp_out,
    )
    back, count_later, cells_later = lax.optimization_barrier((back, vis_count, cells))
    edge_hit, edge_base, mid_hit, mid_base = cell_hits(
        count_later, cells_later, grid_pos, mask_token.reshape(1, -1)
    )
    back = exchange(back)
    gain = dec_gain.reshape(1, -1)
    rows, edge_dec, edge0, edge1 = place_edges(starts, back, edge_hit, edge_base, gain)
    outward = [(i, (i + 1) % n_blk) for i in range(n_blk)]
    inward = [(t, s) for s, t in outward]
    rad_low = lax.ppermute(edge1, "blk", outward)
    rad_high = lax.ppermute(edge0, "blk", inward)
    mid_dec, mid = place_mid(az, rows, mid_hit, mid_base, gain)
    first, last = rim_rows(mid, edge0, edge1, rad_low, rad_high)
    up = [(i, (i + 1) % n_sector) for i in range(n_sector)]
    down = [(t, s) for s, t in up]
    az_low = lax.ppermute(last, "sector", up)
    az_high = lax.ppermute(first, "sector", down)
    weight = conv_weight.reshape(9, 3 * channels, channels)
    inner, partial = conv_inner(
        mid, edge0, edge1, rad_low, rad_high, mid_dec, edge_dec, weight, conv_bias.reshape(1, -1)
    )
    decoded = conv_edges(az_low, az_high, partial, mid_dec, edge_dec, weight, inner)
    return decoded.reshape(az, rad, height, channels)


def solution(mesh):
    lists = P(("sector", "blk"))
    return jax.shard_map(
        body,
        mesh=mesh,
        in_specs=(
            P(("sector", "blk"), None),
            P("sector", "blk", None, None),
            lists,
            lists,
            lists,
            lists,
            P(("sector", "blk"), None),
        )
        + (P(),) * 10,
        out_specs=P("sector", "blk", None, None),
        check_vma=False,
    )
```

```python
import jax
import jax.numpy as jnp
from jax import lax
from jax.experimental import pallas as pl
from jax.experimental.pallas import tpu as pltpu
from jax.sharding import PartitionSpec as P

HEAD_DIM = 32
EPSILON = 1e-05
F32 = jnp.float32
BF16 = jnp.bfloat16
I16 = jnp.int16
I32 = jnp.int32
CAP = 18
MSG = 40


def iota(shape, dim):
    return lax.broadcasted_iota(I32, shape, dim)


def one_hot(mask):
    return jnp.where(mask, 1.0, 0.0).astype(BF16)


def match(col, row):
    n, k = col.shape[0], row.shape[1]
    col = jnp.broadcast_to(col, (n, 128)).astype(I16)
    row = jnp.broadcast_to(row, (16, k)).astype(I16)
    col = jnp.concatenate([col] * (k // 128), axis=1)
    row = jnp.concatenate([row] * (n // 16), axis=0)
    return jnp.where(col == row, jnp.ones((), BF16), jnp.zeros((), BF16))


def dot(a, b):
    return jnp.dot(a, b, preferred_element_type=F32)


def dot_nt(a, b):
    return lax.dot_general(a, b, (((1,), (1,)), ((), ())), preferred_element_type=F32)


def eye_mask(n):
    return iota((n, n), 0) == iota((n, n), 1)


def layer_norm(values, gain_vec):
    center = values - jnp.mean(values, axis=-1, keepdims=True)
    spread = jnp.mean(center * center, axis=-1, keepdims=True)
    return center * lax.rsqrt(spread + EPSILON) * gain_vec


def gelu(x):
    return 0.5 * x * (1.0 + jnp.tanh(0.7978845608028654 * (x + 0.044715 * (x * x * x))))


def send_kernel(
    count_ref, cells_ref, owner_ref, slot_ref, vis_ref, pos_ref,
    msg_ref, starts_ref,
    left_scr, right_scr, meta_scr, starts_smem, sem,
    cells_in, owner_in, slot_in, vis_in, pos_in, in_sems,
):
    entries = cells_ref.shape[1]
    owners = msg_ref.shape[0]
    cell_total = pos_ref.shape[0]
    loads = [
        pltpu.make_async_copy(src, dst, in_sems.at[i])
        for i, (src, dst) in enumerate(
            [
                (owner_ref, owner_in),
                (cells_ref, cells_in),
                (slot_ref, slot_in),
                (pos_ref, pos_in),
                (vis_ref, vis_in),
            ]
        )
    ]
    for load in loads:
        load.start()
    for load in loads[:3]:
        load.wait()
    entry = iota((1, entries), 1)
    live = entry < count_ref[0]
    owner = jnp.where(live, owner_in[...], owners)
    owner_id = iota((owners, entries), 0)
    start_col = jnp.sum(jnp.where(owner < owner_id, 1.0, 0.0), axis=1, keepdims=True)
    start_row = jnp.sum(jnp.where(eye_mask(owners), start_col, 0.0), axis=0, keepdims=True)
    starts_ref[...] = start_row.astype(I32)
    copy = pltpu.make_async_copy(starts_ref, starts_smem, sem)
    copy.start()
    belongs = owner == owner_id
    first = jnp.sum(jnp.where(belongs, start_col, 0.0), axis=0, keepdims=True)
    within = jnp.where(live, entry - first.astype(I32), 64)
    cells = cells_in[...]
    slots = slot_in[...]
    parts = jnp.concatenate(
        [cells >> 6, cells & 63, slots >> 5, slots & 31, within, within, within, within], axis=0
    ).astype(F32).astype(BF16)
    eye = one_hot(eye_mask(128))
    lane = iota((128, 128), 1)
    cell_cols = []
    meta_parts = []
    for b in range(entries // 128):
        turned = dot_nt(eye, parts[:, b * 128 : (b + 1) * 128])
        cell_cols.append((turned[:, 0:1] * 64.0 + turned[:, 1:2]).astype(I32))
        place = turned[:, 4:5].astype(I32)
        meta_parts.append(
            jnp.where(
                lane == place,
                turned[:, 2:3] + 1.0,
                jnp.where(lane == place + 32, turned[:, 3:4], 0.0),
            ).astype(BF16)
        )
    meta_scr[...] = dot(one_hot(belongs), jnp.concatenate(meta_parts, axis=0))
    for load in loads[3:]:
        load.wait()
    step = 512
    for b in range(entries // step):
        col = jnp.concatenate(cell_cols[b * step // 128 : (b + 1) * step // 128], axis=0)
        pick = match(col, iota((1, cell_total), 1))
        rows = vis_in[b * step : (b + 1) * step, :].astype(F32) + dot(pick, pos_in[...])
        rows = rows.astype(BF16).astype(F32)
        left_scr[b * step : (b + 1) * step, :] = rows[:, 0:128]
        right_scr[b * step : (b + 1) * step, :] = rows[:, 128:256]
    left_scr[entries:, :] = jnp.zeros((left_scr.shape[0] - entries, 128), F32)
    right_scr[entries:, :] = jnp.zeros((right_scr.shape[0] - entries, 128), F32)
    copy.wait()
    sub = iota((8, 128), 0)

    def emit(o, carry):
        start = starts_smem[0, o]
        msg_ref[o, 0:16, :] = left_scr[pl.ds(start, 16), :].astype(BF16)
        msg_ref[o, 16:32, :] = right_scr[pl.ds(start, 16), :].astype(BF16)
        left = left_scr[pl.ds(start + 16, 8), :]
        right = pltpu.roll(right_scr[pl.ds(start + 16, 8), :], 2, 0)
        last = jnp.where(sub < 2, left, jnp.where(sub < 4, right, meta_scr[pl.ds(o, 1), :]))
        msg_ref[o, 32:40, :] = last.astype(BF16)
        return carry

    lax.fori_loop(0, owners, emit, 0, unroll=4)


def send_rows(vis_count, cells, owner, slot, vis, pos, owners):
    entries = vis.shape[0]
    vmem = pl.BlockSpec(memory_space=pltpu.VMEM)
    smem = pl.BlockSpec(memory_space=pltpu.SMEM)
    return pl.pallas_call(
        send_kernel,
        out_shape=(
            jax.ShapeDtypeStruct((owners, MSG, 128), BF16),
            jax.ShapeDtypeStruct((1, owners), I32),
        ),
        in_specs=[smem] + [pl.BlockSpec(memory_space=pltpu.HBM)] * 5,
        out_specs=(vmem, vmem),
        scratch_shapes=[
            pltpu.VMEM((entries + 24, 128), F32),
            pltpu.VMEM((entries + 24, 128), F32),
            pltpu.VMEM((owners, 128), F32),
            pltpu.SMEM((1, owners), I32),
            pltpu.SemaphoreType.DMA,
            pltpu.VMEM(cells.shape, I32),
            pltpu.VMEM(cells.shape, I32),
            pltpu.VMEM(cells.shape, I32),
            pltpu.VMEM(vis.shape, BF16),
            pltpu.VMEM(pos.shape, BF16),
            pltpu.SemaphoreType.DMA((5,)),
        ],
        compiler_params=pltpu.CompilerParams(vmem_limit_bytes=60 * 2**20),
        name="send_rows",
    )(vis_count, cells, owner, slot, vis, pos)


def owner_kernel(
    msg_ref, window_ref, gain1_ref, attn_in_ref, attn_out_ref, gain2_ref,
    mlp_in_ref, mlp_out_ref,
    back_ref,
    order_scr, tail_scr, q_scr, k_scr, v_scr, win_scr, att_scr, x_scr,
):
    owners = msg_ref.shape[0]
    rows = window_ref.shape[1]
    channels = attn_out_ref.shape[0]
    head_count = channels // HEAD_DIM
    full = 16 * owners
    ids = window_ref[...]
    windows = range(4)
    length = [jnp.sum(jnp.where(ids == w, 1.0, 0.0)).astype(I32) for w in windows]
    old = [sum(length[:w], jnp.int32(0)) for w in windows]
    new = []
    for w in windows:
        ahead = [
            jnp.where(length[v] >= length[w] if v < w else length[v] > length[w], length[v], 0)
            for v in windows
            if v != w
        ]
        new.append(sum(ahead, jnp.int32(0)))
    end = [new[w] + length[w] for w in windows]
    place_row = iota((1, rows), 1)
    order = sum([jnp.where(place_row >= end[w], 1, 0) for w in windows])
    order_scr[...] = order
    tail_scr[...] = msg_ref[:, 32:40, :].astype(F32).reshape(owners * 8, 128)

    def tail(j):
        return tail_scr[pl.ds(j, owners, stride=8), :]

    meta = tail(4).astype(BF16)
    place = iota((128, full), 0)
    inner = iota((128, full), 1) & 15
    spread = (
        jnp.where(place == inner, 32.0, 0.0) + jnp.where(place == inner + 32, 1.0, 0.0)
    ).astype(BF16)
    wide = dot(meta, spread)
    of_sender = (iota((owners, full), 1) >> 4) == iota((owners, full), 0)
    slot_full = jnp.sum(jnp.where(of_sender, wide, 0.0), axis=0, keepdims=True) - 32.0
    eye = eye_mask(owners)
    meta32 = meta.astype(F32)
    tail_cols = [meta32[:, j : j + 1] * 32.0 + meta32[:, j + 32 : j + 33] - 32.0 for j in (16, 17)]
    tail_slots = [jnp.sum(jnp.where(eye, c, 0.0), axis=0, keepdims=True) for c in tail_cols]
    slot_row = jnp.concatenate([slot_full] + tail_slots, axis=1).astype(I32)
    moved = slot_row + (new[0] - old[0])
    for w in windows[1:]:
        moved = jnp.where(slot_row >= old[w], slot_row + (new[w] - old[w]), moved)
    slot_row = jnp.where(slot_row >= 0, moved, -1)
    left = msg_ref[:, 0:16, :].reshape(full, 128)
    right = msg_ref[:, 16:32, :].reshape(full, 128)
    main = jnp.concatenate([left, right], axis=1)
    rest = jnp.concatenate(
        [
            jnp.concatenate([tail(0), tail(2)], axis=1),
            jnp.concatenate([tail(1), tail(3)], axis=1),
        ],
        axis=0,
    ).astype(BF16)
    step = 256
    step = 1024
    for b in range(rows // step):
        part = slice(b * step, (b + 1) * step)
        sel = match(iota((step, 1), 0) + b * step, slot_row)
        x = dot(sel[:, :full], main) + dot(sel[:, full:], rest)
        x_scr[part, :] = x
        normed = layer_norm(x, gain1_ref[...]).astype(BF16)
        projected = dot(normed, attn_in_ref[...]).astype(BF16)
        q_scr[part, :] = projected[:, :channels]
        k_scr[part, :] = projected[:, channels : 2 * channels]
        ones = jnp.ones((step, 128), BF16)
        v_scr[part, 0:128] = projected[:, 2 * channels : 2 * channels + 128]
        v_scr[part, 128:256] = ones
        v_scr[part, 256:384] = projected[:, 2 * channels + 128 :]
        v_scr[part, 384:512] = ones
    q_step = 256
    eye_q = eye_mask(128)
    for i in range(rows // 128):
        part = slice(i * 128, (i + 1) * 128)
        ids = order_scr[:, part].astype(F32)
        ids = jnp.sum(jnp.where(eye_q, ids, 0.0), axis=1, keepdims=True)
        win_scr[part, :] = jnp.broadcast_to(ids, (128, 128)).astype(I32)
    head_of_lane = iota((1, channels), 1) // HEAD_DIM
    lane_head = (iota((1, channels), 1) & 127) // HEAD_DIM
    head_mask = [one_hot(head_of_lane == h) for h in range(head_count)]
    scale = HEAD_DIM ** (-0.5) * 1.4426950408889634
    stack = 4
    half_heads = head_count // 2

    def attend(qi, key_count, key_start):
        q_rows = pl.ds(pl.multiple_of(qi * q_step, q_step), q_step)
        k_rows = pl.ds(key_start, key_count)
        q = q_scr[q_rows, :]
        keys = k_scr[k_rows, :]
        q_win = win_scr[q_rows, :]
        q_win = jnp.concatenate([q_win] * (key_count // 128), axis=1)
        bias = jnp.where(q_win == order_scr[:, k_rows], 0.0, -jnp.inf)
        bias = jnp.concatenate([bias] * stack, axis=0)
        groups = []
        for half in range(2):
            for g in range(half_heads // 4):
                groups.append((half, range(g * 4, (g + 1) * 4)))

        def scores(half, heads):
            queries = jnp.concatenate([q * head_mask[half * half_heads + h] for h in heads], axis=0)
            return dot_nt(queries, keys) + bias

        def weigh(s):
            top = jnp.max(s, axis=1, keepdims=True)
            return jnp.exp2(((s - top) * scale).astype(BF16))

        totals = [None, None]

        def mix(half, heads, e):
            o = dot(e, v_scr[k_rows, 256 * half : 256 * half + 256])
            total = totals[half]
            for i, h in enumerate(heads):
                block = o[i * q_step : (i + 1) * q_step]
                total = block if total is None else jnp.where(lane_head == h, block, total)
            totals[half] = total

        ahead = scores(*groups[0])
        held = None
        for i in range(len(groups)):
            s = ahead
            if i + 1 < len(groups):
                ahead = scores(*groups[i + 1])
            e = weigh(s)
            if held is not None:
                mix(*held)
            held = (*groups[i], e)
        mix(*held)

        for half in range(2):
            total = totals[half]
            att_scr[q_rows, 128 * half : 128 * half + 128] = (
                total[:, 0:128] * (1.0 / total[:, 128:256])
            ).astype(BF16)

    def q_block(qi, carry):
        first = qi * q_step
        low = jnp.int32(0)
        high = jnp.int32(rows)
        for w in windows:
            low = jnp.maximum(low, jnp.where(new[w] <= first, new[w], 0))
            high = jnp.minimum(high, jnp.where(end[w] >= first + q_step, end[w], rows))
        low = (low >> 7) << 7
        count = (high - low + 255) >> 8
        low = jnp.minimum(low, rows - 256 * count)
        for n in range(1, rows // 256 + 1):

            @pl.when(count == n)
            def _():
                attend(qi, 256 * n, pl.multiple_of(low, 128))

        return carry

    lax.fori_loop(0, rows // q_step, q_block, 0)
    step = 256
    for b in range(rows // step):
        part = slice(b * step, (b + 1) * step)
        x = x_scr[part, :] + dot(att_scr[part, :], attn_out_ref[...])
        normed = layer_norm(x, gain2_ref[...]).astype(BF16)
        hidden = gelu(dot(normed, mlp_in_ref[...])).astype(BF16)
        q_scr[part, :] = (x + dot(hidden, mlp_out_ref[...])).astype(BF16)
    slot_f = slot_row.astype(F32)
    eye128 = eye_mask(128)
    step = 512
    for b in range(full // step + 1):
        size = step if b < full // step else 2 * owners
        cols = []
        for i in range(size // 128):
            at = b * step + i * 128
            cols.append(
                jnp.sum(jnp.where(eye128, slot_f[:, at : at + 128], 0.0), axis=1, keepdims=True)
            )
        col = jnp.concatenate(cols, axis=0).astype(I32)
        pick = match(col, iota((1, rows), 1))
        out = dot(pick, q_scr[...])
        if b < full // step:
            o = b * step // 16
            n = step // 16
            out = out.astype(BF16)
            back_ref[o : o + n, 0:16, :] = out[:, 0:128].reshape(n, 16, 128)
            back_ref[o : o + n, 16:32, :] = out[:, 128:256].reshape(n, 16, 128)
        else:
            for j in range(2):
                tail_scr[pl.ds(j, owners, stride=8), :] = out[j * owners : (j + 1) * owners, 0:128]
                tail_scr[pl.ds(j + 2, owners, stride=8), :] = out[
                    j * owners : (j + 1) * owners, 128:256
                ]
            back_ref[:, 32:40, :] = tail_scr[...].astype(BF16).reshape(owners, 8, 128)


def owner_encode(msg, window, gain1, attn_in, attn_out, gain2, mlp_in, mlp_out):
    owners = msg.shape[0]
    rows = window.shape[1]
    channels = attn_out.shape[0]
    vmem = pl.BlockSpec(memory_space=pltpu.VMEM)
    return pl.pallas_call(
        owner_kernel,
        out_shape=jax.ShapeDtypeStruct((owners, MSG, 128), BF16),
        in_specs=[vmem] * 8,
        out_specs=vmem,
        scratch_shapes=[
            pltpu.VMEM((1, rows), I32),
            pltpu.VMEM((owners * 8, 128), F32),
            pltpu.VMEM((rows, channels), BF16),
            pltpu.VMEM((rows, channels), BF16),
            pltpu.VMEM((rows, 2 * channels), BF16),
            pltpu.VMEM((rows, 128), I32),
            pltpu.VMEM((rows, channels), BF16),
            pltpu.VMEM((rows, channels), F32),
        ],
        compiler_params=pltpu.CompilerParams(vmem_limit_bytes=40 * 2**20),
        name="owner_encode",
    )(msg, window, gain1, attn_in, attn_out, gain2, mlp_in, mlp_out)


def fill_cells(ids, cells, rows, token, pos, gain):
    hit = match(ids, cells)
    filled = dot(hit, rows)
    seen = sum([hit[:, i : i + 128] for i in range(0, hit.shape[1], 128)])
    seen = jnp.sum(seen.astype(F32), axis=1, keepdims=True)
    filled = jnp.where(seen > 0.5, filled, token)
    dec = (filled + pos.astype(F32)).astype(BF16)
    return dec, layer_norm(dec.astype(F32), gain).astype(BF16)


def edge_kernel(
    count_ref, starts_ref, back_ref, cells_ref, pos_ref, token_ref, gain_ref,
    rows_ref, dec_ref, first_ref, last_ref,
    left_scr, right_scr,
):
    owners = back_ref.shape[0]
    entries = cells_ref.shape[1]
    az, rad, height, channels = pos_ref.shape
    left_scr[...] = jnp.zeros(left_scr.shape, F32)
    right_scr[...] = jnp.zeros(right_scr.shape, F32)

    def take(o, carry):
        start = starts_ref[0, o]
        block = back_ref[o].astype(F32)
        left_scr[pl.ds(start, 16), :] = block[0:16]
        right_scr[pl.ds(start, 16), :] = block[16:32]
        left_scr[pl.ds(start + 16, 2), :] = block[32:34]
        right_scr[pl.ds(start + 16, 2), :] = block[34:36]
        return carry

    lax.fori_loop(0, owners, take, 0, unroll=8)
    rows = jnp.concatenate([left_scr[0:entries, :], right_scr[0:entries, :]], axis=1).astype(BF16)
    rows_ref[...] = rows
    cells = jnp.where(iota((1, entries), 1) < count_ref[0], cells_ref[...], -1)
    at = [(a, r) for r in (0, rad - 1) for a in range(az)]
    ids = jnp.concatenate(
        [iota((height, 1), 0) + (a * rad + r) * height for a, r in at], axis=0
    )
    pos = jnp.concatenate([pos_ref[a, r].astype(F32) for a, r in at], axis=0)
    dec, normed = fill_cells(ids, cells, rows, token_ref[...], pos, gain_ref[...])
    dec_ref[...] = dec.reshape(dec_ref.shape)
    first_ref[...] = normed[: az * height]
    last_ref[...] = normed[az * height :]


def place_edges(vis_count, starts, back, cells, pos, token, gain):
    az, rad, height, channels = pos.shape
    entries = cells.shape[1]
    vmem = pl.BlockSpec(memory_space=pltpu.VMEM)
    smem = pl.BlockSpec(memory_space=pltpu.SMEM)
    edges = jax.ShapeDtypeStruct((2, az * height, channels), BF16)
    edge = jax.ShapeDtypeStruct((az * height, channels), BF16)
    return pl.pallas_call(
        edge_kernel,
        out_shape=(jax.ShapeDtypeStruct((entries, channels), BF16), edges, edge, edge),
        in_specs=[smem, smem] + [vmem] * 5,
        out_specs=(vmem,) * 4,
        scratch_shapes=[pltpu.VMEM((entries + 24, 128), F32)] * 2,
        compiler_params=pltpu.CompilerParams(vmem_limit_bytes=24 * 2**20),
        cost_estimate=pl.CostEstimate(flops=6 * 10**8, bytes_accessed=4 * 10**6, transcendentals=0),
        name="place_edges",
    )(vis_count, starts, back, cells, pos, token, gain)


def mid_kernel(
    count_ref, rows_ref, cells_ref, pos_ref, token_ref, gain_ref,
    dec_ref, normed_ref,
):
    entries = cells_ref.shape[1]
    az, rad, height, channels = pos_ref.shape
    size = (rad - 2) * height
    rows = rows_ref[...]
    cells = jnp.where(iota((1, entries), 1) < count_ref[0], cells_ref[...], -1)
    for a in range(0, az, 2):
        ids = jnp.concatenate(
            [iota((size, 1), 0) + (i * rad + 1) * height for i in (a, a + 1)], axis=0
        )
        pos = jnp.concatenate(
            [pos_ref[i, 1 : rad - 1].reshape(size, channels) for i in (a, a + 1)], axis=0
        )
        dec, normed = fill_cells(ids, cells, rows, token_ref[...], pos, gain_ref[...])
        dec_ref[a : a + 2] = dec.reshape(2, size, channels)
        normed_ref[a : a + 2] = normed.reshape(2, size, channels)


def place_mid(vis_count, rows, cells, pos, token, gain):
    az, rad, height, channels = pos.shape
    vmem = pl.BlockSpec(memory_space=pltpu.VMEM)
    smem = pl.BlockSpec(memory_space=pltpu.SMEM)
    mid = jax.ShapeDtypeStruct((az, (rad - 2) * height, channels), BF16)
    return pl.pallas_call(
        mid_kernel,
        out_shape=(mid, mid),
        in_specs=[smem] + [vmem] * 5,
        out_specs=(vmem, vmem),
        compiler_params=pltpu.CompilerParams(vmem_limit_bytes=24 * 2**20),
        cost_estimate=pl.CostEstimate(flops=2 * 10**9, bytes_accessed=6 * 10**6, transcendentals=0),
        name="place_mid",
    )(vis_count, rows, cells, pos, token, gain)


def ring_ends():
    place = lax.axis_index("blk")
    return place == 0, place == lax.axis_size("blk") - 1


def rim_kernel(mid_ref, edge0_ref, edge1_ref, low_ref, high_ref, first_ref, last_ref):
    az, size, channels = mid_ref.shape
    height = low_ref.shape[0] // az
    inside, outside = ring_ends()
    for a, ref in ((0, first_ref), (az - 1, last_ref)):
        part = slice(a * height, (a + 1) * height)
        ref[0:height] = jnp.where(inside, 0.0, low_ref[part].astype(F32)).astype(BF16)
        ref[height : 2 * height] = edge0_ref[part]
        ref[2 * height : 2 * height + size] = mid_ref[a]
        ref[2 * height + size : 3 * height + size] = edge1_ref[part]
        ref[3 * height + size :] = jnp.where(outside, 0.0, high_ref[part].astype(F32)).astype(BF16)


def rim_rows(mid, edge0, edge1, low, high):
    az, size, channels = mid.shape
    vmem = pl.BlockSpec(memory_space=pltpu.VMEM)
    out = jax.ShapeDtypeStruct((size + 4 * (low.shape[0] // az), channels), BF16)
    return pl.pallas_call(
        rim_kernel,
        out_shape=(out, out),
        in_specs=[vmem] * 5,
        out_specs=(vmem, vmem),
        compiler_params=pltpu.CompilerParams(vmem_limit_bytes=8 * 2**20),
        name="rim_rows",
    )(mid, edge0, edge1, low, high)


def widen(scr, at, rows, height, drop=None):
    n, channels = rows.shape
    h = iota((n, 1), 0) % height
    values = rows.astype(F32)
    if drop is not None:
        values = jnp.where(drop, 0.0, values)
        rows = values.astype(BF16)
    scr[at : at + n, channels : 2 * channels] = rows
    below = jnp.where(h == 0, 0.0, pltpu.roll(values, 1, 0))
    scr[at : at + n, 0:channels] = below.astype(BF16)
    above = jnp.where(h == height - 1, 0.0, pltpu.roll(values, n - 1, 0))
    scr[at : at + n, 2 * channels :] = above.astype(BF16)


def conv_kernel(
    mid_ref, edge0_ref, edge1_ref, low_ref, high_ref, mid_dec_ref, edge_dec_ref, weight_ref, bias_ref,
    out_ref, partial_ref,
    wide_scr, done_scr, out_sems,
):
    az, size, channels = mid_ref.shape
    height = low_ref.shape[0] // az
    plane = size + 2 * height
    pitch = plane + 2 * height
    inside, outside = ring_ends()

    def spread(a):
        base = a * pitch
        part = slice(a * height, (a + 1) * height)
        widen(wide_scr, base, low_ref[part], height, inside)
        widen(wide_scr, base + height, edge0_ref[part], height)
        widen(wide_scr, base + 2 * height, mid_ref[a], height)
        widen(wide_scr, base + 2 * height + size, edge1_ref[part], height)
        widen(wide_scr, base + 3 * height + size, high_ref[part], height, outside)

    def taps(a):
        total = jnp.broadcast_to(bias_ref[...], (plane, channels))
        for da in range(3):
            if not 0 <= a + da - 1 < az:
                continue
            for dr in range(3):
                at = (a + da - 1) * pitch + dr * height
                total = total + dot(wide_scr[at : at + plane, :], weight_ref[da * 3 + dr])
        return total

    def finish(a, total):
        if a in (0, az - 1):
            partial_ref[a // (az - 1)] = total
            return
        part = slice(a * height, (a + 1) * height)
        dec = jnp.concatenate([edge_dec_ref[0, part], mid_dec_ref[a], edge_dec_ref[1, part]], axis=0)
        done_scr[a - 1] = (dec.astype(F32) + gelu(total)).astype(BF16)

    spread(0)
    spread(1)
    spread(2)
    stores = []
    held = taps(0)
    for a in range(1, az + 1):
        if a < az:
            total = taps(a)
        if a + 2 < az:
            spread(a + 2)
        finish(a - 1, held)
        held = total
        if 0 < a - 1 < az - 1:
            store = pltpu.make_async_copy(
                done_scr.at[a - 2], out_ref.at[pl.ds((a - 1) * plane, plane)], out_sems.at[a - 2]
            )
            stores.append(store)
            store.start()
    for store in stores:
        store.wait()


def conv_inner(mid, edge0, edge1, low, high, mid_dec, edge_dec, weight, bias):
    az, size, channels = mid.shape
    height = low.shape[0] // az
    plane = size + 2 * height
    vmem = pl.BlockSpec(memory_space=pltpu.VMEM)
    hbm = pl.BlockSpec(memory_space=pltpu.HBM)
    return pl.pallas_call(
        conv_kernel,
        out_shape=(
            jax.ShapeDtypeStruct((az * plane, channels), BF16),
            jax.ShapeDtypeStruct((2, plane, channels), F32),
        ),
        in_specs=[vmem] * 9,
        out_specs=(hbm, vmem),
        scratch_shapes=[
            pltpu.VMEM((az * (plane + 2 * height), 3 * channels), BF16),
            pltpu.VMEM((az - 2, plane, channels), BF16),
            pltpu.SemaphoreType.DMA((az - 2,)),
        ],
        compiler_params=pltpu.CompilerParams(vmem_limit_bytes=32 * 2**20),
        cost_estimate=pl.CostEstimate(flops=8 * 10**9, bytes_accessed=10**7, transcendentals=0),
        name="conv_inner",
    )(mid, edge0, edge1, low, high, mid_dec, edge_dec, weight, bias)


def conv_edge_kernel(
    low_ref, high_ref, partial_ref, mid_dec_ref, edge_dec_ref, weight_ref, given_ref,
    out_ref,
    wide_scr, done_scr, out_sems,
):
    az, size, channels = mid_dec_ref.shape
    plane = partial_ref.shape[1]
    height = (plane - size) // 2
    pitch = plane + 2 * height
    widen(wide_scr, 0, low_ref[...], height)
    widen(wide_scr, pitch, high_ref[...], height)
    stores = []
    for i in range(2):
        a = i * (az - 1)
        total = partial_ref[i]
        for dr in range(3):
            at = i * pitch + dr * height
            total = total + dot(wide_scr[at : at + plane, :], weight_ref[i * 6 + dr])
        part = slice(a * height, (a + 1) * height)
        dec = jnp.concatenate([edge_dec_ref[0, part], mid_dec_ref[a], edge_dec_ref[1, part]], axis=0)
        done_scr[i] = (dec.astype(F32) + gelu(total)).astype(BF16)
        store = pltpu.make_async_copy(
            done_scr.at[i], out_ref.at[pl.ds(a * plane, plane)], out_sems.at[i]
        )
        store.start()
        stores.append(store)
    for store in stores:
        store.wait()


def conv_edges(low, high, partial, mid_dec, edge_dec, weight, given):
    plane, channels = partial.shape[1:]
    vmem = pl.BlockSpec(memory_space=pltpu.VMEM)
    hbm = pl.BlockSpec(memory_space=pltpu.HBM)
    return pl.pallas_call(
        conv_edge_kernel,
        out_shape=jax.ShapeDtypeStruct(given.shape, BF16),
        in_specs=[vmem] * 6 + [hbm],
        out_specs=hbm,
        scratch_shapes=[
            pltpu.VMEM((2 * low.shape[0], 3 * channels), BF16),
            pltpu.VMEM((2, plane, channels), BF16),
            pltpu.SemaphoreType.DMA((2,)),
        ],
        input_output_aliases={6: 0},
        compiler_params=pltpu.CompilerParams(vmem_limit_bytes=16 * 2**20),
        name="conv_edges",
    )(low, high, partial, mid_dec, edge_dec, weight, given)


def exchange(values):
    return lax.all_to_all(values, ("sector", "blk"), split_axis=0, concat_axis=0, tiled=True)


def body(
    visible_feats, grid_pos, vis_cells, vis_count, owner, slot, window, enc_gain1, attn_in,
    attn_out, enc_gain2, mlp_in, mlp_out, mask_token, dec_gain, conv_weight, conv_bias,
):
    n_sector = lax.axis_size("sector")
    n_blk = lax.axis_size("blk")
    owners = n_sector * n_blk
    az, rad, height, channels = grid_pos.shape
    cell_total = az * rad * height
    pos = grid_pos.reshape(cell_total, channels)
    cells = vis_cells.reshape(1, -1)
    message, starts = send_rows(
        vis_count, cells, owner.reshape(1, -1), slot.reshape(1, -1), visible_feats, pos, owners
    )
    message = exchange(message)
    back = owner_encode(
        message, window, enc_gain1.reshape(1, -1), attn_in, attn_out,
        enc_gain2.reshape(1, -1), mlp_in, mlp_out,
    )
    back = exchange(back)
    token = mask_token.reshape(1, -1)
    gain = dec_gain.reshape(1, -1)
    rows, edge_dec, edge0, edge1 = place_edges(vis_count, starts, back, cells, grid_pos, token, gain)
    outward = [(i, (i + 1) % n_blk) for i in range(n_blk)]
    inward = [(t, s) for s, t in outward]
    rad_low = lax.ppermute(edge1, "blk", outward)
    rad_high = lax.ppermute(edge0, "blk", inward)
    mid_dec, mid = place_mid(vis_count, rows, cells, grid_pos, token, gain)
    first, last = rim_rows(mid, edge0, edge1, rad_low, rad_high)
    up = [(i, (i + 1) % n_sector) for i in range(n_sector)]
    down = [(t, s) for s, t in up]
    az_low = lax.ppermute(last, "sector", up)
    az_high = lax.ppermute(first, "sector", down)
    weight = conv_weight.reshape(9, 3 * channels, channels)
    inner, partial = conv_inner(
        mid, edge0, edge1, rad_low, rad_high, mid_dec, edge_dec, weight, conv_bias.reshape(1, -1)
    )
    decoded = conv_edges(az_low, az_high, partial, mid_dec, edge_dec, weight, inner)
    return decoded.reshape(az, rad, height, channels)


def solution(mesh):
    lists = P(("sector", "blk"))
    return jax.shard_map(
        body,
        mesh=mesh,
        in_specs=(
            P(("sector", "blk"), None),
            P("sector", "blk", None, None),
            lists,
            lists,
            lists,
            lists,
            P(("sector", "blk"), None),
        )
        + (P(),) * 10,
        out_specs=P("sector", "blk", None, None),
        check_vma=False,
    )
```

```python
import jax
import jax.numpy as jnp
from jax import lax
from jax.experimental import pallas as pl
from jax.experimental.pallas import tpu as pltpu
from jax.sharding import PartitionSpec as P

HEAD_DIM = 32
EPSILON = 1e-05
F32 = jnp.float32
BF16 = jnp.bfloat16
I16 = jnp.int16
I32 = jnp.int32
CAP = 18
MSG = 40


def iota(shape, dim):
    return lax.broadcasted_iota(I32, shape, dim)


def one_hot(mask):
    return jnp.where(mask, 1.0, 0.0).astype(BF16)


def match(col, row):
    n, k = col.shape[0], row.shape[1]
    col = jnp.broadcast_to(col, (n, 128)).astype(I16)
    row = jnp.broadcast_to(row, (16, k)).astype(I16)
    col = jnp.concatenate([col] * (k // 128), axis=1)
    row = jnp.concatenate([row] * (n // 16), axis=0)
    return jnp.where(col == row, jnp.ones((), BF16), jnp.zeros((), BF16))


def dot(a, b):
    return jnp.dot(a, b, preferred_element_type=F32)


def dot_nt(a, b):
    return lax.dot_general(a, b, (((1,), (1,)), ((), ())), preferred_element_type=F32)


def eye_mask(n):
    return iota((n, n), 0) == iota((n, n), 1)


def layer_norm(values, gain_vec):
    center = values - jnp.mean(values, axis=-1, keepdims=True)
    spread = jnp.mean(center * center, axis=-1, keepdims=True)
    return center * lax.rsqrt(spread + EPSILON) * gain_vec


def gelu(x):
    return 0.5 * x * (1.0 + jnp.tanh(0.7978845608028654 * (x + 0.044715 * (x * x * x))))


def send_kernel(
    count_ref, cells_ref, owner_ref, slot_ref, vis_ref, pos_ref,
    msg_ref, starts_ref,
    left_scr, right_scr, meta_scr, starts_smem, sem,
    cells_in, owner_in, slot_in, vis_in, pos_in, in_sems,
):
    entries = cells_ref.shape[1]
    owners = msg_ref.shape[0]
    cell_total = pos_ref.shape[0]
    loads = [
        pltpu.make_async_copy(src, dst, in_sems.at[i])
        for i, (src, dst) in enumerate(
            [
                (owner_ref, owner_in),
                (cells_ref, cells_in),
                (slot_ref, slot_in),
                (pos_ref, pos_in),
                (vis_ref, vis_in),
            ]
        )
    ]
    for load in loads:
        load.start()
    for load in loads[:3]:
        load.wait()
    entry = iota((1, entries), 1)
    live = entry < count_ref[0]
    owner = jnp.where(live, owner_in[...], owners)
    owner_id = iota((owners, entries), 0)
    start_col = jnp.sum(jnp.where(owner < owner_id, 1.0, 0.0), axis=1, keepdims=True)
    start_row = jnp.sum(jnp.where(eye_mask(owners), start_col, 0.0), axis=0, keepdims=True)
    starts_ref[...] = start_row.astype(I32)
    copy = pltpu.make_async_copy(starts_ref, starts_smem, sem)
    copy.start()
    belongs = owner == owner_id
    first = jnp.sum(jnp.where(belongs, start_col, 0.0), axis=0, keepdims=True)
    within = jnp.where(live, entry - first.astype(I32), 64)
    cells = cells_in[...]
    slots = slot_in[...]
    parts = jnp.concatenate(
        [cells >> 6, cells & 63, slots >> 5, slots & 31, within, within, within, within], axis=0
    ).astype(F32).astype(BF16)
    eye = one_hot(eye_mask(128))
    lane = iota((128, 128), 1)
    cell_cols = []
    meta_parts = []
    for b in range(entries // 128):
        turned = dot_nt(eye, parts[:, b * 128 : (b + 1) * 128])
        cell_cols.append((turned[:, 0:1] * 64.0 + turned[:, 1:2]).astype(I32))
        place = turned[:, 4:5].astype(I32)
        meta_parts.append(
            jnp.where(
                lane == place,
                turned[:, 2:3] + 1.0,
                jnp.where(lane == place + 32, turned[:, 3:4], 0.0),
            ).astype(BF16)
        )
    meta_scr[...] = dot(one_hot(belongs), jnp.concatenate(meta_parts, axis=0))
    for load in loads[3:]:
        load.wait()
    step = 512
    for b in range(entries // step):
        col = jnp.concatenate(cell_cols[b * step // 128 : (b + 1) * step // 128], axis=0)
        pick = match(col, iota((1, cell_total), 1))
        rows = vis_in[b * step : (b + 1) * step, :].astype(F32) + dot(pick, pos_in[...])
        rows = rows.astype(BF16).astype(F32)
        left_scr[b * step : (b + 1) * step, :] = rows[:, 0:128]
        right_scr[b * step : (b + 1) * step, :] = rows[:, 128:256]
    left_scr[entries:, :] = jnp.zeros((left_scr.shape[0] - entries, 128), F32)
    right_scr[entries:, :] = jnp.zeros((right_scr.shape[0] - entries, 128), F32)
    copy.wait()
    sub = iota((8, 128), 0)

    def emit(o, carry):
        start = starts_smem[0, o]
        msg_ref[o, 0:16, :] = left_scr[pl.ds(start, 16), :].astype(BF16)
        msg_ref[o, 16:32, :] = right_scr[pl.ds(start, 16), :].astype(BF16)
        left = left_scr[pl.ds(start + 16, 8), :]
        right = pltpu.roll(right_scr[pl.ds(start + 16, 8), :], 2, 0)
        last = jnp.where(sub < 2, left, jnp.where(sub < 4, right, meta_scr[pl.ds(o, 1), :]))
        msg_ref[o, 32:40, :] = last.astype(BF16)
        return carry

    lax.fori_loop(0, owners, emit, 0, unroll=4)


def send_rows(vis_count, cells, owner, slot, vis, pos, owners):
    entries = vis.shape[0]
    vmem = pl.BlockSpec(memory_space=pltpu.VMEM)
    smem = pl.BlockSpec(memory_space=pltpu.SMEM)
    return pl.pallas_call(
        send_kernel,
        out_shape=(
            jax.ShapeDtypeStruct((owners, MSG, 128), BF16),
            jax.ShapeDtypeStruct((1, owners), I32),
        ),
        in_specs=[smem] + [pl.BlockSpec(memory_space=pltpu.HBM)] * 5,
        out_specs=(vmem, vmem),
        scratch_shapes=[
            pltpu.VMEM((entries + 24, 128), F32),
            pltpu.VMEM((entries + 24, 128), F32),
            pltpu.VMEM((owners, 128), F32),
            pltpu.SMEM((1, owners), I32),
            pltpu.SemaphoreType.DMA,
            pltpu.VMEM(cells.shape, I32),
            pltpu.VMEM(cells.shape, I32),
            pltpu.VMEM(cells.shape, I32),
            pltpu.VMEM(vis.shape, BF16),
            pltpu.VMEM(pos.shape, BF16),
            pltpu.SemaphoreType.DMA((5,)),
        ],
        compiler_params=pltpu.CompilerParams(vmem_limit_bytes=60 * 2**20),
        name="send_rows",
    )(vis_count, cells, owner, slot, vis, pos)


def owner_kernel(
    msg_ref, window_ref, gain1_ref, attn_in_ref, attn_out_ref, gain2_ref,
    mlp_in_ref, mlp_out_ref,
    back_ref,
    order_scr, tail_scr, q_scr, k_scr, v_scr, win_scr, att_scr, x_scr,
):
    owners = msg_ref.shape[0]
    rows = window_ref.shape[1]
    channels = attn_out_ref.shape[0]
    head_count = channels // HEAD_DIM
    full = 16 * owners
    ids = window_ref[...]
    windows = range(4)
    length = [jnp.sum(jnp.where(ids == w, 1.0, 0.0)).astype(I32) for w in windows]
    old = [sum(length[:w], jnp.int32(0)) for w in windows]
    new = []
    for w in windows:
        ahead = [
            jnp.where(length[v] >= length[w] if v < w else length[v] > length[w], length[v], 0)
            for v in windows
            if v != w
        ]
        new.append(sum(ahead, jnp.int32(0)))
    end = [new[w] + length[w] for w in windows]
    place_row = iota((1, rows), 1)
    order = sum([jnp.where(place_row >= end[w], 1, 0) for w in windows])
    order_scr[...] = order
    tail_scr[...] = msg_ref[:, 32:40, :].astype(F32).reshape(owners * 8, 128)

    def tail(j):
        return tail_scr[pl.ds(j, owners, stride=8), :]

    meta = tail(4).astype(BF16)
    place = iota((128, full), 0)
    inner = iota((128, full), 1) & 15
    spread = (
        jnp.where(place == inner, 32.0, 0.0) + jnp.where(place == inner + 32, 1.0, 0.0)
    ).astype(BF16)
    wide = dot(meta, spread)
    of_sender = (iota((owners, full), 1) >> 4) == iota((owners, full), 0)
    slot_full = jnp.sum(jnp.where(of_sender, wide, 0.0), axis=0, keepdims=True) - 32.0
    eye = eye_mask(owners)
    meta32 = meta.astype(F32)
    tail_cols = [meta32[:, j : j + 1] * 32.0 + meta32[:, j + 32 : j + 33] - 32.0 for j in (16, 17)]
    tail_slots = [jnp.sum(jnp.where(eye, c, 0.0), axis=0, keepdims=True) for c in tail_cols]
    slot_row = jnp.concatenate([slot_full] + tail_slots, axis=1).astype(I32)
    moved = slot_row + (new[0] - old[0])
    for w in windows[1:]:
        moved = jnp.where(slot_row >= old[w], slot_row + (new[w] - old[w]), moved)
    slot_row = jnp.where(slot_row >= 0, moved, -1)
    left = msg_ref[:, 0:16, :].reshape(full, 128)
    right = msg_ref[:, 16:32, :].reshape(full, 128)
    main = jnp.concatenate([left, right], axis=1)
    rest = jnp.concatenate(
        [
            jnp.concatenate([tail(0), tail(2)], axis=1),
            jnp.concatenate([tail(1), tail(3)], axis=1),
        ],
        axis=0,
    ).astype(BF16)
    step = 256
    step = 1024
    for b in range(rows // step):
        part = slice(b * step, (b + 1) * step)
        sel = match(iota((step, 1), 0) + b * step, slot_row)
        x = dot(sel[:, :full], main) + dot(sel[:, full:], rest)
        x_scr[part, :] = x
        normed = layer_norm(x, gain1_ref[...]).astype(BF16)
        projected = dot(normed, attn_in_ref[...]).astype(BF16)
        q_scr[part, :] = projected[:, :channels]
        k_scr[part, :] = projected[:, channels : 2 * channels]
        ones = jnp.ones((step, 128), BF16)
        v_scr[part, 0:128] = projected[:, 2 * channels : 2 * channels + 128]
        v_scr[part, 128:256] = ones
        v_scr[part, 256:384] = projected[:, 2 * channels + 128 :]
        v_scr[part, 384:512] = ones
    q_step = 256
    eye_q = eye_mask(128)
    for i in range(rows // 128):
        part = slice(i * 128, (i + 1) * 128)
        ids = order_scr[:, part].astype(F32)
        ids = jnp.sum(jnp.where(eye_q, ids, 0.0), axis=1, keepdims=True)
        win_scr[part, :] = jnp.broadcast_to(ids, (128, 128)).astype(I32)
    head_of_lane = iota((1, channels), 1) // HEAD_DIM
    lane_head = (iota((1, channels), 1) & 127) // HEAD_DIM
    head_mask = [one_hot(head_of_lane == h) for h in range(head_count)]
    scale = HEAD_DIM ** (-0.5) * 1.4426950408889634
    stack = 4
    half_heads = head_count // 2

    def attend(qi, key_count, key_start):
        q_rows = pl.ds(pl.multiple_of(qi * q_step, q_step), q_step)
        k_rows = pl.ds(key_start, key_count)
        q = q_scr[q_rows, :]
        keys = k_scr[k_rows, :]
        q_win = win_scr[q_rows, :]
        q_win = jnp.concatenate([q_win] * (key_count // 128), axis=1)
        bias = jnp.where(q_win == order_scr[:, k_rows], 0.0, -jnp.inf)
        bias = jnp.concatenate([bias] * stack, axis=0)
        groups = []
        for half in range(2):
            for g in range(half_heads // 4):
                groups.append((half, range(g * 4, (g + 1) * 4)))

        def scores(half, heads):
            queries = jnp.concatenate([q * head_mask[half * half_heads + h] for h in heads], axis=0)
            return dot_nt(queries, keys) + bias

        def weigh(s):
            top = jnp.max(s, axis=1, keepdims=True)
            return jnp.exp2(((s - top) * scale).astype(BF16))

        totals = [None, None]

        def mix(half, heads, e):
            o = dot(e, v_scr[k_rows, 256 * half : 256 * half + 256])
            total = totals[half]
            for i, h in enumerate(heads):
                block = o[i * q_step : (i + 1) * q_step]
                total = block if total is None else jnp.where(lane_head == h, block, total)
            totals[half] = total

        ahead = scores(*groups[0])
        held = None
        for i in range(len(groups)):
            s = ahead
            if i + 1 < len(groups):
                ahead = scores(*groups[i + 1])
            e = weigh(s)
            if held is not None:
                mix(*held)
            held = (*groups[i], e)
        mix(*held)

        for half in range(2):
            total = totals[half]
            att_scr[q_rows, 128 * half : 128 * half + 128] = (
                total[:, 0:128] * (1.0 / total[:, 128:256])
            ).astype(BF16)

    def q_block(qi, carry):
        first = qi * q_step
        low = jnp.int32(0)
        high = jnp.int32(rows)
        for w in windows:
            low = jnp.maximum(low, jnp.where(new[w] <= first, new[w], 0))
            high = jnp.minimum(high, jnp.where(end[w] >= first + q_step, end[w], rows))
        low = (low >> 7) << 7
        count = (high - low + 255) >> 8
        low = jnp.minimum(low, rows - 256 * count)
        for n in range(1, rows // 256 + 1):

            @pl.when(count == n)
            def _():
                attend(qi, 256 * n, pl.multiple_of(low, 128))

        return carry

    lax.fori_loop(0, rows // q_step, q_block, 0)
    step = 256
    for b in range(rows // step):
        part = slice(b * step, (b + 1) * step)
        x = x_scr[part, :] + dot(att_scr[part, :], attn_out_ref[...])
        normed = layer_norm(x, gain2_ref[...]).astype(BF16)
        hidden = gelu(dot(normed, mlp_in_ref[...])).astype(BF16)
        q_scr[part, :] = (x + dot(hidden, mlp_out_ref[...])).astype(BF16)
    slot_f = slot_row.astype(F32)
    eye128 = eye_mask(128)
    step = 512
    for b in range(full // step + 1):
        size = step if b < full // step else 2 * owners
        cols = []
        for i in range(size // 128):
            at = b * step + i * 128
            cols.append(
                jnp.sum(jnp.where(eye128, slot_f[:, at : at + 128], 0.0), axis=1, keepdims=True)
            )
        col = jnp.concatenate(cols, axis=0).astype(I32)
        pick = match(col, iota((1, rows), 1))
        out = dot(pick, q_scr[...])
        if b < full // step:
            o = b * step // 16
            n = step // 16
            out = out.astype(BF16)
            back_ref[o : o + n, 0:16, :] = out[:, 0:128].reshape(n, 16, 128)
            back_ref[o : o + n, 16:32, :] = out[:, 128:256].reshape(n, 16, 128)
        else:
            for j in range(2):
                tail_scr[pl.ds(j, owners, stride=8), :] = out[j * owners : (j + 1) * owners, 0:128]
                tail_scr[pl.ds(j + 2, owners, stride=8), :] = out[
                    j * owners : (j + 1) * owners, 128:256
                ]
            back_ref[:, 32:40, :] = tail_scr[...].astype(BF16).reshape(owners, 8, 128)


def owner_encode(msg, window, gain1, attn_in, attn_out, gain2, mlp_in, mlp_out):
    owners = msg.shape[0]
    rows = window.shape[1]
    channels = attn_out.shape[0]
    vmem = pl.BlockSpec(memory_space=pltpu.VMEM)
    return pl.pallas_call(
        owner_kernel,
        out_shape=jax.ShapeDtypeStruct((owners, MSG, 128), BF16),
        in_specs=[vmem] * 8,
        out_specs=vmem,
        scratch_shapes=[
            pltpu.VMEM((1, rows), I32),
            pltpu.VMEM((owners * 8, 128), F32),
            pltpu.VMEM((rows, channels), BF16),
            pltpu.VMEM((rows, channels), BF16),
            pltpu.VMEM((rows, 2 * channels), BF16),
            pltpu.VMEM((rows, 128), I32),
            pltpu.VMEM((rows, channels), BF16),
            pltpu.VMEM((rows, channels), F32),
        ],
        compiler_params=pltpu.CompilerParams(vmem_limit_bytes=40 * 2**20),
        name="owner_encode",
    )(msg, window, gain1, attn_in, attn_out, gain2, mlp_in, mlp_out)


def fill_cells(ids, cells, rows, token, pos, gain):
    hit = match(ids, cells)
    filled = dot(hit, rows)
    seen = sum([hit[:, i : i + 128] for i in range(0, hit.shape[1], 128)])
    seen = jnp.sum(seen.astype(F32), axis=1, keepdims=True)
    filled = jnp.where(seen > 0.5, filled, token)
    dec = (filled + pos.astype(F32)).astype(BF16)
    return dec, layer_norm(dec.astype(F32), gain).astype(BF16)


def edge_kernel(
    count_ref, starts_ref, back_ref, cells_ref, pos_ref, token_ref, gain_ref,
    rows_ref, dec_ref, first_ref, last_ref,
    left_scr, right_scr,
):
    owners = back_ref.shape[0]
    entries = cells_ref.shape[1]
    az, rad, height, channels = pos_ref.shape
    left_scr[...] = jnp.zeros(left_scr.shape, F32)
    right_scr[...] = jnp.zeros(right_scr.shape, F32)

    def take(o, carry):
        start = starts_ref[0, o]
        block = back_ref[o].astype(F32)
        left_scr[pl.ds(start, 16), :] = block[0:16]
        right_scr[pl.ds(start, 16), :] = block[16:32]
        left_scr[pl.ds(start + 16, 2), :] = block[32:34]
        right_scr[pl.ds(start + 16, 2), :] = block[34:36]
        return carry

    lax.fori_loop(0, owners, take, 0, unroll=8)
    rows = jnp.concatenate([left_scr[0:entries, :], right_scr[0:entries, :]], axis=1).astype(BF16)
    rows_ref[...] = rows
    cells = jnp.where(iota((1, entries), 1) < count_ref[0], cells_ref[...], -1)
    at = [(a, r) for r in (0, rad - 1) for a in range(az)]
    ids = jnp.concatenate(
        [iota((height, 1), 0) + (a * rad + r) * height for a, r in at], axis=0
    )
    pos = jnp.concatenate([pos_ref[a, r].astype(F32) for a, r in at], axis=0)
    dec, normed = fill_cells(ids, cells, rows, token_ref[...], pos, gain_ref[...])
    dec_ref[...] = dec.reshape(dec_ref.shape)
    first_ref[...] = normed[: az * height]
    last_ref[...] = normed[az * height :]


def place_edges(vis_count, starts, back, cells, pos, token, gain):
    az, rad, height, channels = pos.shape
    entries = cells.shape[1]
    vmem = pl.BlockSpec(memory_space=pltpu.VMEM)
    smem = pl.BlockSpec(memory_space=pltpu.SMEM)
    edges = jax.ShapeDtypeStruct((2, az * height, channels), BF16)
    edge = jax.ShapeDtypeStruct((az * height, channels), BF16)
    return pl.pallas_call(
        edge_kernel,
        out_shape=(jax.ShapeDtypeStruct((entries, channels), BF16), edges, edge, edge),
        in_specs=[smem, smem] + [vmem] * 5,
        out_specs=(vmem,) * 4,
        scratch_shapes=[pltpu.VMEM((entries + 24, 128), F32)] * 2,
        compiler_params=pltpu.CompilerParams(vmem_limit_bytes=24 * 2**20),
        cost_estimate=pl.CostEstimate(flops=6 * 10**8, bytes_accessed=4 * 10**6, transcendentals=0),
        name="place_edges",
    )(vis_count, starts, back, cells, pos, token, gain)


def mid_kernel(
    count_ref, rows_ref, cells_ref, pos_ref, token_ref, gain_ref,
    dec_ref, normed_ref,
):
    entries = cells_ref.shape[1]
    az, rad, height, channels = pos_ref.shape
    size = (rad - 2) * height
    rows = rows_ref[...]
    cells = jnp.where(iota((1, entries), 1) < count_ref[0], cells_ref[...], -1)
    for a in range(0, az, 2):
        ids = jnp.concatenate(
            [iota((size, 1), 0) + (i * rad + 1) * height for i in (a, a + 1)], axis=0
        )
        pos = jnp.concatenate(
            [pos_ref[i, 1 : rad - 1].reshape(size, channels) for i in (a, a + 1)], axis=0
        )
        dec, normed = fill_cells(ids, cells, rows, token_ref[...], pos, gain_ref[...])
        dec_ref[a : a + 2] = dec.reshape(2, size, channels)
        normed_ref[a : a + 2] = normed.reshape(2, size, channels)


def place_mid(vis_count, rows, cells, pos, token, gain):
    az, rad, height, channels = pos.shape
    vmem = pl.BlockSpec(memory_space=pltpu.VMEM)
    smem = pl.BlockSpec(memory_space=pltpu.SMEM)
    mid = jax.ShapeDtypeStruct((az, (rad - 2) * height, channels), BF16)
    return pl.pallas_call(
        mid_kernel,
        out_shape=(mid, mid),
        in_specs=[smem] + [vmem] * 5,
        out_specs=(vmem, vmem),
        compiler_params=pltpu.CompilerParams(vmem_limit_bytes=24 * 2**20),
        cost_estimate=pl.CostEstimate(flops=2 * 10**9, bytes_accessed=6 * 10**6, transcendentals=0),
        name="place_mid",
    )(vis_count, rows, cells, pos, token, gain)


def ring_ends():
    place = lax.axis_index("blk")
    return place == 0, place == lax.axis_size("blk") - 1


def even_sector():
    return lax.bitwise_and(lax.axis_index("sector"), 1) == 0


def rim_kernel(mid_ref, edge0_ref, edge1_ref, low_ref, high_ref, near_ref, far_ref):
    az, size, channels = mid_ref.shape
    height = low_ref.shape[0] // az
    inside, outside = ring_ends()

    def fill(ref, a):
        part = slice(a * height, (a + 1) * height)
        ref[0:height] = jnp.where(inside, 0.0, low_ref[part].astype(F32)).astype(BF16)
        ref[height : 2 * height] = edge0_ref[part]
        ref[2 * height : 2 * height + size] = mid_ref[a]
        ref[2 * height + size : 3 * height + size] = edge1_ref[part]
        ref[3 * height + size :] = jnp.where(outside, 0.0, high_ref[part].astype(F32)).astype(BF16)

    even = even_sector()

    @pl.when(even)
    def _():
        fill(near_ref, az - 1)
        fill(far_ref, 0)

    @pl.when(jnp.logical_not(even))
    def _():
        fill(near_ref, 0)
        fill(far_ref, az - 1)


def rim_rows(mid, edge0, edge1, low, high):
    az, size, channels = mid.shape
    vmem = pl.BlockSpec(memory_space=pltpu.VMEM)
    out = jax.ShapeDtypeStruct((size + 4 * (low.shape[0] // az), channels), BF16)
    return pl.pallas_call(
        rim_kernel,
        out_shape=(out, out),
        in_specs=[vmem] * 5,
        out_specs=(vmem, vmem),
        compiler_params=pltpu.CompilerParams(vmem_limit_bytes=8 * 2**20),
        name="rim_rows",
    )(mid, edge0, edge1, low, high)


def widen(scr, at, rows, height, drop=None):
    n, channels = rows.shape
    h = iota((n, 1), 0) % height
    values = rows.astype(F32)
    if drop is not None:
        values = jnp.where(drop, 0.0, values)
        rows = values.astype(BF16)
    scr[at : at + n, channels : 2 * channels] = rows
    below = jnp.where(h == 0, 0.0, pltpu.roll(values, 1, 0))
    scr[at : at + n, 0:channels] = below.astype(BF16)
    above = jnp.where(h == height - 1, 0.0, pltpu.roll(values, n - 1, 0))
    scr[at : at + n, 2 * channels :] = above.astype(BF16)


def conv_kernel(
    mid_ref, edge0_ref, edge1_ref, low_ref, high_ref, mid_dec_ref, edge_dec_ref, weight_ref, bias_ref,
    out_ref, partial_ref,
    wide_scr, done_scr, out_sems,
):
    az, size, channels = mid_ref.shape
    height = low_ref.shape[0] // az
    plane = size + 2 * height
    pitch = plane + 2 * height
    inside, outside = ring_ends()

    def spread(a):
        base = a * pitch
        part = slice(a * height, (a + 1) * height)
        widen(wide_scr, base, low_ref[part], height, inside)
        widen(wide_scr, base + height, edge0_ref[part], height)
        widen(wide_scr, base + 2 * height, mid_ref[a], height)
        widen(wide_scr, base + 2 * height + size, edge1_ref[part], height)
        widen(wide_scr, base + 3 * height + size, high_ref[part], height, outside)

    def taps(a):
        total = jnp.broadcast_to(bias_ref[...], (plane, channels))
        for da in range(3):
            if not 0 <= a + da - 1 < az:
                continue
            for dr in range(3):
                at = (a + da - 1) * pitch + dr * height
                total = total + dot(wide_scr[at : at + plane, :], weight_ref[da * 3 + dr])
        return total

    def finish(a, total):
        if a in (0, az - 1):
            partial_ref[a // (az - 1)] = total
            return
        part = slice(a * height, (a + 1) * height)
        dec = jnp.concatenate([edge_dec_ref[0, part], mid_dec_ref[a], edge_dec_ref[1, part]], axis=0)
        done_scr[a - 1] = (dec.astype(F32) + gelu(total)).astype(BF16)

    spread(0)
    spread(1)
    spread(2)
    stores = []
    held = taps(0)
    for a in range(1, az + 1):
        if a < az:
            total = taps(a)
        if a + 2 < az:
            spread(a + 2)
        finish(a - 1, held)
        held = total
        if 0 < a - 1 < az - 1:
            store = pltpu.make_async_copy(
                done_scr.at[a - 2], out_ref.at[pl.ds((a - 1) * plane, plane)], out_sems.at[a - 2]
            )
            stores.append(store)
            store.start()
    for store in stores:
        store.wait()


def conv_inner(mid, edge0, edge1, low, high, mid_dec, edge_dec, weight, bias):
    az, size, channels = mid.shape
    height = low.shape[0] // az
    plane = size + 2 * height
    vmem = pl.BlockSpec(memory_space=pltpu.VMEM)
    hbm = pl.BlockSpec(memory_space=pltpu.HBM)
    return pl.pallas_call(
        conv_kernel,
        out_shape=(
            jax.ShapeDtypeStruct((az * plane, channels), BF16),
            jax.ShapeDtypeStruct((2, plane, channels), F32),
        ),
        in_specs=[vmem] * 9,
        out_specs=(hbm, vmem),
        scratch_shapes=[
            pltpu.VMEM((az * (plane + 2 * height), 3 * channels), BF16),
            pltpu.VMEM((az - 2, plane, channels), BF16),
            pltpu.SemaphoreType.DMA((az - 2,)),
        ],
        compiler_params=pltpu.CompilerParams(vmem_limit_bytes=32 * 2**20),
        cost_estimate=pl.CostEstimate(flops=8 * 10**9, bytes_accessed=10**7, transcendentals=0),
        name="conv_inner",
    )(mid, edge0, edge1, low, high, mid_dec, edge_dec, weight, bias)


def conv_edge_kernel(
    near_ref, far_ref, partial_ref, mid_dec_ref, edge_dec_ref, weight_ref, given_ref,
    out_ref,
    wide_scr, done_scr, out_sems,
):
    az, size, channels = mid_dec_ref.shape
    plane = partial_ref.shape[1]
    height = (plane - size) // 2
    pitch = plane + 2 * height
    even = even_sector()

    @pl.when(even)
    def _():
        widen(wide_scr, 0, far_ref[...], height)
        widen(wide_scr, pitch, near_ref[...], height)

    @pl.when(jnp.logical_not(even))
    def _():
        widen(wide_scr, 0, near_ref[...], height)
        widen(wide_scr, pitch, far_ref[...], height)

    stores = []
    for i in range(2):
        a = i * (az - 1)
        total = partial_ref[i]
        for dr in range(3):
            at = i * pitch + dr * height
            total = total + dot(wide_scr[at : at + plane, :], weight_ref[i * 6 + dr])
        part = slice(a * height, (a + 1) * height)
        dec = jnp.concatenate([edge_dec_ref[0, part], mid_dec_ref[a], edge_dec_ref[1, part]], axis=0)
        done_scr[i] = (dec.astype(F32) + gelu(total)).astype(BF16)
        store = pltpu.make_async_copy(
            done_scr.at[i], out_ref.at[pl.ds(a * plane, plane)], out_sems.at[i]
        )
        store.start()
        stores.append(store)
    for store in stores:
        store.wait()


def conv_edges(near, far, partial, mid_dec, edge_dec, weight, given):
    plane, channels = partial.shape[1:]
    vmem = pl.BlockSpec(memory_space=pltpu.VMEM)
    hbm = pl.BlockSpec(memory_space=pltpu.HBM)
    return pl.pallas_call(
        conv_edge_kernel,
        out_shape=jax.ShapeDtypeStruct(given.shape, BF16),
        in_specs=[vmem] * 6 + [hbm],
        out_specs=hbm,
        scratch_shapes=[
            pltpu.VMEM((2 * near.shape[0], 3 * channels), BF16),
            pltpu.VMEM((2, plane, channels), BF16),
            pltpu.SemaphoreType.DMA((2,)),
        ],
        input_output_aliases={6: 0},
        compiler_params=pltpu.CompilerParams(vmem_limit_bytes=16 * 2**20),
        name="conv_edges",
    )(near, far, partial, mid_dec, edge_dec, weight, given)


def exchange(values):
    return lax.all_to_all(values, ("sector", "blk"), split_axis=0, concat_axis=0, tiled=True)


def body(
    visible_feats, grid_pos, vis_cells, vis_count, owner, slot, window, enc_gain1, attn_in,
    attn_out, enc_gain2, mlp_in, mlp_out, mask_token, dec_gain, conv_weight, conv_bias,
):
    n_sector = lax.axis_size("sector")
    n_blk = lax.axis_size("blk")
    owners = n_sector * n_blk
    az, rad, height, channels = grid_pos.shape
    cell_total = az * rad * height
    pos = grid_pos.reshape(cell_total, channels)
    cells = vis_cells.reshape(1, -1)
    message, starts = send_rows(
        vis_count, cells, owner.reshape(1, -1), slot.reshape(1, -1), visible_feats, pos, owners
    )
    message = exchange(message)
    back = owner_encode(
        message, window, enc_gain1.reshape(1, -1), attn_in, attn_out,
        enc_gain2.reshape(1, -1), mlp_in, mlp_out,
    )
    back = exchange(back)
    token = mask_token.reshape(1, -1)
    gain = dec_gain.reshape(1, -1)
    rows, edge_dec, edge0, edge1 = place_edges(vis_count, starts, back, cells, grid_pos, token, gain)
    outward = [(i, (i + 1) % n_blk) for i in range(n_blk)]
    inward = [(t, s) for s, t in outward]
    rad_low = lax.ppermute(edge1, "blk", outward)
    rad_high = lax.ppermute(edge0, "blk", inward)
    mid_dec, mid = place_mid(vis_count, rows, cells, grid_pos, token, gain)
    near, far = rim_rows(mid, edge0, edge1, rad_low, rad_high)
    pairs = [(i, i + 1) for i in range(0, n_sector, 2)]
    across = [(i, (i + 1) % n_sector) for i in range(1, n_sector, 2)]
    near = lax.ppermute(near, "sector", pairs + [(t, s) for s, t in pairs])
    far = lax.ppermute(far, "sector", across + [(t, s) for s, t in across])
    weight = conv_weight.reshape(9, 3 * channels, channels)
    inner, partial = conv_inner(
        mid, edge0, edge1, rad_low, rad_high, mid_dec, edge_dec, weight, conv_bias.reshape(1, -1)
    )
    decoded = conv_edges(near, far, partial, mid_dec, edge_dec, weight, inner)
    return decoded.reshape(az, rad, height, channels)


def solution(mesh):
    lists = P(("sector", "blk"))
    return jax.shard_map(
        body,
        mesh=mesh,
        in_specs=(
            P(("sector", "blk"), None),
            P("sector", "blk", None, None),
            lists,
            lists,
            lists,
            lists,
            P(("sector", "blk"), None),
        )
        + (P(),) * 10,
        out_specs=P("sector", "blk", None, None),
        check_vma=False,
    )
```

```python
import jax
import jax.numpy as jnp
from jax import lax
from jax.experimental import pallas as pl
from jax.experimental.pallas import tpu as pltpu
from jax.sharding import PartitionSpec as P

HEAD_DIM = 32
EPSILON = 1e-05
F32 = jnp.float32
BF16 = jnp.bfloat16
I16 = jnp.int16
I32 = jnp.int32
CAP = 18
PLANES_FIRST = 2
MSG = 40


def iota(shape, dim):
    return lax.broadcasted_iota(I32, shape, dim)


def one_hot(mask):
    return jnp.where(mask, 1.0, 0.0).astype(BF16)


def match(col, row):
    n, k = col.shape[0], row.shape[1]
    col = jnp.broadcast_to(col, (n, 128)).astype(I16)
    row = jnp.broadcast_to(row, (16, k)).astype(I16)
    col = jnp.concatenate([col] * (k // 128), axis=1)
    row = jnp.concatenate([row] * (n // 16), axis=0)
    return jnp.where(col == row, jnp.ones((), BF16), jnp.zeros((), BF16))


def dot(a, b):
    return jnp.dot(a, b, preferred_element_type=F32)


def dot_nt(a, b):
    return lax.dot_general(a, b, (((1,), (1,)), ((), ())), preferred_element_type=F32)


def eye_mask(n):
    return iota((n, n), 0) == iota((n, n), 1)


def layer_norm(values, gain_vec):
    center = values - jnp.mean(values, axis=-1, keepdims=True)
    spread = jnp.mean(center * center, axis=-1, keepdims=True)
    return center * lax.rsqrt(spread + EPSILON) * gain_vec


def gelu(x):
    return 0.5 * x * (1.0 + jnp.tanh(0.7978845608028654 * (x + 0.044715 * (x * x * x))))


def send_kernel(
    count_ref, cells_ref, owner_ref, slot_ref, vis_ref, pos_ref,
    msg_ref, starts_ref,
    left_scr, right_scr, meta_scr, starts_smem, sem,
    cells_in, owner_in, slot_in, vis_in, pos_in, in_sems,
):
    entries = cells_ref.shape[1]
    owners = msg_ref.shape[0]
    cell_total = pos_ref.shape[0]
    loads = [
        pltpu.make_async_copy(src, dst, in_sems.at[i])
        for i, (src, dst) in enumerate(
            [
                (owner_ref, owner_in),
                (cells_ref, cells_in),
                (slot_ref, slot_in),
                (pos_ref, pos_in),
                (vis_ref, vis_in),
            ]
        )
    ]
    for load in loads:
        load.start()
    for load in loads[:3]:
        load.wait()
    entry = iota((1, entries), 1)
    live = entry < count_ref[0]
    owner = jnp.where(live, owner_in[...], owners)
    owner_id = iota((owners, entries), 0)
    start_col = jnp.sum(jnp.where(owner < owner_id, 1.0, 0.0), axis=1, keepdims=True)
    start_row = jnp.sum(jnp.where(eye_mask(owners), start_col, 0.0), axis=0, keepdims=True)
    starts_ref[...] = start_row.astype(I32)
    copy = pltpu.make_async_copy(starts_ref, starts_smem, sem)
    copy.start()
    belongs = owner == owner_id
    first = jnp.sum(jnp.where(belongs, start_col, 0.0), axis=0, keepdims=True)
    within = jnp.where(live, entry - first.astype(I32), 64)
    cells = cells_in[...]
    slots = slot_in[...]
    parts = jnp.concatenate(
        [cells >> 6, cells & 63, slots >> 5, slots & 31, within, within, within, within], axis=0
    ).astype(F32).astype(BF16)
    eye = one_hot(eye_mask(128))
    lane = iota((128, 128), 1)
    cell_cols = []
    meta_parts = []
    for b in range(entries // 128):
        turned = dot_nt(eye, parts[:, b * 128 : (b + 1) * 128])
        cell_cols.append((turned[:, 0:1] * 64.0 + turned[:, 1:2]).astype(I32))
        place = turned[:, 4:5].astype(I32)
        meta_parts.append(
            jnp.where(
                lane == place,
                turned[:, 2:3] + 1.0,
                jnp.where(lane == place + 32, turned[:, 3:4], 0.0),
            ).astype(BF16)
        )
    meta_scr[...] = dot(one_hot(belongs), jnp.concatenate(meta_parts, axis=0))
    for load in loads[3:]:
        load.wait()
    step = 512
    for b in range(entries // step):
        col = jnp.concatenate(cell_cols[b * step // 128 : (b + 1) * step // 128], axis=0)
        pick = match(col, iota((1, cell_total), 1))
        rows = vis_in[b * step : (b + 1) * step, :].astype(F32) + dot(pick, pos_in[...])
        rows = rows.astype(BF16).astype(F32)
        left_scr[b * step : (b + 1) * step, :] = rows[:, 0:128]
        right_scr[b * step : (b + 1) * step, :] = rows[:, 128:256]
    left_scr[entries:, :] = jnp.zeros((left_scr.shape[0] - entries, 128), F32)
    right_scr[entries:, :] = jnp.zeros((right_scr.shape[0] - entries, 128), F32)
    copy.wait()
    sub = iota((8, 128), 0)

    def emit(o, carry):
        start = starts_smem[0, o]
        msg_ref[o, 0:16, :] = left_scr[pl.ds(start, 16), :].astype(BF16)
        msg_ref[o, 16:32, :] = right_scr[pl.ds(start, 16), :].astype(BF16)
        left = left_scr[pl.ds(start + 16, 8), :]
        right = pltpu.roll(right_scr[pl.ds(start + 16, 8), :], 2, 0)
        last = jnp.where(sub < 2, left, jnp.where(sub < 4, right, meta_scr[pl.ds(o, 1), :]))
        msg_ref[o, 32:40, :] = last.astype(BF16)
        return carry

    lax.fori_loop(0, owners, emit, 0, unroll=4)


def send_rows(vis_count, cells, owner, slot, vis, pos, owners):
    entries = vis.shape[0]
    vmem = pl.BlockSpec(memory_space=pltpu.VMEM)
    smem = pl.BlockSpec(memory_space=pltpu.SMEM)
    return pl.pallas_call(
        send_kernel,
        out_shape=(
            jax.ShapeDtypeStruct((owners, MSG, 128), BF16),
            jax.ShapeDtypeStruct((1, owners), I32),
        ),
        in_specs=[smem] + [pl.BlockSpec(memory_space=pltpu.HBM)] * 5,
        out_specs=(vmem, vmem),
        scratch_shapes=[
            pltpu.VMEM((entries + 24, 128), F32),
            pltpu.VMEM((entries + 24, 128), F32),
            pltpu.VMEM((owners, 128), F32),
            pltpu.SMEM((1, owners), I32),
            pltpu.SemaphoreType.DMA,
            pltpu.VMEM(cells.shape, I32),
            pltpu.VMEM(cells.shape, I32),
            pltpu.VMEM(cells.shape, I32),
            pltpu.VMEM(vis.shape, BF16),
            pltpu.VMEM(pos.shape, BF16),
            pltpu.SemaphoreType.DMA((5,)),
        ],
        compiler_params=pltpu.CompilerParams(vmem_limit_bytes=60 * 2**20),
        name="send_rows",
    )(vis_count, cells, owner, slot, vis, pos)


def owner_kernel(
    msg_ref, window_ref, gain1_ref, attn_in_ref, attn_out_ref, gain2_ref,
    mlp_in_ref, mlp_out_ref,
    back_ref,
    order_scr, tail_scr, q_scr, k_scr, v_scr, win_scr, att_scr, x_scr,
):
    owners = msg_ref.shape[0]
    rows = window_ref.shape[1]
    channels = attn_out_ref.shape[0]
    head_count = channels // HEAD_DIM
    full = 16 * owners
    ids = window_ref[...]
    windows = range(4)
    length = [jnp.sum(jnp.where(ids == w, 1.0, 0.0)).astype(I32) for w in windows]
    old = [sum(length[:w], jnp.int32(0)) for w in windows]
    new = []
    for w in windows:
        ahead = [
            jnp.where(length[v] >= length[w] if v < w else length[v] > length[w], length[v], 0)
            for v in windows
            if v != w
        ]
        new.append(sum(ahead, jnp.int32(0)))
    end = [new[w] + length[w] for w in windows]
    place_row = iota((1, rows), 1)
    order = sum([jnp.where(place_row >= end[w], 1, 0) for w in windows])
    order_scr[...] = order
    tail_scr[...] = msg_ref[:, 32:40, :].astype(F32).reshape(owners * 8, 128)

    def tail(j):
        return tail_scr[pl.ds(j, owners, stride=8), :]

    meta = tail(4).astype(BF16)
    place = iota((128, full), 0)
    inner = iota((128, full), 1) & 15
    spread = (
        jnp.where(place == inner, 32.0, 0.0) + jnp.where(place == inner + 32, 1.0, 0.0)
    ).astype(BF16)
    wide = dot(meta, spread)
    of_sender = (iota((owners, full), 1) >> 4) == iota((owners, full), 0)
    slot_full = jnp.sum(jnp.where(of_sender, wide, 0.0), axis=0, keepdims=True) - 32.0
    eye = eye_mask(owners)
    meta32 = meta.astype(F32)
    tail_cols = [meta32[:, j : j + 1] * 32.0 + meta32[:, j + 32 : j + 33] - 32.0 for j in (16, 17)]
    tail_slots = [jnp.sum(jnp.where(eye, c, 0.0), axis=0, keepdims=True) for c in tail_cols]
    slot_row = jnp.concatenate([slot_full] + tail_slots, axis=1).astype(I32)
    moved = slot_row + (new[0] - old[0])
    for w in windows[1:]:
        moved = jnp.where(slot_row >= old[w], slot_row + (new[w] - old[w]), moved)
    slot_row = jnp.where(slot_row >= 0, moved, -1)
    left = msg_ref[:, 0:16, :].reshape(full, 128)
    right = msg_ref[:, 16:32, :].reshape(full, 128)
    main = jnp.concatenate([left, right], axis=1)
    rest = jnp.concatenate(
        [
            jnp.concatenate([tail(0), tail(2)], axis=1),
            jnp.concatenate([tail(1), tail(3)], axis=1),
        ],
        axis=0,
    ).astype(BF16)
    step = 256
    step = 1024
    for b in range(rows // step):
        part = slice(b * step, (b + 1) * step)
        sel = match(iota((step, 1), 0) + b * step, slot_row)
        x = dot(sel[:, :full], main) + dot(sel[:, full:], rest)
        x_scr[part, :] = x
        normed = layer_norm(x, gain1_ref[...]).astype(BF16)
        projected = dot(normed, attn_in_ref[...]).astype(BF16)
        q_scr[part, :] = projected[:, :channels]
        k_scr[part, :] = projected[:, channels : 2 * channels]
        ones = jnp.ones((step, 128), BF16)
        v_scr[part, 0:128] = projected[:, 2 * channels : 2 * channels + 128]
        v_scr[part, 128:256] = ones
        v_scr[part, 256:384] = projected[:, 2 * channels + 128 :]
        v_scr[part, 384:512] = ones
    q_step = 256
    eye_q = eye_mask(128)
    for i in range(rows // 128):
        part = slice(i * 128, (i + 1) * 128)
        ids = order_scr[:, part].astype(F32)
        ids = jnp.sum(jnp.where(eye_q, ids, 0.0), axis=1, keepdims=True)
        win_scr[part, :] = jnp.broadcast_to(ids, (128, 128)).astype(I32)
    head_of_lane = iota((1, channels), 1) // HEAD_DIM
    lane_head = (iota((1, channels), 1) & 127) // HEAD_DIM
    head_mask = [one_hot(head_of_lane == h) for h in range(head_count)]
    scale = HEAD_DIM ** (-0.5) * 1.4426950408889634
    stack = 4
    half_heads = head_count // 2

    def attend(qi, key_count, key_start):
        q_rows = pl.ds(pl.multiple_of(qi * q_step, q_step), q_step)
        k_rows = pl.ds(key_start, key_count)
        q = q_scr[q_rows, :]
        keys = k_scr[k_rows, :]
        q_win = win_scr[q_rows, :]
        q_win = jnp.concatenate([q_win] * (key_count // 128), axis=1)
        bias = jnp.where(q_win == order_scr[:, k_rows], 0.0, -jnp.inf)
        bias = jnp.concatenate([bias] * stack, axis=0)
        groups = []
        for half in range(2):
            for g in range(half_heads // 4):
                groups.append((half, range(g * 4, (g + 1) * 4)))

        def scores(half, heads):
            queries = jnp.concatenate([q * head_mask[half * half_heads + h] for h in heads], axis=0)
            return dot_nt(queries, keys) + bias

        def weigh(s):
            top = jnp.max(s, axis=1, keepdims=True)
            return jnp.exp2(((s - top) * scale).astype(BF16))

        totals = [None, None]

        def mix(half, heads, e):
            o = dot(e, v_scr[k_rows, 256 * half : 256 * half + 256])
            total = totals[half]
            for i, h in enumerate(heads):
                block = o[i * q_step : (i + 1) * q_step]
                total = block if total is None else jnp.where(lane_head == h, block, total)
            totals[half] = total

        ahead = scores(*groups[0])
        held = None
        for i in range(len(groups)):
            s = ahead
            if i + 1 < len(groups):
                ahead = scores(*groups[i + 1])
            e = weigh(s)
            if held is not None:
                mix(*held)
            held = (*groups[i], e)
        mix(*held)

        for half in range(2):
            total = totals[half]
            att_scr[q_rows, 128 * half : 128 * half + 128] = (
                total[:, 0:128] * (1.0 / total[:, 128:256])
            ).astype(BF16)

    def q_block(qi, carry):
        first = qi * q_step
        low = jnp.int32(0)
        high = jnp.int32(rows)
        for w in windows:
            low = jnp.maximum(low, jnp.where(new[w] <= first, new[w], 0))
            high = jnp.minimum(high, jnp.where(end[w] >= first + q_step, end[w], rows))
        low = (low >> 7) << 7
        count = (high - low + 255) >> 8
        low = jnp.minimum(low, rows - 256 * count)
        for n in range(1, rows // 256 + 1):

            @pl.when(count == n)
            def _():
                attend(qi, 256 * n, pl.multiple_of(low, 128))

        return carry

    lax.fori_loop(0, rows // q_step, q_block, 0)
    step = 256
    for b in range(rows // step):
        part = slice(b * step, (b + 1) * step)
        x = x_scr[part, :] + dot(att_scr[part, :], attn_out_ref[...])
        normed = layer_norm(x, gain2_ref[...]).astype(BF16)
        hidden = gelu(dot(normed, mlp_in_ref[...])).astype(BF16)
        q_scr[part, :] = (x + dot(hidden, mlp_out_ref[...])).astype(BF16)
    slot_f = slot_row.astype(F32)
    eye128 = eye_mask(128)
    step = 512
    for b in range(full // step + 1):
        size = step if b < full // step else 2 * owners
        cols = []
        for i in range(size // 128):
            at = b * step + i * 128
            cols.append(
                jnp.sum(jnp.where(eye128, slot_f[:, at : at + 128], 0.0), axis=1, keepdims=True)
            )
        col = jnp.concatenate(cols, axis=0).astype(I32)
        pick = match(col, iota((1, rows), 1))
        out = dot(pick, q_scr[...])
        if b < full // step:
            o = b * step // 16
            n = step // 16
            out = out.astype(BF16)
            back_ref[o : o + n, 0:16, :] = out[:, 0:128].reshape(n, 16, 128)
            back_ref[o : o + n, 16:32, :] = out[:, 128:256].reshape(n, 16, 128)
        else:
            for j in range(2):
                tail_scr[pl.ds(j, owners, stride=8), :] = out[j * owners : (j + 1) * owners, 0:128]
                tail_scr[pl.ds(j + 2, owners, stride=8), :] = out[
                    j * owners : (j + 1) * owners, 128:256
                ]
            back_ref[:, 32:40, :] = tail_scr[...].astype(BF16).reshape(owners, 8, 128)


def owner_encode(msg, window, gain1, attn_in, attn_out, gain2, mlp_in, mlp_out):
    owners = msg.shape[0]
    rows = window.shape[1]
    channels = attn_out.shape[0]
    vmem = pl.BlockSpec(memory_space=pltpu.VMEM)
    return pl.pallas_call(
        owner_kernel,
        out_shape=jax.ShapeDtypeStruct((owners, MSG, 128), BF16),
        in_specs=[vmem] * 8,
        out_specs=vmem,
        scratch_shapes=[
            pltpu.VMEM((1, rows), I32),
            pltpu.VMEM((owners * 8, 128), F32),
            pltpu.VMEM((rows, channels), BF16),
            pltpu.VMEM((rows, channels), BF16),
            pltpu.VMEM((rows, 2 * channels), BF16),
            pltpu.VMEM((rows, 128), I32),
            pltpu.VMEM((rows, channels), BF16),
            pltpu.VMEM((rows, channels), F32),
        ],
        compiler_params=pltpu.CompilerParams(vmem_limit_bytes=40 * 2**20),
        name="owner_encode",
    )(msg, window, gain1, attn_in, attn_out, gain2, mlp_in, mlp_out)


def fill_cells(ids, cells, rows, token, pos, gain):
    hit = match(ids, cells)
    filled = dot(hit, rows)
    seen = sum([hit[:, i : i + 128] for i in range(0, hit.shape[1], 128)])
    seen = jnp.sum(seen.astype(F32), axis=1, keepdims=True)
    filled = jnp.where(seen > 0.5, filled, token)
    dec = (filled + pos.astype(F32)).astype(BF16)
    return dec, layer_norm(dec.astype(F32), gain).astype(BF16)


def edge_kernel(
    count_ref, starts_ref, back_ref, cells_ref, pos_ref, token_ref, gain_ref,
    rows_ref, dec_ref, first_ref, last_ref,
    left_scr, right_scr,
):
    owners = back_ref.shape[0]
    entries = cells_ref.shape[1]
    az, rad, height, channels = pos_ref.shape
    left_scr[...] = jnp.zeros(left_scr.shape, F32)
    right_scr[...] = jnp.zeros(right_scr.shape, F32)

    def take(o, carry):
        start = starts_ref[0, o]
        block = back_ref[o].astype(F32)
        left_scr[pl.ds(start, 16), :] = block[0:16]
        right_scr[pl.ds(start, 16), :] = block[16:32]
        left_scr[pl.ds(start + 16, 2), :] = block[32:34]
        right_scr[pl.ds(start + 16, 2), :] = block[34:36]
        return carry

    lax.fori_loop(0, owners, take, 0, unroll=8)
    rows = jnp.concatenate([left_scr[0:entries, :], right_scr[0:entries, :]], axis=1).astype(BF16)
    rows_ref[...] = rows
    cells = jnp.where(iota((1, entries), 1) < count_ref[0], cells_ref[...], -1)
    at = [(a, r) for r in (0, rad - 1) for a in range(az)]
    ids = jnp.concatenate(
        [iota((height, 1), 0) + (a * rad + r) * height for a, r in at], axis=0
    )
    pos = jnp.concatenate([pos_ref[a, r].astype(F32) for a, r in at], axis=0)
    dec, normed = fill_cells(ids, cells, rows, token_ref[...], pos, gain_ref[...])
    dec_ref[...] = dec.reshape(dec_ref.shape)
    first_ref[...] = normed[: az * height]
    last_ref[...] = normed[az * height :]


def place_edges(vis_count, starts, back, cells, pos, token, gain):
    az, rad, height, channels = pos.shape
    entries = cells.shape[1]
    vmem = pl.BlockSpec(memory_space=pltpu.VMEM)
    smem = pl.BlockSpec(memory_space=pltpu.SMEM)
    edges = jax.ShapeDtypeStruct((2, az * height, channels), BF16)
    edge = jax.ShapeDtypeStruct((az * height, channels), BF16)
    return pl.pallas_call(
        edge_kernel,
        out_shape=(jax.ShapeDtypeStruct((entries, channels), BF16), edges, edge, edge),
        in_specs=[smem, smem] + [vmem] * 5,
        out_specs=(vmem,) * 4,
        scratch_shapes=[pltpu.VMEM((entries + 24, 128), F32)] * 2,
        compiler_params=pltpu.CompilerParams(vmem_limit_bytes=24 * 2**20),
        cost_estimate=pl.CostEstimate(flops=6 * 10**8, bytes_accessed=4 * 10**6, transcendentals=0),
        name="place_edges",
    )(vis_count, starts, back, cells, pos, token, gain)


def mid_kernel(
    count_ref, rows_ref, cells_ref, pos_ref, token_ref, gain_ref,
    dec_ref, normed_ref,
):
    entries = cells_ref.shape[1]
    az, rad, height, channels = pos_ref.shape
    size = (rad - 2) * height
    rows = rows_ref[...]
    cells = jnp.where(iota((1, entries), 1) < count_ref[0], cells_ref[...], -1)
    for a in range(0, az, 2):
        ids = jnp.concatenate(
            [iota((size, 1), 0) + (i * rad + 1) * height for i in (a, a + 1)], axis=0
        )
        pos = jnp.concatenate(
            [pos_ref[i, 1 : rad - 1].reshape(size, channels) for i in (a, a + 1)], axis=0
        )
        dec, normed = fill_cells(ids, cells, rows, token_ref[...], pos, gain_ref[...])
        dec_ref[a : a + 2] = dec.reshape(2, size, channels)
        normed_ref[a : a + 2] = normed.reshape(2, size, channels)


def place_mid(vis_count, rows, cells, pos, token, gain):
    az, rad, height, channels = pos.shape
    vmem = pl.BlockSpec(memory_space=pltpu.VMEM)
    smem = pl.BlockSpec(memory_space=pltpu.SMEM)
    mid = jax.ShapeDtypeStruct((az, (rad - 2) * height, channels), BF16)
    return pl.pallas_call(
        mid_kernel,
        out_shape=(mid, mid),
        in_specs=[smem] + [vmem] * 5,
        out_specs=(vmem, vmem),
        compiler_params=pltpu.CompilerParams(vmem_limit_bytes=24 * 2**20),
        cost_estimate=pl.CostEstimate(flops=2 * 10**9, bytes_accessed=6 * 10**6, transcendentals=0),
        name="place_mid",
    )(vis_count, rows, cells, pos, token, gain)


def ring_ends():
    place = lax.axis_index("blk")
    return place == 0, place == lax.axis_size("blk") - 1


def even_sector():
    return lax.bitwise_and(lax.axis_index("sector"), 1) == 0


def rim_kernel(mid_ref, edge0_ref, edge1_ref, low_ref, high_ref, after_ref, near_ref, far_ref):
    az, size, channels = mid_ref.shape
    height = low_ref.shape[0] // az
    inside, outside = ring_ends()

    def fill(ref, a):
        part = slice(a * height, (a + 1) * height)
        ref[0:height] = jnp.where(inside, 0.0, low_ref[part].astype(F32)).astype(BF16)
        ref[height : 2 * height] = edge0_ref[part]
        ref[2 * height : 2 * height + size] = mid_ref[a]
        ref[2 * height + size : 3 * height + size] = edge1_ref[part]
        ref[3 * height + size :] = jnp.where(outside, 0.0, high_ref[part].astype(F32)).astype(BF16)

    even = even_sector()

    @pl.when(even)
    def _():
        fill(near_ref, az - 1)
        fill(far_ref, 0)

    @pl.when(jnp.logical_not(even))
    def _():
        fill(near_ref, 0)
        fill(far_ref, az - 1)


def rim_rows(mid, edge0, edge1, low, high, after):
    az, size, channels = mid.shape
    vmem = pl.BlockSpec(memory_space=pltpu.VMEM)
    out = jax.ShapeDtypeStruct((size + 4 * (low.shape[0] // az), channels), BF16)
    return pl.pallas_call(
        rim_kernel,
        out_shape=(out, out),
        in_specs=[vmem] * 5 + [pl.BlockSpec(memory_space=pl.ANY)],
        out_specs=(vmem, vmem),
        compiler_params=pltpu.CompilerParams(vmem_limit_bytes=8 * 2**20),
        name="rim_rows",
    )(mid, edge0, edge1, low, high, after)


def widen(scr, at, rows, height, drop=None):
    n, channels = rows.shape
    h = iota((n, 1), 0) % height
    values = rows.astype(F32)
    if drop is not None:
        values = jnp.where(drop, 0.0, values)
        rows = values.astype(BF16)
    scr[at : at + n, channels : 2 * channels] = rows
    below = jnp.where(h == 0, 0.0, pltpu.roll(values, 1, 0))
    scr[at : at + n, 0:channels] = below.astype(BF16)
    above = jnp.where(h == height - 1, 0.0, pltpu.roll(values, n - 1, 0))
    scr[at : at + n, 2 * channels :] = above.astype(BF16)


def first_kernel(
    mid_ref, edge0_ref, edge1_ref, mid_dec_ref, weight_ref, bias_ref,
    out_ref,
    wide_scr,
):
    planes, size, channels = out_ref.shape
    height = edge0_ref.shape[0] // mid_ref.shape[0]
    pitch = size + 2 * height

    def spread(a):
        base = a * pitch
        part = slice(a * height, (a + 1) * height)
        widen(wide_scr, base, edge0_ref[part], height)
        widen(wide_scr, base + height, mid_ref[a], height)
        widen(wide_scr, base + height + size, edge1_ref[part], height)

    def taps(a):
        total = jnp.broadcast_to(bias_ref[...], (size, channels))
        for da in range(3):
            for dr in range(3):
                at = (a + da - 1) * pitch + dr * height
                total = total + dot(wide_scr[at : at + size, :], weight_ref[da * 3 + dr])
        return total

    for a in range(3):
        spread(a)
    for a in range(1, planes + 1):
        total = taps(a)
        if a < planes:
            spread(a + 2)
        out_ref[a - 1] = (mid_dec_ref[a].astype(F32) + gelu(total)).astype(BF16)


def conv_first(planes, mid, edge0, edge1, mid_dec, weight, bias):
    az, size, channels = mid.shape
    pitch = size + 2 * (edge0.shape[0] // az)
    vmem = pl.BlockSpec(memory_space=pltpu.VMEM)
    return pl.pallas_call(
        first_kernel,
        out_shape=jax.ShapeDtypeStruct((planes, size, channels), BF16),
        in_specs=[vmem] * 6,
        out_specs=vmem,
        scratch_shapes=[pltpu.VMEM(((planes + 2) * pitch, 3 * channels), BF16)],
        compiler_params=pltpu.CompilerParams(vmem_limit_bytes=24 * 2**20),
        cost_estimate=pl.CostEstimate(flops=25 * 10**8, bytes_accessed=10**7, transcendentals=0),
        name="conv_first",
    )(mid, edge0, edge1, mid_dec, weight, bias)


def conv_kernel(
    mid_ref, edge0_ref, edge1_ref, low_ref, high_ref, mid_dec_ref, edge_dec_ref, weight_ref, bias_ref,
    first_ref,
    out_ref, partial_ref,
    wide_scr, done_scr, out_sems,
):
    az, size, channels = mid_ref.shape
    height = low_ref.shape[0] // az
    plane = size + 2 * height
    pitch = plane + 2 * height
    inside, outside = ring_ends()

    def spread(a):
        base = a * pitch
        part = slice(a * height, (a + 1) * height)
        widen(wide_scr, base, low_ref[part], height, inside)
        widen(wide_scr, base + height, edge0_ref[part], height)
        widen(wide_scr, base + 2 * height, mid_ref[a], height)
        widen(wide_scr, base + 2 * height + size, edge1_ref[part], height)
        widen(wide_scr, base + 3 * height + size, high_ref[part], height, outside)

    def taps(a):
        total = jnp.broadcast_to(bias_ref[...], (plane, channels))
        for da in range(3):
            if not 0 <= a + da - 1 < az:
                continue
            for dr in range(3):
                at = (a + da - 1) * pitch + dr * height
                total = total + dot(wide_scr[at : at + plane, :], weight_ref[da * 3 + dr])
        return total

    def side_taps():
        total = jnp.broadcast_to(bias_ref[...], (2 * planes * height, channels))
        for da in range(3):
            for dr in range(3):
                at = [
                    (a + da - 1) * pitch + (r + dr) * height
                    for a in range(1, planes + 1)
                    for r in (0, size // height + 1)
                ]
                rows = jnp.concatenate([wide_scr[i : i + height, :] for i in at], axis=0)
                total = total + dot(rows, weight_ref[da * 3 + dr])
        return total

    def finish(unit, total):
        if unit == "sides":
            done = []
            for a in range(1, planes + 1):
                part = slice(a * height, (a + 1) * height)
                for side, to in ((0, 0), (1, height + size)):
                    at = (2 * (a - 1) + side) * height
                    value = edge_dec_ref[side, part].astype(F32) + gelu(total[at : at + height])
                    done_scr[a - 1, to : to + height] = value.astype(BF16)
                done_scr[a - 1, height : height + size] = first_ref[a - 1]
                done.append(a)
            return done
        if unit in (0, az - 1):
            partial_ref[unit // (az - 1)] = total
            return []
        part = slice(unit * height, (unit + 1) * height)
        dec = jnp.concatenate(
            [edge_dec_ref[0, part], mid_dec_ref[unit], edge_dec_ref[1, part]], axis=0
        )
        done_scr[unit - 1] = (dec.astype(F32) + gelu(total)).astype(BF16)
        return [unit]

    planes = first_ref.shape[0]
    units = [(0, 1), ("sides", planes + 1)] + [(a, a + 1) for a in range(planes + 1, az)]
    ready = 0
    stores = []
    held = None
    for i, (unit, need) in enumerate(units):
        ahead = units[i + 1][1] if i + 1 < len(units) else az
        if held is None:
            while ready < need + 1:
                spread(ready)
                ready += 1
        total = side_taps() if unit == "sides" else taps(unit)
        while ready < min(ahead + 1, az):
            spread(ready)
            ready += 1
        if held is not None:
            for a in finish(*held):
                store = pltpu.make_async_copy(
                    done_scr.at[a - 1], out_ref.at[pl.ds(a * plane, plane)], out_sems.at[a - 1]
                )
                store.start()
                stores.append(store)
        held = (unit, total)
    finish(*held)
    for store in stores:
        store.wait()


def conv_inner(mid, edge0, edge1, low, high, mid_dec, edge_dec, weight, bias, first):
    az, size, channels = mid.shape
    height = low.shape[0] // az
    plane = size + 2 * height
    vmem = pl.BlockSpec(memory_space=pltpu.VMEM)
    hbm = pl.BlockSpec(memory_space=pltpu.HBM)
    return pl.pallas_call(
        conv_kernel,
        out_shape=(
            jax.ShapeDtypeStruct((az * plane, channels), BF16),
            jax.ShapeDtypeStruct((2, plane, channels), F32),
        ),
        in_specs=[vmem] * 10,
        out_specs=(hbm, vmem),
        scratch_shapes=[
            pltpu.VMEM((az * (plane + 2 * height), 3 * channels), BF16),
            pltpu.VMEM((az - 2, plane, channels), BF16),
            pltpu.SemaphoreType.DMA((az - 2,)),
        ],
        compiler_params=pltpu.CompilerParams(vmem_limit_bytes=32 * 2**20),
        cost_estimate=pl.CostEstimate(flops=6 * 10**9, bytes_accessed=10**7, transcendentals=0),
        name="conv_inner",
    )(mid, edge0, edge1, low, high, mid_dec, edge_dec, weight, bias, first)


def conv_edge_kernel(
    near_ref, far_ref, partial_ref, mid_dec_ref, edge_dec_ref, weight_ref, given_ref,
    out_ref,
    wide_scr, done_scr, out_sems,
):
    az, size, channels = mid_dec_ref.shape
    plane = partial_ref.shape[1]
    height = (plane - size) // 2
    pitch = plane + 2 * height
    even = even_sector()

    @pl.when(even)
    def _():
        widen(wide_scr, 0, far_ref[...], height)
        widen(wide_scr, pitch, near_ref[...], height)

    @pl.when(jnp.logical_not(even))
    def _():
        widen(wide_scr, 0, near_ref[...], height)
        widen(wide_scr, pitch, far_ref[...], height)

    stores = []
    for i in range(2):
        a = i * (az - 1)
        total = partial_ref[i]
        for dr in range(3):
            at = i * pitch + dr * height
            total = total + dot(wide_scr[at : at + plane, :], weight_ref[i * 6 + dr])
        part = slice(a * height, (a + 1) * height)
        dec = jnp.concatenate([edge_dec_ref[0, part], mid_dec_ref[a], edge_dec_ref[1, part]], axis=0)
        done_scr[i] = (dec.astype(F32) + gelu(total)).astype(BF16)
        store = pltpu.make_async_copy(
            done_scr.at[i], out_ref.at[pl.ds(a * plane, plane)], out_sems.at[i]
        )
        store.start()
        stores.append(store)
    for store in stores:
        store.wait()


def conv_edges(near, far, partial, mid_dec, edge_dec, weight, given):
    plane, channels = partial.shape[1:]
    vmem = pl.BlockSpec(memory_space=pltpu.VMEM)
    hbm = pl.BlockSpec(memory_space=pltpu.HBM)
    return pl.pallas_call(
        conv_edge_kernel,
        out_shape=jax.ShapeDtypeStruct(given.shape, BF16),
        in_specs=[vmem] * 6 + [hbm],
        out_specs=hbm,
        scratch_shapes=[
            pltpu.VMEM((2 * near.shape[0], 3 * channels), BF16),
            pltpu.VMEM((2, plane, channels), BF16),
            pltpu.SemaphoreType.DMA((2,)),
        ],
        input_output_aliases={6: 0},
        compiler_params=pltpu.CompilerParams(vmem_limit_bytes=16 * 2**20),
        name="conv_edges",
    )(near, far, partial, mid_dec, edge_dec, weight, given)


def exchange(values):
    return lax.all_to_all(values, ("sector", "blk"), split_axis=0, concat_axis=0, tiled=True)


def body(
    visible_feats, grid_pos, vis_cells, vis_count, owner, slot, window, enc_gain1, attn_in,
    attn_out, enc_gain2, mlp_in, mlp_out, mask_token, dec_gain, conv_weight, conv_bias,
):
    n_sector = lax.axis_size("sector")
    n_blk = lax.axis_size("blk")
    owners = n_sector * n_blk
    az, rad, height, channels = grid_pos.shape
    cell_total = az * rad * height
    pos = grid_pos.reshape(cell_total, channels)
    cells = vis_cells.reshape(1, -1)
    message, starts = send_rows(
        vis_count, cells, owner.reshape(1, -1), slot.reshape(1, -1), visible_feats, pos, owners
    )
    message = exchange(message)
    back = owner_encode(
        message, window, enc_gain1.reshape(1, -1), attn_in, attn_out,
        enc_gain2.reshape(1, -1), mlp_in, mlp_out,
    )
    back = exchange(back)
    token = mask_token.reshape(1, -1)
    gain = dec_gain.reshape(1, -1)
    rows, edge_dec, edge0, edge1 = place_edges(vis_count, starts, back, cells, grid_pos, token, gain)
    outward = [(i, (i + 1) % n_blk) for i in range(n_blk)]
    inward = [(t, s) for s, t in outward]
    rad_low = lax.ppermute(edge1, "blk", outward)
    rad_high = lax.ppermute(edge0, "blk", inward)
    mid_dec, mid = place_mid(vis_count, rows, cells, grid_pos, token, gain)
    weight = conv_weight.reshape(9, 3 * channels, channels)
    bias = conv_bias.reshape(1, -1)
    first = conv_first(PLANES_FIRST, mid, edge0, edge1, mid_dec, weight, bias)
    near, far = rim_rows(mid, edge0, edge1, rad_low, rad_high, first)
    pairs = [(i, i + 1) for i in range(0, n_sector, 2)]
    across = [(i, (i + 1) % n_sector) for i in range(1, n_sector, 2)]
    near = lax.ppermute(near, "sector", pairs + [(t, s) for s, t in pairs])
    far = lax.ppermute(far, "sector", across + [(t, s) for s, t in across])
    inner, partial = conv_inner(
        mid, edge0, edge1, rad_low, rad_high, mid_dec, edge_dec, weight, bias, first
    )
    decoded = conv_edges(near, far, partial, mid_dec, edge_dec, weight, inner)
    return decoded.reshape(az, rad, height, channels)


def solution(mesh):
    lists = P(("sector", "blk"))
    return jax.shard_map(
        body,
        mesh=mesh,
        in_specs=(
            P(("sector", "blk"), None),
            P("sector", "blk", None, None),
            lists,
            lists,
            lists,
            lists,
            P(("sector", "blk"), None),
        )
        + (P(),) * 10,
        out_specs=P("sector", "blk", None, None),
        check_vma=False,
    )
```

```python
import jax
import jax.numpy as jnp
from jax import lax
from jax.experimental import pallas as pl
from jax.experimental.pallas import tpu as pltpu
from jax.sharding import PartitionSpec as P

HEAD_DIM = 32
EPSILON = 1e-05
F32 = jnp.float32
BF16 = jnp.bfloat16
I16 = jnp.int16
I32 = jnp.int32
CAP = 18
PLANES_FIRST = 3
MSG = 40


def iota(shape, dim):
    return lax.broadcasted_iota(I32, shape, dim)


def one_hot(mask):
    return jnp.where(mask, 1.0, 0.0).astype(BF16)


def match(col, row):
    n, k = col.shape[0], row.shape[1]
    col = jnp.broadcast_to(col, (n, 128)).astype(I16)
    row = jnp.broadcast_to(row, (16, k)).astype(I16)
    col = jnp.concatenate([col] * (k // 128), axis=1)
    row = jnp.concatenate([row] * (n // 16), axis=0)
    return jnp.where(col == row, jnp.ones((), BF16), jnp.zeros((), BF16))


def dot(a, b):
    return jnp.dot(a, b, preferred_element_type=F32)


def dot_nt(a, b):
    return lax.dot_general(a, b, (((1,), (1,)), ((), ())), preferred_element_type=F32)


def eye_mask(n):
    return iota((n, n), 0) == iota((n, n), 1)


def layer_norm(values, gain_vec):
    center = values - jnp.mean(values, axis=-1, keepdims=True)
    spread = jnp.mean(center * center, axis=-1, keepdims=True)
    return center * lax.rsqrt(spread + EPSILON) * gain_vec


def gelu(x):
    return 0.5 * x * (1.0 + jnp.tanh(0.7978845608028654 * (x + 0.044715 * (x * x * x))))


def send_kernel(
    count_ref, cells_ref, owner_ref, slot_ref, vis_ref, pos_ref,
    msg_ref, starts_ref,
    left_scr, right_scr, meta_scr, starts_smem, sem,
    cells_in, owner_in, slot_in, vis_in, pos_in, in_sems,
):
    entries = cells_ref.shape[1]
    owners = msg_ref.shape[0]
    cell_total = pos_ref.shape[0]
    loads = [
        pltpu.make_async_copy(src, dst, in_sems.at[i])
        for i, (src, dst) in enumerate(
            [
                (owner_ref, owner_in),
                (cells_ref, cells_in),
                (slot_ref, slot_in),
                (pos_ref, pos_in),
                (vis_ref, vis_in),
            ]
        )
    ]
    for load in loads:
        load.start()
    for load in loads[:3]:
        load.wait()
    entry = iota((1, entries), 1)
    live = entry < count_ref[0]
    owner = jnp.where(live, owner_in[...], owners)
    owner_id = iota((owners, entries), 0)
    start_col = jnp.sum(jnp.where(owner < owner_id, 1.0, 0.0), axis=1, keepdims=True)
    start_row = jnp.sum(jnp.where(eye_mask(owners), start_col, 0.0), axis=0, keepdims=True)
    starts_ref[...] = start_row.astype(I32)
    copy = pltpu.make_async_copy(starts_ref, starts_smem, sem)
    copy.start()
    belongs = owner == owner_id
    first = jnp.sum(jnp.where(belongs, start_col, 0.0), axis=0, keepdims=True)
    within = jnp.where(live, entry - first.astype(I32), 64)
    cells = cells_in[...]
    slots = slot_in[...]
    parts = jnp.concatenate(
        [cells >> 6, cells & 63, slots >> 5, slots & 31, within, within, within, within], axis=0
    ).astype(F32).astype(BF16)
    eye = one_hot(eye_mask(128))
    lane = iota((128, 128), 1)
    cell_cols = []
    meta_parts = []
    for b in range(entries // 128):
        turned = dot_nt(eye, parts[:, b * 128 : (b + 1) * 128])
        cell_cols.append((turned[:, 0:1] * 64.0 + turned[:, 1:2]).astype(I32))
        place = turned[:, 4:5].astype(I32)
        meta_parts.append(
            jnp.where(
                lane == place,
                turned[:, 2:3] + 1.0,
                jnp.where(lane == place + 32, turned[:, 3:4], 0.0),
            ).astype(BF16)
        )
    meta_scr[...] = dot(one_hot(belongs), jnp.concatenate(meta_parts, axis=0))
    for load in loads[3:]:
        load.wait()
    step = 512
    for b in range(entries // step):
        col = jnp.concatenate(cell_cols[b * step // 128 : (b + 1) * step // 128], axis=0)
        pick = match(col, iota((1, cell_total), 1))
        rows = vis_in[b * step : (b + 1) * step, :].astype(F32) + dot(pick, pos_in[...])
        rows = rows.astype(BF16).astype(F32)
        left_scr[b * step : (b + 1) * step, :] = rows[:, 0:128]
        right_scr[b * step : (b + 1) * step, :] = rows[:, 128:256]
    left_scr[entries:, :] = jnp.zeros((left_scr.shape[0] - entries, 128), F32)
    right_scr[entries:, :] = jnp.zeros((right_scr.shape[0] - entries, 128), F32)
    copy.wait()
    sub = iota((8, 128), 0)

    def emit(o, carry):
        start = starts_smem[0, o]
        msg_ref[o, 0:16, :] = left_scr[pl.ds(start, 16), :].astype(BF16)
        msg_ref[o, 16:32, :] = right_scr[pl.ds(start, 16), :].astype(BF16)
        left = left_scr[pl.ds(start + 16, 8), :]
        right = pltpu.roll(right_scr[pl.ds(start + 16, 8), :], 2, 0)
        last = jnp.where(sub < 2, left, jnp.where(sub < 4, right, meta_scr[pl.ds(o, 1), :]))
        msg_ref[o, 32:40, :] = last.astype(BF16)
        return carry

    lax.fori_loop(0, owners, emit, 0, unroll=4)


def send_rows(vis_count, cells, owner, slot, vis, pos, owners):
    entries = vis.shape[0]
    vmem = pl.BlockSpec(memory_space=pltpu.VMEM)
    smem = pl.BlockSpec(memory_space=pltpu.SMEM)
    return pl.pallas_call(
        send_kernel,
        out_shape=(
            jax.ShapeDtypeStruct((owners, MSG, 128), BF16),
            jax.ShapeDtypeStruct((1, owners), I32),
        ),
        in_specs=[smem] + [pl.BlockSpec(memory_space=pltpu.HBM)] * 5,
        out_specs=(vmem, vmem),
        scratch_shapes=[
            pltpu.VMEM((entries + 24, 128), F32),
            pltpu.VMEM((entries + 24, 128), F32),
            pltpu.VMEM((owners, 128), F32),
            pltpu.SMEM((1, owners), I32),
            pltpu.SemaphoreType.DMA,
            pltpu.VMEM(cells.shape, I32),
            pltpu.VMEM(cells.shape, I32),
            pltpu.VMEM(cells.shape, I32),
            pltpu.VMEM(vis.shape, BF16),
            pltpu.VMEM(pos.shape, BF16),
            pltpu.SemaphoreType.DMA((5,)),
        ],
        compiler_params=pltpu.CompilerParams(vmem_limit_bytes=60 * 2**20),
        name="send_rows",
    )(vis_count, cells, owner, slot, vis, pos)


def owner_kernel(
    msg_ref, window_ref, gain1_ref, attn_in_ref, attn_out_ref, gain2_ref,
    mlp_in_ref, mlp_out_ref,
    back_ref,
    order_scr, tail_scr, q_scr, k_scr, v_scr, win_scr, att_scr, x_scr,
):
    owners = msg_ref.shape[0]
    rows = window_ref.shape[1]
    channels = attn_out_ref.shape[0]
    head_count = channels // HEAD_DIM
    full = 16 * owners
    ids = window_ref[...]
    windows = range(4)
    length = [jnp.sum(jnp.where(ids == w, 1.0, 0.0)).astype(I32) for w in windows]
    old = [sum(length[:w], jnp.int32(0)) for w in windows]
    new = []
    for w in windows:
        ahead = [
            jnp.where(length[v] >= length[w] if v < w else length[v] > length[w], length[v], 0)
            for v in windows
            if v != w
        ]
        new.append(sum(ahead, jnp.int32(0)))
    end = [new[w] + length[w] for w in windows]
    place_row = iota((1, rows), 1)
    order = sum([jnp.where(place_row >= end[w], 1, 0) for w in windows])
    order_scr[...] = order
    tail_scr[...] = msg_ref[:, 32:40, :].astype(F32).reshape(owners * 8, 128)

    def tail(j):
        return tail_scr[pl.ds(j, owners, stride=8), :]

    meta = tail(4).astype(BF16)
    place = iota((128, full), 0)
    inner = iota((128, full), 1) & 15
    spread = (
        jnp.where(place == inner, 32.0, 0.0) + jnp.where(place == inner + 32, 1.0, 0.0)
    ).astype(BF16)
    wide = dot(meta, spread)
    of_sender = (iota((owners, full), 1) >> 4) == iota((owners, full), 0)
    slot_full = jnp.sum(jnp.where(of_sender, wide, 0.0), axis=0, keepdims=True) - 32.0
    eye = eye_mask(owners)
    meta32 = meta.astype(F32)
    tail_cols = [meta32[:, j : j + 1] * 32.0 + meta32[:, j + 32 : j + 33] - 32.0 for j in (16, 17)]
    tail_slots = [jnp.sum(jnp.where(eye, c, 0.0), axis=0, keepdims=True) for c in tail_cols]
    slot_row = jnp.concatenate([slot_full] + tail_slots, axis=1).astype(I32)
    moved = slot_row + (new[0] - old[0])
    for w in windows[1:]:
        moved = jnp.where(slot_row >= old[w], slot_row + (new[w] - old[w]), moved)
    slot_row = jnp.where(slot_row >= 0, moved, -1)
    left = msg_ref[:, 0:16, :].reshape(full, 128)
    right = msg_ref[:, 16:32, :].reshape(full, 128)
    main = jnp.concatenate([left, right], axis=1)
    rest = jnp.concatenate(
        [
            jnp.concatenate([tail(0), tail(2)], axis=1),
            jnp.concatenate([tail(1), tail(3)], axis=1),
        ],
        axis=0,
    ).astype(BF16)
    step = 256
    step = 1024
    for b in range(rows // step):
        part = slice(b * step, (b + 1) * step)
        sel = match(iota((step, 1), 0) + b * step, slot_row)
        x = dot(sel[:, :full], main) + dot(sel[:, full:], rest)
        x_scr[part, :] = x
        normed = layer_norm(x, gain1_ref[...]).astype(BF16)
        projected = dot(normed, attn_in_ref[...]).astype(BF16)
        q_scr[part, :] = projected[:, :channels]
        k_scr[part, :] = projected[:, channels : 2 * channels]
        ones = jnp.ones((step, 128), BF16)
        v_scr[part, 0:128] = projected[:, 2 * channels : 2 * channels + 128]
        v_scr[part, 128:256] = ones
        v_scr[part, 256:384] = projected[:, 2 * channels + 128 :]
        v_scr[part, 384:512] = ones
    q_step = 256
    eye_q = eye_mask(128)
    for i in range(rows // 128):
        part = slice(i * 128, (i + 1) * 128)
        ids = order_scr[:, part].astype(F32)
        ids = jnp.sum(jnp.where(eye_q, ids, 0.0), axis=1, keepdims=True)
        win_scr[part, :] = jnp.broadcast_to(ids, (128, 128)).astype(I32)
    head_of_lane = iota((1, channels), 1) // HEAD_DIM
    lane_head = (iota((1, channels), 1) & 127) // HEAD_DIM
    head_mask = [one_hot(head_of_lane == h) for h in range(head_count)]
    scale = HEAD_DIM ** (-0.5) * 1.4426950408889634
    stack = 4
    half_heads = head_count // 2

    def attend(qi, key_count, key_start):
        q_rows = pl.ds(pl.multiple_of(qi * q_step, q_step), q_step)
        k_rows = pl.ds(key_start, key_count)
        q = q_scr[q_rows, :]
        keys = k_scr[k_rows, :]
        q_win = win_scr[q_rows, :]
        q_win = jnp.concatenate([q_win] * (key_count // 128), axis=1)
        bias = jnp.where(q_win == order_scr[:, k_rows], 0.0, -jnp.inf)
        bias = jnp.concatenate([bias] * stack, axis=0)
        groups = []
        for half in range(2):
            for g in range(half_heads // 4):
                groups.append((half, range(g * 4, (g + 1) * 4)))

        def scores(half, heads):
            queries = jnp.concatenate([q * head_mask[half * half_heads + h] for h in heads], axis=0)
            return dot_nt(queries, keys) + bias

        def weigh(s):
            top = jnp.max(s, axis=1, keepdims=True)
            return jnp.exp2(((s - top) * scale).astype(BF16))

        totals = [None, None]

        def mix(half, heads, e):
            o = dot(e, v_scr[k_rows, 256 * half : 256 * half + 256])
            total = totals[half]
            for i, h in enumerate(heads):
                block = o[i * q_step : (i + 1) * q_step]
                total = block if total is None else jnp.where(lane_head == h, block, total)
            totals[half] = total

        ahead = scores(*groups[0])
        held = None
        for i in range(len(groups)):
            s = ahead
            if i + 1 < len(groups):
                ahead = scores(*groups[i + 1])
            e = weigh(s)
            if held is not None:
                mix(*held)
            held = (*groups[i], e)
        mix(*held)

        for half in range(2):
            total = totals[half]
            att_scr[q_rows, 128 * half : 128 * half + 128] = (
                total[:, 0:128] * (1.0 / total[:, 128:256])
            ).astype(BF16)

    def q_block(qi, carry):
        first = qi * q_step
        low = jnp.int32(0)
        high = jnp.int32(rows)
        for w in windows:
            low = jnp.maximum(low, jnp.where(new[w] <= first, new[w], 0))
            high = jnp.minimum(high, jnp.where(end[w] >= first + q_step, end[w], rows))
        low = (low >> 7) << 7
        count = (high - low + 255) >> 8
        low = jnp.minimum(low, rows - 256 * count)
        for n in range(1, rows // 256 + 1):

            @pl.when(count == n)
            def _():
                attend(qi, 256 * n, pl.multiple_of(low, 128))

        return carry

    lax.fori_loop(0, rows // q_step, q_block, 0)
    step = 256
    for b in range(rows // step):
        part = slice(b * step, (b + 1) * step)
        x = x_scr[part, :] + dot(att_scr[part, :], attn_out_ref[...])
        normed = layer_norm(x, gain2_ref[...]).astype(BF16)
        hidden = gelu(dot(normed, mlp_in_ref[...])).astype(BF16)
        q_scr[part, :] = (x + dot(hidden, mlp_out_ref[...])).astype(BF16)
    slot_f = slot_row.astype(F32)
    eye128 = eye_mask(128)
    step = 512
    for b in range(full // step + 1):
        size = step if b < full // step else 2 * owners
        cols = []
        for i in range(size // 128):
            at = b * step + i * 128
            cols.append(
                jnp.sum(jnp.where(eye128, slot_f[:, at : at + 128], 0.0), axis=1, keepdims=True)
            )
        col = jnp.concatenate(cols, axis=0).astype(I32)
        pick = match(col, iota((1, rows), 1))
        out = dot(pick, q_scr[...])
        if b < full // step:
            o = b * step // 16
            n = step // 16
            out = out.astype(BF16)
            back_ref[o : o + n, 0:16, :] = out[:, 0:128].reshape(n, 16, 128)
            back_ref[o : o + n, 16:32, :] = out[:, 128:256].reshape(n, 16, 128)
        else:
            for j in range(2):
                tail_scr[pl.ds(j, owners, stride=8), :] = out[j * owners : (j + 1) * owners, 0:128]
                tail_scr[pl.ds(j + 2, owners, stride=8), :] = out[
                    j * owners : (j + 1) * owners, 128:256
                ]
            back_ref[:, 32:40, :] = tail_scr[...].astype(BF16).reshape(owners, 8, 128)


def owner_encode(msg, window, gain1, attn_in, attn_out, gain2, mlp_in, mlp_out):
    owners = msg.shape[0]
    rows = window.shape[1]
    channels = attn_out.shape[0]
    vmem = pl.BlockSpec(memory_space=pltpu.VMEM)
    return pl.pallas_call(
        owner_kernel,
        out_shape=jax.ShapeDtypeStruct((owners, MSG, 128), BF16),
        in_specs=[vmem] * 8,
        out_specs=vmem,
        scratch_shapes=[
            pltpu.VMEM((1, rows), I32),
            pltpu.VMEM((owners * 8, 128), F32),
            pltpu.VMEM((rows, channels), BF16),
            pltpu.VMEM((rows, channels), BF16),
            pltpu.VMEM((rows, 2 * channels), BF16),
            pltpu.VMEM((rows, 128), I32),
            pltpu.VMEM((rows, channels), BF16),
            pltpu.VMEM((rows, channels), F32),
        ],
        compiler_params=pltpu.CompilerParams(vmem_limit_bytes=40 * 2**20),
        name="owner_encode",
    )(msg, window, gain1, attn_in, attn_out, gain2, mlp_in, mlp_out)


def cell_hits(ids, cells):
    hit = match(ids, cells)
    seen = sum([hit[:, i : i + 128] for i in range(0, hit.shape[1], 128)])
    return hit, jnp.sum(seen.astype(F32), axis=1, keepdims=True) > 0.5


def norm_cells(filled, seen, token, pos, gain):
    dec = (jnp.where(seen, filled, token) + pos.astype(F32)).astype(BF16)
    return dec, layer_norm(dec.astype(F32), gain).astype(BF16)


def edge_kernel(
    count_ref, starts_ref, back_ref, cells_ref, pos_ref, token_ref, gain_ref,
    rows_ref, dec_ref, first_ref, last_ref,
    left_scr, right_scr,
):
    owners = back_ref.shape[0]
    entries = cells_ref.shape[1]
    az, rad, height, channels = pos_ref.shape
    left_scr[...] = jnp.zeros(left_scr.shape, F32)
    right_scr[...] = jnp.zeros(right_scr.shape, F32)

    def take(o, carry):
        start = starts_ref[0, o]
        block = back_ref[o].astype(F32)
        left_scr[pl.ds(start, 16), :] = block[0:16]
        right_scr[pl.ds(start, 16), :] = block[16:32]
        left_scr[pl.ds(start + 16, 2), :] = block[32:34]
        right_scr[pl.ds(start + 16, 2), :] = block[34:36]
        return carry

    lax.fori_loop(0, owners, take, 0, unroll=8)
    rows = jnp.concatenate([left_scr[0:entries, :], right_scr[0:entries, :]], axis=1).astype(BF16)
    rows_ref[...] = rows
    cells = jnp.where(iota((1, entries), 1) < count_ref[0], cells_ref[...], -1)
    at = [(a, r) for r in (0, rad - 1) for a in range(az)]
    ids = jnp.concatenate(
        [iota((height, 1), 0) + (a * rad + r) * height for a, r in at], axis=0
    )
    pos = jnp.concatenate([pos_ref[a, r].astype(F32) for a, r in at], axis=0)
    hit, seen = cell_hits(ids, cells)
    dec, normed = norm_cells(dot(hit, rows), seen, token_ref[...], pos, gain_ref[...])
    dec_ref[...] = dec.reshape(dec_ref.shape)
    first_ref[...] = normed[: az * height]
    last_ref[...] = normed[az * height :]


def place_edges(vis_count, starts, back, cells, pos, token, gain):
    az, rad, height, channels = pos.shape
    entries = cells.shape[1]
    vmem = pl.BlockSpec(memory_space=pltpu.VMEM)
    smem = pl.BlockSpec(memory_space=pltpu.SMEM)
    edges = jax.ShapeDtypeStruct((2, az * height, channels), BF16)
    edge = jax.ShapeDtypeStruct((az * height, channels), BF16)
    return pl.pallas_call(
        edge_kernel,
        out_shape=(jax.ShapeDtypeStruct((entries, channels), BF16), edges, edge, edge),
        in_specs=[smem, smem] + [vmem] * 5,
        out_specs=(vmem,) * 4,
        scratch_shapes=[pltpu.VMEM((entries + 24, 128), F32)] * 2,
        compiler_params=pltpu.CompilerParams(vmem_limit_bytes=24 * 2**20),
        cost_estimate=pl.CostEstimate(flops=6 * 10**8, bytes_accessed=4 * 10**6, transcendentals=0),
        name="place_edges",
    )(vis_count, starts, back, cells, pos, token, gain)


def mid_kernel(
    count_ref, rows_ref, cells_ref, pos_ref, token_ref, gain_ref,
    dec_ref, normed_ref,
):
    entries = cells_ref.shape[1]
    az, rad, height, channels = pos_ref.shape
    size = (rad - 2) * height
    rows = rows_ref[...]
    cells = jnp.where(iota((1, entries), 1) < count_ref[0], cells_ref[...], -1)

    def pick(a):
        return cell_hits(iota((size, 1), 0) + (a * rad + 1) * height, cells)

    def finish(a, filled, seen):
        pos = pos_ref[a, 1 : rad - 1].reshape(size, channels)
        dec, normed = norm_cells(filled, seen, token_ref[...], pos, gain_ref[...])
        dec_ref[a] = dec
        normed_ref[a] = normed

    ahead = pick(0)
    held = None
    for a in range(az):
        hit, seen = ahead
        if a + 1 < az:
            ahead = pick(a + 1)
        filled = dot(hit, rows)
        if held is not None:
            finish(*held)
        held = (a, filled, seen)
    finish(*held)


def place_mid(vis_count, rows, cells, pos, token, gain):
    az, rad, height, channels = pos.shape
    vmem = pl.BlockSpec(memory_space=pltpu.VMEM)
    smem = pl.BlockSpec(memory_space=pltpu.SMEM)
    mid = jax.ShapeDtypeStruct((az, (rad - 2) * height, channels), BF16)
    return pl.pallas_call(
        mid_kernel,
        out_shape=(mid, mid),
        in_specs=[smem] + [vmem] * 5,
        out_specs=(vmem, vmem),
        compiler_params=pltpu.CompilerParams(vmem_limit_bytes=24 * 2**20),
        cost_estimate=pl.CostEstimate(flops=2 * 10**9, bytes_accessed=6 * 10**6, transcendentals=0),
        name="place_mid",
    )(vis_count, rows, cells, pos, token, gain)


def ring_ends():
    place = lax.axis_index("blk")
    return place == 0, place == lax.axis_size("blk") - 1


def even_sector():
    return lax.bitwise_and(lax.axis_index("sector"), 1) == 0


def rim_kernel(mid_ref, edge0_ref, edge1_ref, low_ref, high_ref, after_ref, near_ref, far_ref):
    az, size, channels = mid_ref.shape
    height = low_ref.shape[0] // az
    inside, outside = ring_ends()

    def fill(ref, a):
        part = slice(a * height, (a + 1) * height)
        ref[0:height] = jnp.where(inside, 0.0, low_ref[part].astype(F32)).astype(BF16)
        ref[height : 2 * height] = edge0_ref[part]
        ref[2 * height : 2 * height + size] = mid_ref[a]
        ref[2 * height + size : 3 * height + size] = edge1_ref[part]
        ref[3 * height + size :] = jnp.where(outside, 0.0, high_ref[part].astype(F32)).astype(BF16)

    even = even_sector()

    @pl.when(even)
    def _():
        fill(near_ref, az - 1)
        fill(far_ref, 0)

    @pl.when(jnp.logical_not(even))
    def _():
        fill(near_ref, 0)
        fill(far_ref, az - 1)


def rim_rows(mid, edge0, edge1, low, high, after):
    az, size, channels = mid.shape
    vmem = pl.BlockSpec(memory_space=pltpu.VMEM)
    out = jax.ShapeDtypeStruct((size + 4 * (low.shape[0] // az), channels), BF16)
    return pl.pallas_call(
        rim_kernel,
        out_shape=(out, out),
        in_specs=[vmem] * 5 + [pl.BlockSpec(memory_space=pl.ANY)],
        out_specs=(vmem, vmem),
        compiler_params=pltpu.CompilerParams(vmem_limit_bytes=8 * 2**20),
        name="rim_rows",
    )(mid, edge0, edge1, low, high, after)


def widen(scr, at, rows, height, drop=None):
    n, channels = rows.shape
    h = iota((n, 1), 0) % height
    values = rows.astype(F32)
    if drop is not None:
        values = jnp.where(drop, 0.0, values)
        rows = values.astype(BF16)
    scr[at : at + n, channels : 2 * channels] = rows
    below = jnp.where(h == 0, 0.0, pltpu.roll(values, 1, 0))
    scr[at : at + n, 0:channels] = below.astype(BF16)
    above = jnp.where(h == height - 1, 0.0, pltpu.roll(values, n - 1, 0))
    scr[at : at + n, 2 * channels :] = above.astype(BF16)


def first_kernel(
    mid_ref, edge0_ref, edge1_ref, mid_dec_ref, weight_ref, bias_ref,
    out_ref,
    wide_scr,
):
    planes, size, channels = out_ref.shape
    height = edge0_ref.shape[0] // mid_ref.shape[0]
    pitch = size + 2 * height

    def spread(a):
        base = a * pitch
        part = slice(a * height, (a + 1) * height)
        widen(wide_scr, base, edge0_ref[part], height)
        widen(wide_scr, base + height, mid_ref[a], height)
        widen(wide_scr, base + height + size, edge1_ref[part], height)

    def taps(a):
        total = jnp.broadcast_to(bias_ref[...], (size, channels))
        for da in range(3):
            for dr in range(3):
                at = (a + da - 1) * pitch + dr * height
                total = total + dot(wide_scr[at : at + size, :], weight_ref[da * 3 + dr])
        return total

    for a in range(3):
        spread(a)
    for a in range(1, planes + 1):
        total = taps(a)
        if a < planes:
            spread(a + 2)
        out_ref[a - 1] = (mid_dec_ref[a].astype(F32) + gelu(total)).astype(BF16)


def conv_first(planes, mid, edge0, edge1, mid_dec, weight, bias):
    az, size, channels = mid.shape
    pitch = size + 2 * (edge0.shape[0] // az)
    vmem = pl.BlockSpec(memory_space=pltpu.VMEM)
    return pl.pallas_call(
        first_kernel,
        out_shape=jax.ShapeDtypeStruct((planes, size, channels), BF16),
        in_specs=[vmem] * 6,
        out_specs=vmem,
        scratch_shapes=[pltpu.VMEM(((planes + 2) * pitch, 3 * channels), BF16)],
        compiler_params=pltpu.CompilerParams(vmem_limit_bytes=24 * 2**20),
        cost_estimate=pl.CostEstimate(flops=25 * 10**8, bytes_accessed=10**7, transcendentals=0),
        name="conv_first",
    )(mid, edge0, edge1, mid_dec, weight, bias)


def conv_kernel(
    mid_ref, edge0_ref, edge1_ref, low_ref, high_ref, mid_dec_ref, edge_dec_ref, weight_ref, bias_ref,
    first_ref,
    out_ref, partial_ref,
    wide_scr, done_scr, out_sems,
):
    az, size, channels = mid_ref.shape
    height = low_ref.shape[0] // az
    plane = size + 2 * height
    pitch = plane + 2 * height
    inside, outside = ring_ends()

    def spread(a):
        base = a * pitch
        part = slice(a * height, (a + 1) * height)
        widen(wide_scr, base, low_ref[part], height, inside)
        widen(wide_scr, base + height, edge0_ref[part], height)
        widen(wide_scr, base + 2 * height, mid_ref[a], height)
        widen(wide_scr, base + 2 * height + size, edge1_ref[part], height)
        widen(wide_scr, base + 3 * height + size, high_ref[part], height, outside)

    def taps(a):
        total = jnp.broadcast_to(bias_ref[...], (plane, channels))
        for da in range(3):
            if not 0 <= a + da - 1 < az:
                continue
            for dr in range(3):
                at = (a + da - 1) * pitch + dr * height
                total = total + dot(wide_scr[at : at + plane, :], weight_ref[da * 3 + dr])
        return total

    def side_taps():
        total = jnp.broadcast_to(bias_ref[...], (2 * planes * height, channels))
        for da in range(3):
            for dr in range(3):
                at = [
                    (a + da - 1) * pitch + (r + dr) * height
                    for a in range(1, planes + 1)
                    for r in (0, size // height + 1)
                ]
                rows = jnp.concatenate([wide_scr[i : i + height, :] for i in at], axis=0)
                total = total + dot(rows, weight_ref[da * 3 + dr])
        return total

    def finish(unit, total):
        if unit == "sides":
            done = []
            for a in range(1, planes + 1):
                part = slice(a * height, (a + 1) * height)
                for side, to in ((0, 0), (1, height + size)):
                    at = (2 * (a - 1) + side) * height
                    value = edge_dec_ref[side, part].astype(F32) + gelu(total[at : at + height])
                    done_scr[a - 1, to : to + height] = value.astype(BF16)
                done_scr[a - 1, height : height + size] = first_ref[a - 1]
                done.append(a)
            return done
        if unit in (0, az - 1):
            partial_ref[unit // (az - 1)] = total
            return []
        part = slice(unit * height, (unit + 1) * height)
        dec = jnp.concatenate(
            [edge_dec_ref[0, part], mid_dec_ref[unit], edge_dec_ref[1, part]], axis=0
        )
        done_scr[unit - 1] = (dec.astype(F32) + gelu(total)).astype(BF16)
        return [unit]

    planes = first_ref.shape[0]
    units = [(0, 1), ("sides", planes + 1)] + [(a, a + 1) for a in range(planes + 1, az)]
    ready = 0
    stores = []
    held = None
    for i, (unit, need) in enumerate(units):
        ahead = units[i + 1][1] if i + 1 < len(units) else az
        if held is None:
            while ready < need + 1:
                spread(ready)
                ready += 1
        total = side_taps() if unit == "sides" else taps(unit)
        while ready < min(ahead + 1, az):
            spread(ready)
            ready += 1
        if held is not None:
            for a in finish(*held):
                store = pltpu.make_async_copy(
                    done_scr.at[a - 1], out_ref.at[pl.ds(a * plane, plane)], out_sems.at[a - 1]
                )
                store.start()
                stores.append(store)
        held = (unit, total)
    finish(*held)
    for store in stores:
        store.wait()


def conv_inner(mid, edge0, edge1, low, high, mid_dec, edge_dec, weight, bias, first):
    az, size, channels = mid.shape
    height = low.shape[0] // az
    plane = size + 2 * height
    vmem = pl.BlockSpec(memory_space=pltpu.VMEM)
    hbm = pl.BlockSpec(memory_space=pltpu.HBM)
    return pl.pallas_call(
        conv_kernel,
        out_shape=(
            jax.ShapeDtypeStruct((az * plane, channels), BF16),
            jax.ShapeDtypeStruct((2, plane, channels), F32),
        ),
        in_specs=[vmem] * 10,
        out_specs=(hbm, vmem),
        scratch_shapes=[
            pltpu.VMEM((az * (plane + 2 * height), 3 * channels), BF16),
            pltpu.VMEM((az - 2, plane, channels), BF16),
            pltpu.SemaphoreType.DMA((az - 2,)),
        ],
        compiler_params=pltpu.CompilerParams(vmem_limit_bytes=32 * 2**20),
        cost_estimate=pl.CostEstimate(flops=6 * 10**9, bytes_accessed=10**7, transcendentals=0),
        name="conv_inner",
    )(mid, edge0, edge1, low, high, mid_dec, edge_dec, weight, bias, first)


def conv_edge_kernel(
    near_ref, far_ref, partial_ref, mid_dec_ref, edge_dec_ref, weight_ref, given_ref,
    out_ref,
    wide_scr, done_scr, out_sems,
):
    az, size, channels = mid_dec_ref.shape
    plane = partial_ref.shape[1]
    height = (plane - size) // 2
    pitch = plane + 2 * height
    even = even_sector()

    @pl.when(even)
    def _():
        widen(wide_scr, 0, far_ref[...], height)
        widen(wide_scr, pitch, near_ref[...], height)

    @pl.when(jnp.logical_not(even))
    def _():
        widen(wide_scr, 0, near_ref[...], height)
        widen(wide_scr, pitch, far_ref[...], height)

    stores = []
    for i in range(2):
        a = i * (az - 1)
        total = partial_ref[i]
        for dr in range(3):
            at = i * pitch + dr * height
            total = total + dot(wide_scr[at : at + plane, :], weight_ref[i * 6 + dr])
        part = slice(a * height, (a + 1) * height)
        dec = jnp.concatenate([edge_dec_ref[0, part], mid_dec_ref[a], edge_dec_ref[1, part]], axis=0)
        done_scr[i] = (dec.astype(F32) + gelu(total)).astype(BF16)
        store = pltpu.make_async_copy(
            done_scr.at[i], out_ref.at[pl.ds(a * plane, plane)], out_sems.at[i]
        )
        store.start()
        stores.append(store)
    for store in stores:
        store.wait()


def conv_edges(near, far, partial, mid_dec, edge_dec, weight, given):
    plane, channels = partial.shape[1:]
    vmem = pl.BlockSpec(memory_space=pltpu.VMEM)
    hbm = pl.BlockSpec(memory_space=pltpu.HBM)
    return pl.pallas_call(
        conv_edge_kernel,
        out_shape=jax.ShapeDtypeStruct(given.shape, BF16),
        in_specs=[vmem] * 6 + [hbm],
        out_specs=hbm,
        scratch_shapes=[
            pltpu.VMEM((2 * near.shape[0], 3 * channels), BF16),
            pltpu.VMEM((2, plane, channels), BF16),
            pltpu.SemaphoreType.DMA((2,)),
        ],
        input_output_aliases={6: 0},
        compiler_params=pltpu.CompilerParams(vmem_limit_bytes=16 * 2**20),
        name="conv_edges",
    )(near, far, partial, mid_dec, edge_dec, weight, given)


def exchange(values):
    return lax.all_to_all(values, ("sector", "blk"), split_axis=0, concat_axis=0, tiled=True)


def body(
    visible_feats, grid_pos, vis_cells, vis_count, owner, slot, window, enc_gain1, attn_in,
    attn_out, enc_gain2, mlp_in, mlp_out, mask_token, dec_gain, conv_weight, conv_bias,
):
    n_sector = lax.axis_size("sector")
    n_blk = lax.axis_size("blk")
    owners = n_sector * n_blk
    az, rad, height, channels = grid_pos.shape
    cell_total = az * rad * height
    pos = grid_pos.reshape(cell_total, channels)
    cells = vis_cells.reshape(1, -1)
    message, starts = send_rows(
        vis_count, cells, owner.reshape(1, -1), slot.reshape(1, -1), visible_feats, pos, owners
    )
    message = exchange(message)
    back = owner_encode(
        message, window, enc_gain1.reshape(1, -1), attn_in, attn_out,
        enc_gain2.reshape(1, -1), mlp_in, mlp_out,
    )
    back = exchange(back)
    token = mask_token.reshape(1, -1)
    gain = dec_gain.reshape(1, -1)
    rows, edge_dec, edge0, edge1 = place_edges(vis_count, starts, back, cells, grid_pos, token, gain)
    outward = [(i, (i + 1) % n_blk) for i in range(n_blk)]
    inward = [(t, s) for s, t in outward]
    rad_low = lax.ppermute(edge1, "blk", outward)
    rad_high = lax.ppermute(edge0, "blk", inward)
    mid_dec, mid = place_mid(vis_count, rows, cells, grid_pos, token, gain)
    weight = conv_weight.reshape(9, 3 * channels, channels)
    bias = conv_bias.reshape(1, -1)
    first = conv_first(PLANES_FIRST, mid, edge0, edge1, mid_dec, weight, bias)
    near, far = rim_rows(mid, edge0, edge1, rad_low, rad_high, first)
    pairs = [(i, i + 1) for i in range(0, n_sector, 2)]
    across = [(i, (i + 1) % n_sector) for i in range(1, n_sector, 2)]
    near = lax.ppermute(near, "sector", pairs + [(t, s) for s, t in pairs])
    far = lax.ppermute(far, "sector", across + [(t, s) for s, t in across])
    inner, partial = conv_inner(
        mid, edge0, edge1, rad_low, rad_high, mid_dec, edge_dec, weight, bias, first
    )
    decoded = conv_edges(near, far, partial, mid_dec, edge_dec, weight, inner)
    return decoded.reshape(az, rad, height, channels)


def solution(mesh):
    lists = P(("sector", "blk"))
    return jax.shard_map(
        body,
        mesh=mesh,
        in_specs=(
            P(("sector", "blk"), None),
            P("sector", "blk", None, None),
            lists,
            lists,
            lists,
            lists,
            P(("sector", "blk"), None),
        )
        + (P(),) * 10,
        out_specs=P("sector", "blk", None, None),
        check_vma=False,
    )
```

```python
import jax
import jax.numpy as jnp
from jax import lax
from jax.experimental import pallas as pl
from jax.experimental.pallas import tpu as pltpu
from jax.sharding import PartitionSpec as P

HEAD_DIM = 32
EPSILON = 1e-05
F32 = jnp.float32
BF16 = jnp.bfloat16
I16 = jnp.int16
I32 = jnp.int32
CAP = 18
PLANES_FIRST = 3
MSG = 40


def iota(shape, dim):
    return lax.broadcasted_iota(I32, shape, dim)


def one_hot(mask):
    return jnp.where(mask, 1.0, 0.0).astype(BF16)


def match(col, row):
    n, k = col.shape[0], row.shape[1]
    col = jnp.broadcast_to(col, (n, 128)).astype(I16)
    row = jnp.broadcast_to(row, (16, k)).astype(I16)
    col = jnp.concatenate([col] * (k // 128), axis=1)
    row = jnp.concatenate([row] * (n // 16), axis=0)
    return jnp.where(col == row, jnp.ones((), BF16), jnp.zeros((), BF16))


def dot(a, b):
    return jnp.dot(a, b, preferred_element_type=F32)


def dot_nt(a, b):
    return lax.dot_general(a, b, (((1,), (1,)), ((), ())), preferred_element_type=F32)


def eye_mask(n):
    return iota((n, n), 0) == iota((n, n), 1)


def layer_norm(values, gain_vec):
    center = values - jnp.mean(values, axis=-1, keepdims=True)
    spread = jnp.mean(center * center, axis=-1, keepdims=True)
    return center * lax.rsqrt(spread + EPSILON) * gain_vec


def gelu(x):
    return 0.5 * x * (1.0 + jnp.tanh(0.7978845608028654 * (x + 0.044715 * (x * x * x))))


def send_kernel(
    count_ref, cells_ref, owner_ref, slot_ref, vis_ref, pos_ref,
    msg_ref, starts_ref,
    left_scr, right_scr, meta_scr, starts_smem, sem,
    cells_in, owner_in, slot_in, vis_in, pos_in, in_sems,
):
    entries = cells_ref.shape[1]
    owners = msg_ref.shape[0]
    cell_total = pos_ref.shape[0]
    loads = [
        pltpu.make_async_copy(src, dst, in_sems.at[i])
        for i, (src, dst) in enumerate(
            [
                (owner_ref, owner_in),
                (cells_ref, cells_in),
                (slot_ref, slot_in),
                (pos_ref, pos_in),
                (vis_ref, vis_in),
            ]
        )
    ]
    for load in loads:
        load.start()
    for load in loads[:3]:
        load.wait()
    entry = iota((1, entries), 1)
    live = entry < count_ref[0]
    owner = jnp.where(live, owner_in[...], owners)
    owner_id = iota((owners, entries), 0)
    start_col = jnp.sum(jnp.where(owner < owner_id, 1.0, 0.0), axis=1, keepdims=True)
    start_row = jnp.sum(jnp.where(eye_mask(owners), start_col, 0.0), axis=0, keepdims=True)
    starts_ref[...] = start_row.astype(I32)
    copy = pltpu.make_async_copy(starts_ref, starts_smem, sem)
    copy.start()
    belongs = owner == owner_id
    first = jnp.sum(jnp.where(belongs, start_col, 0.0), axis=0, keepdims=True)
    within = jnp.where(live, entry - first.astype(I32), 64)
    cells = cells_in[...]
    slots = slot_in[...]
    parts = jnp.concatenate(
        [cells >> 6, cells & 63, slots >> 5, slots & 31, within, within, within, within], axis=0
    ).astype(F32).astype(BF16)
    eye = one_hot(eye_mask(128))
    lane = iota((128, 128), 1)
    cell_cols = []
    meta_parts = []
    for b in range(entries // 128):
        turned = dot_nt(eye, parts[:, b * 128 : (b + 1) * 128])
        cell_cols.append((turned[:, 0:1] * 64.0 + turned[:, 1:2]).astype(I32))
        place = turned[:, 4:5].astype(I32)
        meta_parts.append(
            jnp.where(
                lane == place,
                turned[:, 2:3] + 1.0,
                jnp.where(lane == place + 32, turned[:, 3:4], 0.0),
            ).astype(BF16)
        )
    meta_scr[...] = dot(one_hot(belongs), jnp.concatenate(meta_parts, axis=0))
    for load in loads[3:]:
        load.wait()
    step = 512
    for b in range(entries // step):
        col = jnp.concatenate(cell_cols[b * step // 128 : (b + 1) * step // 128], axis=0)
        pick = match(col, iota((1, cell_total), 1))
        rows = vis_in[b * step : (b + 1) * step, :].astype(F32) + dot(pick, pos_in[...])
        rows = rows.astype(BF16).astype(F32)
        left_scr[b * step : (b + 1) * step, :] = rows[:, 0:128]
        right_scr[b * step : (b + 1) * step, :] = rows[:, 128:256]
    left_scr[entries:, :] = jnp.zeros((left_scr.shape[0] - entries, 128), F32)
    right_scr[entries:, :] = jnp.zeros((right_scr.shape[0] - entries, 128), F32)
    copy.wait()
    sub = iota((8, 128), 0)

    def emit(o, carry):
        start = starts_smem[0, o]
        msg_ref[o, 0:16, :] = left_scr[pl.ds(start, 16), :].astype(BF16)
        msg_ref[o, 16:32, :] = right_scr[pl.ds(start, 16), :].astype(BF16)
        left = left_scr[pl.ds(start + 16, 8), :]
        right = pltpu.roll(right_scr[pl.ds(start + 16, 8), :], 2, 0)
        last = jnp.where(sub < 2, left, jnp.where(sub < 4, right, meta_scr[pl.ds(o, 1), :]))
        msg_ref[o, 32:40, :] = last.astype(BF16)
        return carry

    lax.fori_loop(0, owners, emit, 0, unroll=4)


def send_rows(vis_count, cells, owner, slot, vis, pos, owners):
    entries = vis.shape[0]
    vmem = pl.BlockSpec(memory_space=pltpu.VMEM)
    smem = pl.BlockSpec(memory_space=pltpu.SMEM)
    return pl.pallas_call(
        send_kernel,
        out_shape=(
            jax.ShapeDtypeStruct((owners, MSG, 128), BF16),
            jax.ShapeDtypeStruct((1, owners), I32),
        ),
        in_specs=[smem] + [pl.BlockSpec(memory_space=pltpu.HBM)] * 5,
        out_specs=(vmem, vmem),
        scratch_shapes=[
            pltpu.VMEM((entries + 24, 128), F32),
            pltpu.VMEM((entries + 24, 128), F32),
            pltpu.VMEM((owners, 128), F32),
            pltpu.SMEM((1, owners), I32),
            pltpu.SemaphoreType.DMA,
            pltpu.VMEM(cells.shape, I32),
            pltpu.VMEM(cells.shape, I32),
            pltpu.VMEM(cells.shape, I32),
            pltpu.VMEM(vis.shape, BF16),
            pltpu.VMEM(pos.shape, BF16),
            pltpu.SemaphoreType.DMA((5,)),
        ],
        compiler_params=pltpu.CompilerParams(vmem_limit_bytes=60 * 2**20),
        name="send_rows",
    )(vis_count, cells, owner, slot, vis, pos)


def owner_kernel(
    msg_ref, window_ref, gain1_ref, attn_in_ref, attn_out_ref, gain2_ref,
    mlp_in_ref, mlp_out_ref,
    back_ref,
    order_scr, tail_scr, q_scr, k_scr, v_scr, win_scr, att_scr, x_scr,
):
    owners = msg_ref.shape[0]
    rows = window_ref.shape[1]
    channels = attn_out_ref.shape[0]
    head_count = channels // HEAD_DIM
    full = 16 * owners
    ids = window_ref[...]
    windows = range(4)
    length = [jnp.sum(jnp.where(ids == w, 1.0, 0.0)).astype(I32) for w in windows]
    old = [sum(length[:w], jnp.int32(0)) for w in windows]
    new = []
    for w in windows:
        ahead = [
            jnp.where(length[v] >= length[w] if v < w else length[v] > length[w], length[v], 0)
            for v in windows
            if v != w
        ]
        new.append(sum(ahead, jnp.int32(0)))
    end = [new[w] + length[w] for w in windows]
    place_row = iota((1, rows), 1)
    order = sum([jnp.where(place_row >= end[w], 1, 0) for w in windows])
    order_scr[...] = order
    tail_scr[...] = msg_ref[:, 32:40, :].astype(F32).reshape(owners * 8, 128)

    def tail(j):
        return tail_scr[pl.ds(j, owners, stride=8), :]

    meta = tail(4).astype(BF16)
    place = iota((128, full), 0)
    inner = iota((128, full), 1) & 15
    spread = (
        jnp.where(place == inner, 32.0, 0.0) + jnp.where(place == inner + 32, 1.0, 0.0)
    ).astype(BF16)
    wide = dot(meta, spread)
    of_sender = (iota((owners, full), 1) >> 4) == iota((owners, full), 0)
    slot_full = jnp.sum(jnp.where(of_sender, wide, 0.0), axis=0, keepdims=True) - 32.0
    eye = eye_mask(owners)
    meta32 = meta.astype(F32)
    tail_cols = [meta32[:, j : j + 1] * 32.0 + meta32[:, j + 32 : j + 33] - 32.0 for j in (16, 17)]
    tail_slots = [jnp.sum(jnp.where(eye, c, 0.0), axis=0, keepdims=True) for c in tail_cols]
    slot_row = jnp.concatenate([slot_full] + tail_slots, axis=1).astype(I32)
    moved = slot_row + (new[0] - old[0])
    for w in windows[1:]:
        moved = jnp.where(slot_row >= old[w], slot_row + (new[w] - old[w]), moved)
    slot_row = jnp.where(slot_row >= 0, moved, -1)
    left = msg_ref[:, 0:16, :].reshape(full, 128)
    right = msg_ref[:, 16:32, :].reshape(full, 128)
    main = jnp.concatenate([left, right], axis=1)
    rest = jnp.concatenate(
        [
            jnp.concatenate([tail(0), tail(2)], axis=1),
            jnp.concatenate([tail(1), tail(3)], axis=1),
        ],
        axis=0,
    ).astype(BF16)
    step = 256
    step = 1024
    for b in range(rows // step):
        part = slice(b * step, (b + 1) * step)
        sel = match(iota((step, 1), 0) + b * step, slot_row)
        x = dot(sel[:, :full], main) + dot(sel[:, full:], rest)
        x_scr[part, :] = x
        normed = layer_norm(x, gain1_ref[...]).astype(BF16)
        projected = dot(normed, attn_in_ref[...]).astype(BF16)
        q_scr[part, :] = projected[:, :channels]
        k_scr[part, :] = projected[:, channels : 2 * channels]
        ones = jnp.ones((step, 128), BF16)
        v_scr[part, 0:128] = projected[:, 2 * channels : 2 * channels + 128]
        v_scr[part, 128:256] = ones
        v_scr[part, 256:384] = projected[:, 2 * channels + 128 :]
        v_scr[part, 384:512] = ones
    q_step = 256
    eye_q = eye_mask(128)
    for i in range(rows // 128):
        part = slice(i * 128, (i + 1) * 128)
        ids = order_scr[:, part].astype(F32)
        ids = jnp.sum(jnp.where(eye_q, ids, 0.0), axis=1, keepdims=True)
        win_scr[part, :] = jnp.broadcast_to(ids, (128, 128)).astype(I32)
    head_of_lane = iota((1, channels), 1) // HEAD_DIM
    lane_head = (iota((1, channels), 1) & 127) // HEAD_DIM
    head_mask = [one_hot(head_of_lane == h) for h in range(head_count)]
    scale = HEAD_DIM ** (-0.5) * 1.4426950408889634
    stack = 4
    half_heads = head_count // 2

    def attend(qi, key_count, key_start):
        q_rows = pl.ds(pl.multiple_of(qi * q_step, q_step), q_step)
        k_rows = pl.ds(key_start, key_count)
        q = q_scr[q_rows, :]
        keys = k_scr[k_rows, :]
        q_win = win_scr[q_rows, :]
        q_win = jnp.concatenate([q_win] * (key_count // 128), axis=1)
        bias = jnp.where(q_win == order_scr[:, k_rows], 0.0, -jnp.inf)
        bias = jnp.concatenate([bias] * stack, axis=0)
        groups = []
        for half in range(2):
            for g in range(half_heads // 4):
                groups.append((half, range(g * 4, (g + 1) * 4)))

        def scores(half, heads):
            queries = jnp.concatenate([q * head_mask[half * half_heads + h] for h in heads], axis=0)
            return dot_nt(queries, keys) + bias

        def weigh(s):
            top = jnp.max(s, axis=1, keepdims=True)
            return jnp.exp2(((s - top) * scale).astype(BF16))

        totals = [None, None]

        def mix(half, heads, e):
            o = dot(e, v_scr[k_rows, 256 * half : 256 * half + 256])
            total = totals[half]
            for i, h in enumerate(heads):
                block = o[i * q_step : (i + 1) * q_step]
                total = block if total is None else jnp.where(lane_head == h, block, total)
            totals[half] = total

        ahead = scores(*groups[0])
        held = None
        for i in range(len(groups)):
            s = ahead
            if i + 1 < len(groups):
                ahead = scores(*groups[i + 1])
            e = weigh(s)
            if held is not None:
                mix(*held)
            held = (*groups[i], e)
        mix(*held)

        for half in range(2):
            total = totals[half]
            att_scr[q_rows, 128 * half : 128 * half + 128] = (
                total[:, 0:128] * (1.0 / total[:, 128:256])
            ).astype(BF16)

    def q_block(qi, carry):
        first = qi * q_step
        low = jnp.int32(0)
        high = jnp.int32(rows)
        for w in windows:
            low = jnp.maximum(low, jnp.where(new[w] <= first, new[w], 0))
            high = jnp.minimum(high, jnp.where(end[w] >= first + q_step, end[w], rows))
        low = (low >> 7) << 7
        count = (high - low + 255) >> 8
        low = jnp.minimum(low, rows - 256 * count)
        for n in range(1, rows // 256 + 1):

            @pl.when(count == n)
            def _():
                attend(qi, 256 * n, pl.multiple_of(low, 128))

        return carry

    lax.fori_loop(0, rows // q_step, q_block, 0)
    step = 256
    for b in range(rows // step):
        part = slice(b * step, (b + 1) * step)
        x = x_scr[part, :] + dot(att_scr[part, :], attn_out_ref[...])
        normed = layer_norm(x, gain2_ref[...]).astype(BF16)
        hidden = gelu(dot(normed, mlp_in_ref[...])).astype(BF16)
        q_scr[part, :] = (x + dot(hidden, mlp_out_ref[...])).astype(BF16)
    slot_f = slot_row.astype(F32)
    eye128 = eye_mask(128)
    step = 512
    for b in range(full // step + 1):
        size = step if b < full // step else 2 * owners
        cols = []
        for i in range(size // 128):
            at = b * step + i * 128
            cols.append(
                jnp.sum(jnp.where(eye128, slot_f[:, at : at + 128], 0.0), axis=1, keepdims=True)
            )
        col = jnp.concatenate(cols, axis=0).astype(I32)
        pick = match(col, iota((1, rows), 1))
        out = dot(pick, q_scr[...])
        if b < full // step:
            o = b * step // 16
            n = step // 16
            out = out.astype(BF16)
            back_ref[o : o + n, 0:16, :] = out[:, 0:128].reshape(n, 16, 128)
            back_ref[o : o + n, 16:32, :] = out[:, 128:256].reshape(n, 16, 128)
        else:
            for j in range(2):
                tail_scr[pl.ds(j, owners, stride=8), :] = out[j * owners : (j + 1) * owners, 0:128]
                tail_scr[pl.ds(j + 2, owners, stride=8), :] = out[
                    j * owners : (j + 1) * owners, 128:256
                ]
            back_ref[:, 32:40, :] = tail_scr[...].astype(BF16).reshape(owners, 8, 128)


def owner_encode(msg, window, gain1, attn_in, attn_out, gain2, mlp_in, mlp_out):
    owners = msg.shape[0]
    rows = window.shape[1]
    channels = attn_out.shape[0]
    vmem = pl.BlockSpec(memory_space=pltpu.VMEM)
    return pl.pallas_call(
        owner_kernel,
        out_shape=jax.ShapeDtypeStruct((owners, MSG, 128), BF16),
        in_specs=[vmem] * 8,
        out_specs=vmem,
        scratch_shapes=[
            pltpu.VMEM((1, rows), I32),
            pltpu.VMEM((owners * 8, 128), F32),
            pltpu.VMEM((rows, channels), BF16),
            pltpu.VMEM((rows, channels), BF16),
            pltpu.VMEM((rows, 2 * channels), BF16),
            pltpu.VMEM((rows, 128), I32),
            pltpu.VMEM((rows, channels), BF16),
            pltpu.VMEM((rows, channels), F32),
        ],
        compiler_params=pltpu.CompilerParams(vmem_limit_bytes=40 * 2**20),
        name="owner_encode",
    )(msg, window, gain1, attn_in, attn_out, gain2, mlp_in, mlp_out)


def cell_hits(ids, cells):
    hit = match(ids, cells)
    seen = sum([hit[:, i : i + 128] for i in range(0, hit.shape[1], 128)])
    return hit, jnp.sum(seen.astype(F32), axis=1, keepdims=True) > 0.5


def norm_cells(filled, seen, token, pos, gain):
    dec = (jnp.where(seen, filled, token) + pos.astype(F32)).astype(BF16)
    return dec, layer_norm(dec.astype(F32), gain).astype(BF16)


def edge_kernel(
    count_ref, starts_ref, back_ref, cells_ref, pos_ref, token_ref, gain_ref,
    rows_ref, dec_ref, first_ref, last_ref,
    left_scr, right_scr,
):
    owners = back_ref.shape[0]
    entries = cells_ref.shape[1]
    az, rad, height, channels = pos_ref.shape
    left_scr[...] = jnp.zeros(left_scr.shape, F32)
    right_scr[...] = jnp.zeros(right_scr.shape, F32)

    def take(o, carry):
        start = starts_ref[0, o]
        block = back_ref[o].astype(F32)
        left_scr[pl.ds(start, 16), :] = block[0:16]
        right_scr[pl.ds(start, 16), :] = block[16:32]
        left_scr[pl.ds(start + 16, 2), :] = block[32:34]
        right_scr[pl.ds(start + 16, 2), :] = block[34:36]
        return carry

    lax.fori_loop(0, owners, take, 0, unroll=8)
    rows = jnp.concatenate([left_scr[0:entries, :], right_scr[0:entries, :]], axis=1).astype(BF16)
    rows_ref[...] = rows
    cells = jnp.where(iota((1, entries), 1) < count_ref[0], cells_ref[...], -1)
    at = [(a, r) for r in (0, rad - 1) for a in range(az)]
    ids = jnp.concatenate(
        [iota((height, 1), 0) + (a * rad + r) * height for a, r in at], axis=0
    )
    pos = jnp.concatenate([pos_ref[a, r].astype(F32) for a, r in at], axis=0)
    hit, seen = cell_hits(ids, cells)
    dec, normed = norm_cells(dot(hit, rows), seen, token_ref[...], pos, gain_ref[...])
    dec_ref[...] = dec.reshape(dec_ref.shape)
    first_ref[...] = normed[: az * height]
    last_ref[...] = normed[az * height :]


def place_edges(vis_count, starts, back, cells, pos, token, gain):
    az, rad, height, channels = pos.shape
    entries = cells.shape[1]
    vmem = pl.BlockSpec(memory_space=pltpu.VMEM)
    smem = pl.BlockSpec(memory_space=pltpu.SMEM)
    edges = jax.ShapeDtypeStruct((2, az * height, channels), BF16)
    edge = jax.ShapeDtypeStruct((az * height, channels), BF16)
    return pl.pallas_call(
        edge_kernel,
        out_shape=(jax.ShapeDtypeStruct((entries, channels), BF16), edges, edge, edge),
        in_specs=[smem, smem] + [vmem] * 5,
        out_specs=(vmem,) * 4,
        scratch_shapes=[pltpu.VMEM((entries + 24, 128), F32)] * 2,
        compiler_params=pltpu.CompilerParams(vmem_limit_bytes=24 * 2**20),
        cost_estimate=pl.CostEstimate(flops=6 * 10**8, bytes_accessed=4 * 10**6, transcendentals=0),
        name="place_edges",
    )(vis_count, starts, back, cells, pos, token, gain)


def mid_kernel(
    count_ref, rows_ref, cells_ref, pos_ref, token_ref, gain_ref,
    dec_ref, normed_ref,
):
    entries = cells_ref.shape[1]
    az, rad, height, channels = pos_ref.shape
    size = (rad - 2) * height
    rows = rows_ref[...]
    cells = jnp.where(iota((1, entries), 1) < count_ref[0], cells_ref[...], -1)

    def pick(a):
        return cell_hits(iota((size, 1), 0) + (a * rad + 1) * height, cells)

    def finish(a, filled, seen):
        pos = pos_ref[a, 1 : rad - 1].reshape(size, channels)
        dec, normed = norm_cells(filled, seen, token_ref[...], pos, gain_ref[...])
        dec_ref[a] = dec
        normed_ref[a] = normed

    ahead = pick(0)
    held = None
    for a in range(az):
        hit, seen = ahead
        if a + 1 < az:
            ahead = pick(a + 1)
        filled = dot(hit, rows)
        if held is not None:
            finish(*held)
        held = (a, filled, seen)
    finish(*held)


def place_mid(vis_count, rows, cells, pos, token, gain):
    az, rad, height, channels = pos.shape
    vmem = pl.BlockSpec(memory_space=pltpu.VMEM)
    smem = pl.BlockSpec(memory_space=pltpu.SMEM)
    mid = jax.ShapeDtypeStruct((az, (rad - 2) * height, channels), BF16)
    return pl.pallas_call(
        mid_kernel,
        out_shape=(mid, mid),
        in_specs=[smem] + [vmem] * 5,
        out_specs=(vmem, vmem),
        compiler_params=pltpu.CompilerParams(vmem_limit_bytes=24 * 2**20),
        cost_estimate=pl.CostEstimate(flops=3 * 10**8, bytes_accessed=10**6, transcendentals=0),
        name="place_mid",
    )(vis_count, rows, cells, pos, token, gain)


def ring_ends():
    place = lax.axis_index("blk")
    return place == 0, place == lax.axis_size("blk") - 1


def even_sector():
    return lax.bitwise_and(lax.axis_index("sector"), 1) == 0


def rim_kernel(mid_ref, edge0_ref, edge1_ref, low_ref, high_ref, after_ref, near_ref, far_ref):
    az, size, channels = mid_ref.shape
    height = low_ref.shape[0] // az
    inside, outside = ring_ends()

    def fill(ref, a):
        part = slice(a * height, (a + 1) * height)
        ref[0:height] = jnp.where(inside, 0.0, low_ref[part].astype(F32)).astype(BF16)
        ref[height : 2 * height] = edge0_ref[part]
        ref[2 * height : 2 * height + size] = mid_ref[a]
        ref[2 * height + size : 3 * height + size] = edge1_ref[part]
        ref[3 * height + size :] = jnp.where(outside, 0.0, high_ref[part].astype(F32)).astype(BF16)

    even = even_sector()

    @pl.when(even)
    def _():
        fill(near_ref, az - 1)
        fill(far_ref, 0)

    @pl.when(jnp.logical_not(even))
    def _():
        fill(near_ref, 0)
        fill(far_ref, az - 1)


def rim_rows(mid, edge0, edge1, low, high, after):
    az, size, channels = mid.shape
    vmem = pl.BlockSpec(memory_space=pltpu.VMEM)
    out = jax.ShapeDtypeStruct((size + 4 * (low.shape[0] // az), channels), BF16)
    return pl.pallas_call(
        rim_kernel,
        out_shape=(out, out),
        in_specs=[vmem] * 5 + [pl.BlockSpec(memory_space=pl.ANY)],
        out_specs=(vmem, vmem),
        compiler_params=pltpu.CompilerParams(vmem_limit_bytes=8 * 2**20),
        name="rim_rows",
    )(mid, edge0, edge1, low, high, after)


def widen(scr, at, rows, height, drop=None):
    n, channels = rows.shape
    h = iota((n, 1), 0) % height
    values = rows.astype(F32)
    if drop is not None:
        values = jnp.where(drop, 0.0, values)
        rows = values.astype(BF16)
    scr[at : at + n, channels : 2 * channels] = rows
    below = jnp.where(h == 0, 0.0, pltpu.roll(values, 1, 0))
    scr[at : at + n, 0:channels] = below.astype(BF16)
    above = jnp.where(h == height - 1, 0.0, pltpu.roll(values, n - 1, 0))
    scr[at : at + n, 2 * channels :] = above.astype(BF16)


def first_kernel(
    mid_ref, edge0_ref, edge1_ref, mid_dec_ref, weight_ref, bias_ref,
    out_ref,
    wide_scr,
):
    planes, size, channels = out_ref.shape
    height = edge0_ref.shape[0] // mid_ref.shape[0]
    pitch = size + 2 * height

    def spread(a):
        base = a * pitch
        part = slice(a * height, (a + 1) * height)
        widen(wide_scr, base, edge0_ref[part], height)
        widen(wide_scr, base + height, mid_ref[a], height)
        widen(wide_scr, base + height + size, edge1_ref[part], height)

    def taps(a):
        total = jnp.broadcast_to(bias_ref[...], (size, channels))
        for da in range(3):
            for dr in range(3):
                at = (a + da - 1) * pitch + dr * height
                total = total + dot(wide_scr[at : at + size, :], weight_ref[da * 3 + dr])
        return total

    for a in range(3):
        spread(a)
    for a in range(1, planes + 1):
        total = taps(a)
        if a < planes:
            spread(a + 2)
        out_ref[a - 1] = (mid_dec_ref[a].astype(F32) + gelu(total)).astype(BF16)


def conv_first(planes, mid, edge0, edge1, mid_dec, weight, bias):
    az, size, channels = mid.shape
    pitch = size + 2 * (edge0.shape[0] // az)
    vmem = pl.BlockSpec(memory_space=pltpu.VMEM)
    return pl.pallas_call(
        first_kernel,
        out_shape=jax.ShapeDtypeStruct((planes, size, channels), BF16),
        in_specs=[vmem] * 6,
        out_specs=vmem,
        scratch_shapes=[pltpu.VMEM(((planes + 2) * pitch, 3 * channels), BF16)],
        compiler_params=pltpu.CompilerParams(vmem_limit_bytes=24 * 2**20),
        cost_estimate=pl.CostEstimate(flops=3 * 10**8, bytes_accessed=10**6, transcendentals=0),
        name="conv_first",
    )(mid, edge0, edge1, mid_dec, weight, bias)


def conv_kernel(
    mid_ref, edge0_ref, edge1_ref, low_ref, high_ref, mid_dec_ref, edge_dec_ref, weight_ref, bias_ref,
    first_ref,
    out_ref, partial_ref,
    wide_scr, done_scr, out_sems,
):
    az, size, channels = mid_ref.shape
    height = low_ref.shape[0] // az
    plane = size + 2 * height
    pitch = plane + 2 * height
    inside, outside = ring_ends()

    def spread(a):
        base = a * pitch
        part = slice(a * height, (a + 1) * height)
        widen(wide_scr, base, low_ref[part], height, inside)
        widen(wide_scr, base + height, edge0_ref[part], height)
        widen(wide_scr, base + 2 * height, mid_ref[a], height)
        widen(wide_scr, base + 2 * height + size, edge1_ref[part], height)
        widen(wide_scr, base + 3 * height + size, high_ref[part], height, outside)

    def taps(a):
        total = jnp.broadcast_to(bias_ref[...], (plane, channels))
        for da in range(3):
            if not 0 <= a + da - 1 < az:
                continue
            for dr in range(3):
                at = (a + da - 1) * pitch + dr * height
                total = total + dot(wide_scr[at : at + plane, :], weight_ref[da * 3 + dr])
        return total

    def side_taps():
        total = jnp.broadcast_to(bias_ref[...], (2 * planes * height, channels))
        for da in range(3):
            for dr in range(3):
                at = [
                    (a + da - 1) * pitch + (r + dr) * height
                    for a in range(1, planes + 1)
                    for r in (0, size // height + 1)
                ]
                rows = jnp.concatenate([wide_scr[i : i + height, :] for i in at], axis=0)
                total = total + dot(rows, weight_ref[da * 3 + dr])
        return total

    def finish(unit, total):
        if unit == "sides":
            done = []
            for a in range(1, planes + 1):
                part = slice(a * height, (a + 1) * height)
                for side, to in ((0, 0), (1, height + size)):
                    at = (2 * (a - 1) + side) * height
                    value = edge_dec_ref[side, part].astype(F32) + gelu(total[at : at + height])
                    done_scr[a - 1, to : to + height] = value.astype(BF16)
                done_scr[a - 1, height : height + size] = first_ref[a - 1]
                done.append(a)
            return done
        if unit in (0, az - 1):
            partial_ref[unit // (az - 1)] = total
            return []
        part = slice(unit * height, (unit + 1) * height)
        dec = jnp.concatenate(
            [edge_dec_ref[0, part], mid_dec_ref[unit], edge_dec_ref[1, part]], axis=0
        )
        done_scr[unit - 1] = (dec.astype(F32) + gelu(total)).astype(BF16)
        return [unit]

    planes = first_ref.shape[0]
    units = [(0, 1), ("sides", planes + 1)] + [(a, a + 1) for a in range(planes + 1, az)]
    ready = 0
    stores = []
    held = None
    for i, (unit, need) in enumerate(units):
        ahead = units[i + 1][1] if i + 1 < len(units) else az
        if held is None:
            while ready < need + 1:
                spread(ready)
                ready += 1
        total = side_taps() if unit == "sides" else taps(unit)
        while ready < min(ahead + 1, az):
            spread(ready)
            ready += 1
        if held is not None:
            for a in finish(*held):
                store = pltpu.make_async_copy(
                    done_scr.at[a - 1], out_ref.at[pl.ds(a * plane, plane)], out_sems.at[a - 1]
                )
                store.start()
                stores.append(store)
        held = (unit, total)
    finish(*held)
    for store in stores:
        store.wait()


def conv_inner(mid, edge0, edge1, low, high, mid_dec, edge_dec, weight, bias, first):
    az, size, channels = mid.shape
    height = low.shape[0] // az
    plane = size + 2 * height
    vmem = pl.BlockSpec(memory_space=pltpu.VMEM)
    hbm = pl.BlockSpec(memory_space=pltpu.HBM)
    return pl.pallas_call(
        conv_kernel,
        out_shape=(
            jax.ShapeDtypeStruct((az * plane, channels), BF16),
            jax.ShapeDtypeStruct((2, plane, channels), F32),
        ),
        in_specs=[vmem] * 10,
        out_specs=(hbm, vmem),
        scratch_shapes=[
            pltpu.VMEM((az * (plane + 2 * height), 3 * channels), BF16),
            pltpu.VMEM((az - 2, plane, channels), BF16),
            pltpu.SemaphoreType.DMA((az - 2,)),
        ],
        compiler_params=pltpu.CompilerParams(vmem_limit_bytes=32 * 2**20),
        cost_estimate=pl.CostEstimate(flops=6 * 10**9, bytes_accessed=10**7, transcendentals=0),
        name="conv_inner",
    )(mid, edge0, edge1, low, high, mid_dec, edge_dec, weight, bias, first)


def conv_edge_kernel(
    near_ref, far_ref, partial_ref, mid_dec_ref, edge_dec_ref, weight_ref, given_ref,
    out_ref,
    wide_scr, done_scr, out_sems,
):
    az, size, channels = mid_dec_ref.shape
    plane = partial_ref.shape[1]
    height = (plane - size) // 2
    pitch = plane + 2 * height
    even = even_sector()

    @pl.when(even)
    def _():
        widen(wide_scr, 0, far_ref[...], height)
        widen(wide_scr, pitch, near_ref[...], height)

    @pl.when(jnp.logical_not(even))
    def _():
        widen(wide_scr, 0, near_ref[...], height)
        widen(wide_scr, pitch, far_ref[...], height)

    stores = []
    for i in range(2):
        a = i * (az - 1)
        total = partial_ref[i]
        for dr in range(3):
            at = i * pitch + dr * height
            total = total + dot(wide_scr[at : at + plane, :], weight_ref[i * 6 + dr])
        part = slice(a * height, (a + 1) * height)
        dec = jnp.concatenate([edge_dec_ref[0, part], mid_dec_ref[a], edge_dec_ref[1, part]], axis=0)
        done_scr[i] = (dec.astype(F32) + gelu(total)).astype(BF16)
        store = pltpu.make_async_copy(
            done_scr.at[i], out_ref.at[pl.ds(a * plane, plane)], out_sems.at[i]
        )
        store.start()
        stores.append(store)
    for store in stores:
        store.wait()


def conv_edges(near, far, partial, mid_dec, edge_dec, weight, given):
    plane, channels = partial.shape[1:]
    vmem = pl.BlockSpec(memory_space=pltpu.VMEM)
    hbm = pl.BlockSpec(memory_space=pltpu.HBM)
    return pl.pallas_call(
        conv_edge_kernel,
        out_shape=jax.ShapeDtypeStruct(given.shape, BF16),
        in_specs=[vmem] * 6 + [hbm],
        out_specs=hbm,
        scratch_shapes=[
            pltpu.VMEM((2 * near.shape[0], 3 * channels), BF16),
            pltpu.VMEM((2, plane, channels), BF16),
            pltpu.SemaphoreType.DMA((2,)),
        ],
        input_output_aliases={6: 0},
        compiler_params=pltpu.CompilerParams(vmem_limit_bytes=16 * 2**20),
        name="conv_edges",
    )(near, far, partial, mid_dec, edge_dec, weight, given)


def exchange(values):
    return lax.all_to_all(values, ("sector", "blk"), split_axis=0, concat_axis=0, tiled=True)


def body(
    visible_feats, grid_pos, vis_cells, vis_count, owner, slot, window, enc_gain1, attn_in,
    attn_out, enc_gain2, mlp_in, mlp_out, mask_token, dec_gain, conv_weight, conv_bias,
):
    n_sector = lax.axis_size("sector")
    n_blk = lax.axis_size("blk")
    owners = n_sector * n_blk
    az, rad, height, channels = grid_pos.shape
    cell_total = az * rad * height
    pos = grid_pos.reshape(cell_total, channels)
    cells = vis_cells.reshape(1, -1)
    message, starts = send_rows(
        vis_count, cells, owner.reshape(1, -1), slot.reshape(1, -1), visible_feats, pos, owners
    )
    message = exchange(message)
    back = owner_encode(
        message, window, enc_gain1.reshape(1, -1), attn_in, attn_out,
        enc_gain2.reshape(1, -1), mlp_in, mlp_out,
    )
    back = exchange(back)
    token = mask_token.reshape(1, -1)
    gain = dec_gain.reshape(1, -1)
    rows, edge_dec, edge0, edge1 = place_edges(vis_count, starts, back, cells, grid_pos, token, gain)
    outward = [(i, (i + 1) % n_blk) for i in range(n_blk)]
    inward = [(t, s) for s, t in outward]
    rad_low = lax.ppermute(edge1, "blk", outward)
    rad_high = lax.ppermute(edge0, "blk", inward)
    mid_dec, mid = place_mid(vis_count, rows, cells, grid_pos, token, gain)
    weight = conv_weight.reshape(9, 3 * channels, channels)
    bias = conv_bias.reshape(1, -1)
    first = conv_first(PLANES_FIRST, mid, edge0, edge1, mid_dec, weight, bias)
    near, far = rim_rows(mid, edge0, edge1, rad_low, rad_high, first)
    pairs = [(i, i + 1) for i in range(0, n_sector, 2)]
    across = [(i, (i + 1) % n_sector) for i in range(1, n_sector, 2)]
    near = lax.ppermute(near, "sector", pairs + [(t, s) for s, t in pairs])
    far = lax.ppermute(far, "sector", across + [(t, s) for s, t in across])
    inner, partial = conv_inner(
        mid, edge0, edge1, rad_low, rad_high, mid_dec, edge_dec, weight, bias, first
    )
    decoded = conv_edges(near, far, partial, mid_dec, edge_dec, weight, inner)
    return decoded.reshape(az, rad, height, channels)


def solution(mesh):
    lists = P(("sector", "blk"))
    return jax.shard_map(
        body,
        mesh=mesh,
        in_specs=(
            P(("sector", "blk"), None),
            P("sector", "blk", None, None),
            lists,
            lists,
            lists,
            lists,
            P(("sector", "blk"), None),
        )
        + (P(),) * 10,
        out_specs=P("sector", "blk", None, None),
        check_vma=False,
    )
```

```python
import jax
import jax.numpy as jnp
from jax import lax
from jax.experimental import pallas as pl
from jax.experimental.pallas import tpu as pltpu
from jax.sharding import PartitionSpec as P

HEAD_DIM = 32
EPSILON = 1e-05
F32 = jnp.float32
BF16 = jnp.bfloat16
I16 = jnp.int16
I32 = jnp.int32
CAP = 18
PLANES_FIRST = 2
MSG = 40


def iota(shape, dim):
    return lax.broadcasted_iota(I32, shape, dim)


def one_hot(mask):
    return jnp.where(mask, 1.0, 0.0).astype(BF16)


def match(col, row):
    n, k = col.shape[0], row.shape[1]
    col = jnp.broadcast_to(col, (n, 128)).astype(I16)
    row = jnp.broadcast_to(row, (16, k)).astype(I16)
    col = jnp.concatenate([col] * (k // 128), axis=1)
    row = jnp.concatenate([row] * (n // 16), axis=0)
    return jnp.where(col == row, jnp.ones((), BF16), jnp.zeros((), BF16))


def dot(a, b):
    return jnp.dot(a, b, preferred_element_type=F32)


def dot_nt(a, b):
    return lax.dot_general(a, b, (((1,), (1,)), ((), ())), preferred_element_type=F32)


def eye_mask(n):
    return iota((n, n), 0) == iota((n, n), 1)


def layer_norm(values, gain_vec):
    center = values - jnp.mean(values, axis=-1, keepdims=True)
    spread = jnp.mean(center * center, axis=-1, keepdims=True)
    return center * lax.rsqrt(spread + EPSILON) * gain_vec


def gelu(x):
    return 0.5 * x * (1.0 + jnp.tanh(0.7978845608028654 * (x + 0.044715 * (x * x * x))))


def send_kernel(
    count_ref, cells_ref, owner_ref, slot_ref, vis_ref, pos_ref,
    msg_ref, starts_ref,
    left_scr, right_scr, meta_scr, starts_smem, sem,
    cells_in, owner_in, slot_in, vis_in, pos_in, in_sems,
):
    entries = cells_ref.shape[1]
    owners = msg_ref.shape[0]
    cell_total = pos_ref.shape[0]
    loads = [
        pltpu.make_async_copy(src, dst, in_sems.at[i])
        for i, (src, dst) in enumerate(
            [
                (owner_ref, owner_in),
                (cells_ref, cells_in),
                (slot_ref, slot_in),
                (pos_ref, pos_in),
                (vis_ref, vis_in),
            ]
        )
    ]
    for load in loads:
        load.start()
    for load in loads[:3]:
        load.wait()
    entry = iota((1, entries), 1)
    live = entry < count_ref[0]
    owner = jnp.where(live, owner_in[...], owners)
    owner_id = iota((owners, entries), 0)
    start_col = jnp.sum(jnp.where(owner < owner_id, 1.0, 0.0), axis=1, keepdims=True)
    start_row = jnp.sum(jnp.where(eye_mask(owners), start_col, 0.0), axis=0, keepdims=True)
    starts_ref[...] = start_row.astype(I32)
    copy = pltpu.make_async_copy(starts_ref, starts_smem, sem)
    copy.start()
    belongs = owner == owner_id
    first = jnp.sum(jnp.where(belongs, start_col, 0.0), axis=0, keepdims=True)
    within = jnp.where(live, entry - first.astype(I32), 64)
    cells = cells_in[...]
    slots = slot_in[...]
    parts = jnp.concatenate(
        [cells >> 6, cells & 63, slots >> 5, slots & 31, within, within, within, within], axis=0
    ).astype(F32).astype(BF16)
    eye = one_hot(eye_mask(128))
    lane = iota((128, 128), 1)
    cell_cols = []
    meta_parts = []
    for b in range(entries // 128):
        turned = dot_nt(eye, parts[:, b * 128 : (b + 1) * 128])
        cell_cols.append((turned[:, 0:1] * 64.0 + turned[:, 1:2]).astype(I32))
        place = turned[:, 4:5].astype(I32)
        meta_parts.append(
            jnp.where(
                lane == place,
                turned[:, 2:3] + 1.0,
                jnp.where(lane == place + 32, turned[:, 3:4], 0.0),
            ).astype(BF16)
        )
    meta_scr[...] = dot(one_hot(belongs), jnp.concatenate(meta_parts, axis=0))
    for load in loads[3:]:
        load.wait()
    step = 512
    for b in range(entries // step):
        col = jnp.concatenate(cell_cols[b * step // 128 : (b + 1) * step // 128], axis=0)
        pick = match(col, iota((1, cell_total), 1))
        rows = vis_in[b * step : (b + 1) * step, :].astype(F32) + dot(pick, pos_in[...])
        rows = rows.astype(BF16).astype(F32)
        left_scr[b * step : (b + 1) * step, :] = rows[:, 0:128]
        right_scr[b * step : (b + 1) * step, :] = rows[:, 128:256]
    left_scr[entries:, :] = jnp.zeros((left_scr.shape[0] - entries, 128), F32)
    right_scr[entries:, :] = jnp.zeros((right_scr.shape[0] - entries, 128), F32)
    copy.wait()
    sub = iota((8, 128), 0)

    def emit(o, carry):
        start = starts_smem[0, o]
        msg_ref[o, 0:16, :] = left_scr[pl.ds(start, 16), :].astype(BF16)
        msg_ref[o, 16:32, :] = right_scr[pl.ds(start, 16), :].astype(BF16)
        left = left_scr[pl.ds(start + 16, 8), :]
        right = pltpu.roll(right_scr[pl.ds(start + 16, 8), :], 2, 0)
        last = jnp.where(sub < 2, left, jnp.where(sub < 4, right, meta_scr[pl.ds(o, 1), :]))
        msg_ref[o, 32:40, :] = last.astype(BF16)
        return carry

    lax.fori_loop(0, owners, emit, 0, unroll=4)


def send_rows(vis_count, cells, owner, slot, vis, pos, owners):
    entries = vis.shape[0]
    vmem = pl.BlockSpec(memory_space=pltpu.VMEM)
    smem = pl.BlockSpec(memory_space=pltpu.SMEM)
    return pl.pallas_call(
        send_kernel,
        out_shape=(
            jax.ShapeDtypeStruct((owners, MSG, 128), BF16),
            jax.ShapeDtypeStruct((1, owners), I32),
        ),
        in_specs=[smem] + [pl.BlockSpec(memory_space=pltpu.HBM)] * 5,
        out_specs=(vmem, vmem),
        scratch_shapes=[
            pltpu.VMEM((entries + 24, 128), F32),
            pltpu.VMEM((entries + 24, 128), F32),
            pltpu.VMEM((owners, 128), F32),
            pltpu.SMEM((1, owners), I32),
            pltpu.SemaphoreType.DMA,
            pltpu.VMEM(cells.shape, I32),
            pltpu.VMEM(cells.shape, I32),
            pltpu.VMEM(cells.shape, I32),
            pltpu.VMEM(vis.shape, BF16),
            pltpu.VMEM(pos.shape, BF16),
            pltpu.SemaphoreType.DMA((5,)),
        ],
        compiler_params=pltpu.CompilerParams(vmem_limit_bytes=60 * 2**20),
        name="send_rows",
    )(vis_count, cells, owner, slot, vis, pos)


def owner_kernel(
    msg_ref, window_ref, gain1_ref, attn_in_ref, attn_out_ref, gain2_ref,
    mlp_in_ref, mlp_out_ref,
    back_ref,
    order_scr, tail_scr, q_scr, k_scr, v_scr, win_scr, att_scr, x_scr,
):
    owners = msg_ref.shape[0]
    rows = window_ref.shape[1]
    channels = attn_out_ref.shape[0]
    head_count = channels // HEAD_DIM
    full = 16 * owners
    ids = window_ref[...]
    windows = range(4)
    length = [jnp.sum(jnp.where(ids == w, 1.0, 0.0)).astype(I32) for w in windows]
    old = [sum(length[:w], jnp.int32(0)) for w in windows]
    new = []
    for w in windows:
        ahead = [
            jnp.where(length[v] >= length[w] if v < w else length[v] > length[w], length[v], 0)
            for v in windows
            if v != w
        ]
        new.append(sum(ahead, jnp.int32(0)))
    end = [new[w] + length[w] for w in windows]
    place_row = iota((1, rows), 1)
    order = sum([jnp.where(place_row >= end[w], 1, 0) for w in windows])
    order_scr[...] = order
    tail_scr[...] = msg_ref[:, 32:40, :].astype(F32).reshape(owners * 8, 128)

    def tail(j):
        return tail_scr[pl.ds(j, owners, stride=8), :]

    meta = tail(4).astype(BF16)
    place = iota((128, full), 0)
    inner = iota((128, full), 1) & 15
    spread = (
        jnp.where(place == inner, 32.0, 0.0) + jnp.where(place == inner + 32, 1.0, 0.0)
    ).astype(BF16)
    wide = dot(meta, spread)
    of_sender = (iota((owners, full), 1) >> 4) == iota((owners, full), 0)
    slot_full = jnp.sum(jnp.where(of_sender, wide, 0.0), axis=0, keepdims=True) - 32.0
    eye = eye_mask(owners)
    meta32 = meta.astype(F32)
    tail_cols = [meta32[:, j : j + 1] * 32.0 + meta32[:, j + 32 : j + 33] - 32.0 for j in (16, 17)]
    tail_slots = [jnp.sum(jnp.where(eye, c, 0.0), axis=0, keepdims=True) for c in tail_cols]
    slot_row = jnp.concatenate([slot_full] + tail_slots, axis=1).astype(I32)
    moved = slot_row + (new[0] - old[0])
    for w in windows[1:]:
        moved = jnp.where(slot_row >= old[w], slot_row + (new[w] - old[w]), moved)
    slot_row = jnp.where(slot_row >= 0, moved, -1)
    left = msg_ref[:, 0:16, :].reshape(full, 128)
    right = msg_ref[:, 16:32, :].reshape(full, 128)
    main = jnp.concatenate([left, right], axis=1)
    rest = jnp.concatenate(
        [
            jnp.concatenate([tail(0), tail(2)], axis=1),
            jnp.concatenate([tail(1), tail(3)], axis=1),
        ],
        axis=0,
    ).astype(BF16)
    step = 256
    step = 1024
    for b in range(rows // step):
        part = slice(b * step, (b + 1) * step)
        sel = match(iota((step, 1), 0) + b * step, slot_row)
        x = dot(sel[:, :full], main) + dot(sel[:, full:], rest)
        x_scr[part, :] = x
        normed = layer_norm(x, gain1_ref[...]).astype(BF16)
        projected = dot(normed, attn_in_ref[...]).astype(BF16)
        q_scr[part, :] = projected[:, :channels]
        k_scr[part, :] = projected[:, channels : 2 * channels]
        ones = jnp.ones((step, 128), BF16)
        v_scr[part, 0:128] = projected[:, 2 * channels : 2 * channels + 128]
        v_scr[part, 128:256] = ones
        v_scr[part, 256:384] = projected[:, 2 * channels + 128 :]
        v_scr[part, 384:512] = ones
    q_step = 256
    eye_q = eye_mask(128)
    for i in range(rows // 128):
        part = slice(i * 128, (i + 1) * 128)
        ids = order_scr[:, part].astype(F32)
        ids = jnp.sum(jnp.where(eye_q, ids, 0.0), axis=1, keepdims=True)
        win_scr[part, :] = jnp.broadcast_to(ids, (128, 128)).astype(I32)
    head_of_lane = iota((1, channels), 1) // HEAD_DIM
    lane_head = (iota((1, channels), 1) & 127) // HEAD_DIM
    head_mask = [one_hot(head_of_lane == h) for h in range(head_count)]
    scale = HEAD_DIM ** (-0.5) * 1.4426950408889634
    stack = 4
    half_heads = head_count // 2

    def attend(qi, key_count, key_start):
        q_rows = pl.ds(pl.multiple_of(qi * q_step, q_step), q_step)
        k_rows = pl.ds(key_start, key_count)
        q = q_scr[q_rows, :]
        keys = k_scr[k_rows, :]
        q_win = win_scr[q_rows, :]
        q_win = jnp.concatenate([q_win] * (key_count // 128), axis=1)
        bias = jnp.where(q_win == order_scr[:, k_rows], 0.0, -jnp.inf)
        bias = jnp.concatenate([bias] * stack, axis=0)
        groups = []
        for half in range(2):
            for g in range(half_heads // 4):
                groups.append((half, range(g * 4, (g + 1) * 4)))

        def scores(half, heads):
            queries = jnp.concatenate([q * head_mask[half * half_heads + h] for h in heads], axis=0)
            return dot_nt(queries, keys) + bias

        def weigh(s):
            top = jnp.max(s, axis=1, keepdims=True)
            return jnp.exp2(((s - top) * scale).astype(BF16))

        totals = [None, None]

        def mix(half, heads, e):
            o = dot(e, v_scr[k_rows, 256 * half : 256 * half + 256])
            total = totals[half]
            for i, h in enumerate(heads):
                block = o[i * q_step : (i + 1) * q_step]
                total = block if total is None else jnp.where(lane_head == h, block, total)
            totals[half] = total

        ahead = scores(*groups[0])
        held = None
        for i in range(len(groups)):
            s = ahead
            if i + 1 < len(groups):
                ahead = scores(*groups[i + 1])
            e = weigh(s)
            if held is not None:
                mix(*held)
            held = (*groups[i], e)
        mix(*held)

        for half in range(2):
            total = totals[half]
            att_scr[q_rows, 128 * half : 128 * half + 128] = (
                total[:, 0:128] * (1.0 / total[:, 128:256])
            ).astype(BF16)

    def q_block(qi, carry):
        first = qi * q_step
        low = jnp.int32(0)
        high = jnp.int32(rows)
        for w in windows:
            low = jnp.maximum(low, jnp.where(new[w] <= first, new[w], 0))
            high = jnp.minimum(high, jnp.where(end[w] >= first + q_step, end[w], rows))
        low = (low >> 7) << 7
        count = (high - low + 255) >> 8
        low = jnp.minimum(low, rows - 256 * count)
        for n in range(1, rows // 256 + 1):

            @pl.when(count == n)
            def _():
                attend(qi, 256 * n, pl.multiple_of(low, 128))

        return carry

    lax.fori_loop(0, rows // q_step, q_block, 0)
    step = 256
    for b in range(rows // step):
        part = slice(b * step, (b + 1) * step)
        x = x_scr[part, :] + dot(att_scr[part, :], attn_out_ref[...])
        normed = layer_norm(x, gain2_ref[...]).astype(BF16)
        hidden = gelu(dot(normed, mlp_in_ref[...])).astype(BF16)
        q_scr[part, :] = (x + dot(hidden, mlp_out_ref[...])).astype(BF16)
    slot_f = slot_row.astype(F32)
    eye128 = eye_mask(128)
    step = 512
    for b in range(full // step + 1):
        size = step if b < full // step else 2 * owners
        cols = []
        for i in range(size // 128):
            at = b * step + i * 128
            cols.append(
                jnp.sum(jnp.where(eye128, slot_f[:, at : at + 128], 0.0), axis=1, keepdims=True)
            )
        col = jnp.concatenate(cols, axis=0).astype(I32)
        pick = match(col, iota((1, rows), 1))
        out = dot(pick, q_scr[...])
        if b < full // step:
            o = b * step // 16
            n = step // 16
            out = out.astype(BF16)
            back_ref[o : o + n, 0:16, :] = out[:, 0:128].reshape(n, 16, 128)
            back_ref[o : o + n, 16:32, :] = out[:, 128:256].reshape(n, 16, 128)
        else:
            for j in range(2):
                tail_scr[pl.ds(j, owners, stride=8), :] = out[j * owners : (j + 1) * owners, 0:128]
                tail_scr[pl.ds(j + 2, owners, stride=8), :] = out[
                    j * owners : (j + 1) * owners, 128:256
                ]
            back_ref[:, 32:40, :] = tail_scr[...].astype(BF16).reshape(owners, 8, 128)


def owner_encode(msg, window, gain1, attn_in, attn_out, gain2, mlp_in, mlp_out):
    owners = msg.shape[0]
    rows = window.shape[1]
    channels = attn_out.shape[0]
    vmem = pl.BlockSpec(memory_space=pltpu.VMEM)
    return pl.pallas_call(
        owner_kernel,
        out_shape=jax.ShapeDtypeStruct((owners, MSG, 128), BF16),
        in_specs=[vmem] * 8,
        out_specs=vmem,
        scratch_shapes=[
            pltpu.VMEM((1, rows), I32),
            pltpu.VMEM((owners * 8, 128), F32),
            pltpu.VMEM((rows, channels), BF16),
            pltpu.VMEM((rows, channels), BF16),
            pltpu.VMEM((rows, 2 * channels), BF16),
            pltpu.VMEM((rows, 128), I32),
            pltpu.VMEM((rows, channels), BF16),
            pltpu.VMEM((rows, channels), F32),
        ],
        compiler_params=pltpu.CompilerParams(vmem_limit_bytes=40 * 2**20),
        name="owner_encode",
    )(msg, window, gain1, attn_in, attn_out, gain2, mlp_in, mlp_out)


def cell_hits(ids, cells):
    hit = match(ids, cells)
    seen = sum([hit[:, i : i + 128] for i in range(0, hit.shape[1], 128)])
    return hit, jnp.sum(seen.astype(F32), axis=1, keepdims=True) > 0.5


def norm_cells(filled, seen, token, pos, gain):
    dec = (jnp.where(seen, filled, token) + pos.astype(F32)).astype(BF16)
    return dec, layer_norm(dec.astype(F32), gain).astype(BF16)


def edge_kernel(
    count_ref, starts_ref, back_ref, cells_ref, pos_ref, token_ref, gain_ref,
    rows_ref, dec_ref, first_ref, last_ref,
    left_scr, right_scr,
):
    owners = back_ref.shape[0]
    entries = cells_ref.shape[1]
    az, rad, height, channels = pos_ref.shape
    left_scr[...] = jnp.zeros(left_scr.shape, F32)
    right_scr[...] = jnp.zeros(right_scr.shape, F32)

    def take(o, carry):
        start = starts_ref[0, o]
        block = back_ref[o].astype(F32)
        left_scr[pl.ds(start, 16), :] = block[0:16]
        right_scr[pl.ds(start, 16), :] = block[16:32]
        left_scr[pl.ds(start + 16, 2), :] = block[32:34]
        right_scr[pl.ds(start + 16, 2), :] = block[34:36]
        return carry

    lax.fori_loop(0, owners, take, 0, unroll=8)
    rows = jnp.concatenate([left_scr[0:entries, :], right_scr[0:entries, :]], axis=1).astype(BF16)
    rows_ref[...] = rows
    cells = jnp.where(iota((1, entries), 1) < count_ref[0], cells_ref[...], -1)
    at = [(a, r) for r in (0, rad - 1) for a in range(az)]
    ids = jnp.concatenate(
        [iota((height, 1), 0) + (a * rad + r) * height for a, r in at], axis=0
    )
    pos = jnp.concatenate([pos_ref[a, r].astype(F32) for a, r in at], axis=0)
    hit, seen = cell_hits(ids, cells)
    dec, normed = norm_cells(dot(hit, rows), seen, token_ref[...], pos, gain_ref[...])
    dec_ref[...] = dec.reshape(dec_ref.shape)
    first_ref[...] = normed[: az * height]
    last_ref[...] = normed[az * height :]


def place_edges(vis_count, starts, back, cells, pos, token, gain):
    az, rad, height, channels = pos.shape
    entries = cells.shape[1]
    vmem = pl.BlockSpec(memory_space=pltpu.VMEM)
    smem = pl.BlockSpec(memory_space=pltpu.SMEM)
    edges = jax.ShapeDtypeStruct((2, az * height, channels), BF16)
    edge = jax.ShapeDtypeStruct((az * height, channels), BF16)
    return pl.pallas_call(
        edge_kernel,
        out_shape=(jax.ShapeDtypeStruct((entries, channels), BF16), edges, edge, edge),
        in_specs=[smem, smem] + [vmem] * 5,
        out_specs=(vmem,) * 4,
        scratch_shapes=[pltpu.VMEM((entries + 24, 128), F32)] * 2,
        compiler_params=pltpu.CompilerParams(vmem_limit_bytes=24 * 2**20),
        cost_estimate=pl.CostEstimate(flops=6 * 10**8, bytes_accessed=4 * 10**6, transcendentals=0),
        name="place_edges",
    )(vis_count, starts, back, cells, pos, token, gain)


def mid_kernel(
    count_ref, rows_ref, cells_ref, pos_ref, token_ref, gain_ref,
    dec_ref, normed_ref,
):
    entries = cells_ref.shape[1]
    az, rad, height, channels = pos_ref.shape
    size = (rad - 2) * height
    rows = rows_ref[...]
    cells = jnp.where(iota((1, entries), 1) < count_ref[0], cells_ref[...], -1)

    def pick(a):
        return cell_hits(iota((size, 1), 0) + (a * rad + 1) * height, cells)

    def finish(a, filled, seen):
        pos = pos_ref[a, 1 : rad - 1].reshape(size, channels)
        dec, normed = norm_cells(filled, seen, token_ref[...], pos, gain_ref[...])
        dec_ref[a] = dec
        normed_ref[a] = normed

    ahead = pick(0)
    held = None
    for a in range(az):
        hit, seen = ahead
        if a + 1 < az:
            ahead = pick(a + 1)
        filled = dot(hit, rows)
        if held is not None:
            finish(*held)
        held = (a, filled, seen)
    finish(*held)


def place_mid(vis_count, rows, cells, pos, token, gain):
    az, rad, height, channels = pos.shape
    vmem = pl.BlockSpec(memory_space=pltpu.VMEM)
    smem = pl.BlockSpec(memory_space=pltpu.SMEM)
    mid = jax.ShapeDtypeStruct((az, (rad - 2) * height, channels), BF16)
    return pl.pallas_call(
        mid_kernel,
        out_shape=(mid, mid),
        in_specs=[smem] + [vmem] * 5,
        out_specs=(vmem, vmem),
        compiler_params=pltpu.CompilerParams(vmem_limit_bytes=24 * 2**20),
        cost_estimate=pl.CostEstimate(flops=3 * 10**8, bytes_accessed=10**6, transcendentals=0),
        name="place_mid",
    )(vis_count, rows, cells, pos, token, gain)


def ring_ends():
    place = lax.axis_index("blk")
    return place == 0, place == lax.axis_size("blk") - 1


def even_sector():
    return lax.bitwise_and(lax.axis_index("sector"), 1) == 0


def rim_kernel(mid_ref, edge0_ref, edge1_ref, low_ref, high_ref, after_ref, near_ref, far_ref):
    az, size, channels = mid_ref.shape
    height = low_ref.shape[0] // az
    inside, outside = ring_ends()

    def fill(ref, a):
        part = slice(a * height, (a + 1) * height)
        ref[0:height] = jnp.where(inside, 0.0, low_ref[part].astype(F32)).astype(BF16)
        ref[height : 2 * height] = edge0_ref[part]
        ref[2 * height : 2 * height + size] = mid_ref[a]
        ref[2 * height + size : 3 * height + size] = edge1_ref[part]
        ref[3 * height + size :] = jnp.where(outside, 0.0, high_ref[part].astype(F32)).astype(BF16)

    even = even_sector()

    @pl.when(even)
    def _():
        fill(near_ref, az - 1)
        fill(far_ref, 0)

    @pl.when(jnp.logical_not(even))
    def _():
        fill(near_ref, 0)
        fill(far_ref, az - 1)


def rim_rows(mid, edge0, edge1, low, high, after):
    az, size, channels = mid.shape
    vmem = pl.BlockSpec(memory_space=pltpu.VMEM)
    out = jax.ShapeDtypeStruct((size + 4 * (low.shape[0] // az), channels), BF16)
    return pl.pallas_call(
        rim_kernel,
        out_shape=(out, out),
        in_specs=[vmem] * 5 + [pl.BlockSpec(memory_space=pl.ANY)],
        out_specs=(vmem, vmem),
        compiler_params=pltpu.CompilerParams(vmem_limit_bytes=8 * 2**20),
        name="rim_rows",
    )(mid, edge0, edge1, low, high, after)


def widen(scr, at, rows, height, drop=None):
    n, channels = rows.shape
    h = iota((n, 1), 0) % height
    values = rows.astype(F32)
    if drop is not None:
        values = jnp.where(drop, 0.0, values)
        rows = values.astype(BF16)
    scr[at : at + n, channels : 2 * channels] = rows
    below = jnp.where(h == 0, 0.0, pltpu.roll(values, 1, 0))
    scr[at : at + n, 0:channels] = below.astype(BF16)
    above = jnp.where(h == height - 1, 0.0, pltpu.roll(values, n - 1, 0))
    scr[at : at + n, 2 * channels :] = above.astype(BF16)


def first_kernel(
    mid_ref, edge0_ref, edge1_ref, mid_dec_ref, weight_ref, bias_ref,
    out_ref,
    wide_scr,
):
    planes, size, channels = out_ref.shape
    height = edge0_ref.shape[0] // mid_ref.shape[0]
    pitch = size + 2 * height

    def spread(a):
        base = a * pitch
        part = slice(a * height, (a + 1) * height)
        widen(wide_scr, base, edge0_ref[part], height)
        widen(wide_scr, base + height, mid_ref[a], height)
        widen(wide_scr, base + height + size, edge1_ref[part], height)

    def taps(a):
        total = jnp.broadcast_to(bias_ref[...], (size, channels))
        for da in range(3):
            for dr in range(3):
                at = (a + da - 1) * pitch + dr * height
                total = total + dot(wide_scr[at : at + size, :], weight_ref[da * 3 + dr])
        return total

    for a in range(3):
        spread(a)
    for a in range(1, planes + 1):
        total = taps(a)
        if a < planes:
            spread(a + 2)
        out_ref[a - 1] = (mid_dec_ref[a].astype(F32) + gelu(total)).astype(BF16)


def conv_first(planes, mid, edge0, edge1, mid_dec, weight, bias):
    az, size, channels = mid.shape
    pitch = size + 2 * (edge0.shape[0] // az)
    vmem = pl.BlockSpec(memory_space=pltpu.VMEM)
    return pl.pallas_call(
        first_kernel,
        out_shape=jax.ShapeDtypeStruct((planes, size, channels), BF16),
        in_specs=[vmem] * 6,
        out_specs=vmem,
        scratch_shapes=[pltpu.VMEM(((planes + 2) * pitch, 3 * channels), BF16)],
        compiler_params=pltpu.CompilerParams(vmem_limit_bytes=24 * 2**20),
        cost_estimate=pl.CostEstimate(flops=3 * 10**8, bytes_accessed=10**6, transcendentals=0),
        name="conv_first",
    )(mid, edge0, edge1, mid_dec, weight, bias)


def conv_kernel(
    mid_ref, edge0_ref, edge1_ref, low_ref, high_ref, mid_dec_ref, edge_dec_ref, weight_ref, bias_ref,
    first_ref,
    out_ref, partial_ref,
    wide_scr, done_scr, out_sems,
):
    az, size, channels = mid_ref.shape
    height = low_ref.shape[0] // az
    plane = size + 2 * height
    pitch = plane + 2 * height
    inside, outside = ring_ends()

    def spread(a):
        base = a * pitch
        part = slice(a * height, (a + 1) * height)
        widen(wide_scr, base, low_ref[part], height, inside)
        widen(wide_scr, base + height, edge0_ref[part], height)
        widen(wide_scr, base + 2 * height, mid_ref[a], height)
        widen(wide_scr, base + 2 * height + size, edge1_ref[part], height)
        widen(wide_scr, base + 3 * height + size, high_ref[part], height, outside)

    def taps(a):
        total = jnp.broadcast_to(bias_ref[...], (plane, channels))
        for da in range(3):
            if not 0 <= a + da - 1 < az:
                continue
            for dr in range(3):
                at = (a + da - 1) * pitch + dr * height
                total = total + dot(wide_scr[at : at + plane, :], weight_ref[da * 3 + dr])
        return total

    def side_taps():
        total = jnp.broadcast_to(bias_ref[...], (2 * planes * height, channels))
        for da in range(3):
            for dr in range(3):
                at = [
                    (a + da - 1) * pitch + (r + dr) * height
                    for a in range(1, planes + 1)
                    for r in (0, size // height + 1)
                ]
                rows = jnp.concatenate([wide_scr[i : i + height, :] for i in at], axis=0)
                total = total + dot(rows, weight_ref[da * 3 + dr])
        return total

    def finish(unit, total):
        if unit == "sides":
            done = []
            for a in range(1, planes + 1):
                part = slice(a * height, (a + 1) * height)
                for side, to in ((0, 0), (1, height + size)):
                    at = (2 * (a - 1) + side) * height
                    value = edge_dec_ref[side, part].astype(F32) + gelu(total[at : at + height])
                    done_scr[a - 1, to : to + height] = value.astype(BF16)
                done_scr[a - 1, height : height + size] = first_ref[a - 1]
                done.append(a)
            return done
        if unit in (0, az - 1):
            partial_ref[unit // (az - 1)] = total
            return []
        part = slice(unit * height, (unit + 1) * height)
        dec = jnp.concatenate(
            [edge_dec_ref[0, part], mid_dec_ref[unit], edge_dec_ref[1, part]], axis=0
        )
        done_scr[unit - 1] = (dec.astype(F32) + gelu(total)).astype(BF16)
        return [unit]

    planes = first_ref.shape[0]
    units = [(0, 1), ("sides", planes + 1)] + [(a, a + 1) for a in range(planes + 1, az)]
    ready = 0
    stores = []
    held = None
    for i, (unit, need) in enumerate(units):
        ahead = units[i + 1][1] if i + 1 < len(units) else az
        if held is None:
            while ready < need + 1:
                spread(ready)
                ready += 1
        total = side_taps() if unit == "sides" else taps(unit)
        while ready < min(ahead + 1, az):
            spread(ready)
            ready += 1
        if held is not None:
            for a in finish(*held):
                store = pltpu.make_async_copy(
                    done_scr.at[a - 1], out_ref.at[pl.ds(a * plane, plane)], out_sems.at[a - 1]
                )
                store.start()
                stores.append(store)
        held = (unit, total)
    finish(*held)
    for store in stores:
        store.wait()


def conv_inner(mid, edge0, edge1, low, high, mid_dec, edge_dec, weight, bias, first):
    az, size, channels = mid.shape
    height = low.shape[0] // az
    plane = size + 2 * height
    vmem = pl.BlockSpec(memory_space=pltpu.VMEM)
    hbm = pl.BlockSpec(memory_space=pltpu.HBM)
    return pl.pallas_call(
        conv_kernel,
        out_shape=(
            jax.ShapeDtypeStruct((az * plane, channels), BF16),
            jax.ShapeDtypeStruct((2, plane, channels), F32),
        ),
        in_specs=[vmem] * 10,
        out_specs=(hbm, vmem),
        scratch_shapes=[
            pltpu.VMEM((az * (plane + 2 * height), 3 * channels), BF16),
            pltpu.VMEM((az - 2, plane, channels), BF16),
            pltpu.SemaphoreType.DMA((az - 2,)),
        ],
        compiler_params=pltpu.CompilerParams(vmem_limit_bytes=32 * 2**20),
        cost_estimate=pl.CostEstimate(flops=6 * 10**9, bytes_accessed=10**7, transcendentals=0),
        name="conv_inner",
    )(mid, edge0, edge1, low, high, mid_dec, edge_dec, weight, bias, first)


def conv_edge_kernel(
    near_ref, far_ref, partial_ref, mid_dec_ref, edge_dec_ref, weight_ref, given_ref,
    out_ref,
    wide_scr, done_scr, out_sems,
):
    az, size, channels = mid_dec_ref.shape
    plane = partial_ref.shape[1]
    height = (plane - size) // 2
    pitch = plane + 2 * height
    even = even_sector()

    @pl.when(even)
    def _():
        widen(wide_scr, 0, far_ref[...], height)
        widen(wide_scr, pitch, near_ref[...], height)

    @pl.when(jnp.logical_not(even))
    def _():
        widen(wide_scr, 0, near_ref[...], height)
        widen(wide_scr, pitch, far_ref[...], height)

    stores = []
    for i in range(2):
        a = i * (az - 1)
        total = partial_ref[i]
        for dr in range(3):
            at = i * pitch + dr * height
            total = total + dot(wide_scr[at : at + plane, :], weight_ref[i * 6 + dr])
        part = slice(a * height, (a + 1) * height)
        dec = jnp.concatenate([edge_dec_ref[0, part], mid_dec_ref[a], edge_dec_ref[1, part]], axis=0)
        done_scr[i] = (dec.astype(F32) + gelu(total)).astype(BF16)
        store = pltpu.make_async_copy(
            done_scr.at[i], out_ref.at[pl.ds(a * plane, plane)], out_sems.at[i]
        )
        store.start()
        stores.append(store)
    for store in stores:
        store.wait()


def conv_edges(near, far, partial, mid_dec, edge_dec, weight, given):
    plane, channels = partial.shape[1:]
    vmem = pl.BlockSpec(memory_space=pltpu.VMEM)
    hbm = pl.BlockSpec(memory_space=pltpu.HBM)
    return pl.pallas_call(
        conv_edge_kernel,
        out_shape=jax.ShapeDtypeStruct(given.shape, BF16),
        in_specs=[vmem] * 6 + [hbm],
        out_specs=hbm,
        scratch_shapes=[
            pltpu.VMEM((2 * near.shape[0], 3 * channels), BF16),
            pltpu.VMEM((2, plane, channels), BF16),
            pltpu.SemaphoreType.DMA((2,)),
        ],
        input_output_aliases={6: 0},
        compiler_params=pltpu.CompilerParams(vmem_limit_bytes=16 * 2**20),
        name="conv_edges",
    )(near, far, partial, mid_dec, edge_dec, weight, given)


def exchange(values):
    return lax.all_to_all(values, ("sector", "blk"), split_axis=0, concat_axis=0, tiled=True)


def body(
    visible_feats, grid_pos, vis_cells, vis_count, owner, slot, window, enc_gain1, attn_in,
    attn_out, enc_gain2, mlp_in, mlp_out, mask_token, dec_gain, conv_weight, conv_bias,
):
    n_sector = lax.axis_size("sector")
    n_blk = lax.axis_size("blk")
    owners = n_sector * n_blk
    az, rad, height, channels = grid_pos.shape
    cell_total = az * rad * height
    pos = grid_pos.reshape(cell_total, channels)
    cells = vis_cells.reshape(1, -1)
    message, starts = send_rows(
        vis_count, cells, owner.reshape(1, -1), slot.reshape(1, -1), visible_feats, pos, owners
    )
    message = exchange(message)
    back = owner_encode(
        message, window, enc_gain1.reshape(1, -1), attn_in, attn_out,
        enc_gain2.reshape(1, -1), mlp_in, mlp_out,
    )
    back = exchange(back)
    token = mask_token.reshape(1, -1)
    gain = dec_gain.reshape(1, -1)
    rows, edge_dec, edge0, edge1 = place_edges(vis_count, starts, back, cells, grid_pos, token, gain)
    outward = [(i, (i + 1) % n_blk) for i in range(n_blk)]
    inward = [(t, s) for s, t in outward]
    rad_high = lax.ppermute(edge0, "blk", inward)
    rad_low = lax.ppermute(edge1, "blk", outward)
    mid_dec, mid = place_mid(vis_count, rows, cells, grid_pos, token, gain)
    weight = conv_weight.reshape(9, 3 * channels, channels)
    bias = conv_bias.reshape(1, -1)
    first = conv_first(PLANES_FIRST, mid, edge0, edge1, mid_dec, weight, bias)
    near, far = rim_rows(mid, edge0, edge1, rad_low, rad_high, first)
    pairs = [(i, i + 1) for i in range(0, n_sector, 2)]
    across = [(i, (i + 1) % n_sector) for i in range(1, n_sector, 2)]
    near = lax.ppermute(near, "sector", pairs + [(t, s) for s, t in pairs])
    far = lax.ppermute(far, "sector", across + [(t, s) for s, t in across])
    inner, partial = conv_inner(
        mid, edge0, edge1, rad_low, rad_high, mid_dec, edge_dec, weight, bias, first
    )
    decoded = conv_edges(near, far, partial, mid_dec, edge_dec, weight, inner)
    return decoded.reshape(az, rad, height, channels)


def solution(mesh):
    lists = P(("sector", "blk"))
    return jax.shard_map(
        body,
        mesh=mesh,
        in_specs=(
            P(("sector", "blk"), None),
            P("sector", "blk", None, None),
            lists,
            lists,
            lists,
            lists,
            P(("sector", "blk"), None),
        )
        + (P(),) * 10,
        out_specs=P("sector", "blk", None, None),
        check_vma=False,
    )
```
